32 devices in a mesh: groups: 2 (over y), ctx: 4 (over x, core), head: 4 (over z).
Axes of the slice: x: 2, y: 2, z: 4, core: 2. Of those that a mesh axis runs over, the one named last changes fastest.
Arguments:
- queries: bfloat16 [12288, 512], P(('groups', 'ctx', 'head')), parts along dimension 0, may hold values from -8 to 8
- keys: bfloat16 [12288, 512], P(('groups', 'ctx', 'head')), parts along dimension 0, may hold values from -8 to 8
- values: bfloat16 [12288, 512], P(('groups', 'ctx', 'head')), parts along dimension 0, may hold values from -6 to 6
- tile_lists: int32 [96, 16], P(('groups', 'ctx')), parts along dimension 0, may hold values from -8 to 54, as said below
- live_counts: int32 [96], P(('groups', 'ctx')), parts along dimension 0, may hold values from 8 to 16
Outputs:
- attended: bfloat16 [12288, 512], P(('groups', 'ctx', 'head')), parts along dimension 0
The draws below stay inside these ranges and needn't reach their ends.
There are 2 independent parts, one for each index of `groups`. The reference program is written for one: setup_inputs(seed, part) draws one part's arguments, and reference() takes and returns one part's arrays. A program takes and returns all parts, laid end to end along the dimension named above; each array names one. Nothing has to cross between parts.
Inputs may be any that keep to these rules, and one draw needn't show every extreme that they name: `tile_lists`: row t holds t + o for each offset o from -8 to 7 exactly once, the first entry being t itself; entries outside 0 to 47 occur only near the ends of the video.
All inputs are finite; a program needn't handle non-finite values.
Results may differ from the reference program's by a relative error of at most 0.0047.
Values may be sent and summed in bfloat16 or wider, within the bound.
No kernel may reach another device: no remote copies, remote signals or barrier semaphores. Data moves between devices by JAX's collectives and lax.ppermute only.
A program may use at most 64 MiB of HBM per device.

```python
import jax
import jax.numpy as jnp
from jax import lax

HDIM = 128
TILE = 128
EDGE = 8
LIST = 16
HEADS = 4
NTILES = 48
TOKENS = 6144


def draw_queries(key, part):
    sample = jax.random.normal(jax.random.fold_in(key, 1), (TOKENS, HEADS * HDIM), jnp.float32)
    sample = jnp.clip(sample, -8.0, 8.0)
    return sample.astype(jnp.bfloat16)


def draw_keys(key, part):
    sample = jax.random.normal(jax.random.fold_in(key, 2), (TOKENS, HEADS * HDIM), jnp.float32)
    sample = jnp.clip(sample, -8.0, 8.0)
    return sample.astype(jnp.bfloat16)


def draw_tile_lists(key, part):
    others = jnp.concatenate([jnp.arange(-EDGE, 0), jnp.arange(1, EDGE)]).astype(jnp.int32)
    row_keys = jax.random.split(jax.random.fold_in(key, 3), NTILES)
    shuffled = jax.vmap(lambda row_key: jax.random.permutation(row_key, others))(row_keys)
    offsets = jnp.concatenate([jnp.zeros((NTILES, 1), jnp.int32), shuffled.astype(jnp.int32)], axis=1)
    return (jnp.arange(NTILES, dtype=jnp.int32)[:, None] + offsets).astype(jnp.int32)


def draw_live_counts(key, part):
    counts = jax.random.randint(jax.random.fold_in(key, 4), (NTILES,), LIST // 2, LIST + 1).astype(jnp.int32)
    counts = counts.at[0].set(LIST)
    return counts.at[1].set(LIST // 2)


def steps_of(stream_key, shape, shards, smallest, high):
    level, own = 1.0, jax.random.fold_in(stream_key, 6)
    for axis_at, shards_of in shards:
        steps = jnp.exp(jax.random.uniform(jax.random.fold_in(own, axis_at), (shards_of,), jnp.float32, smallest / len(shards), high / len(shards)))
        level = level * jnp.repeat(steps, shape[axis_at] // shards_of).reshape([-1 if axis == axis_at else 1 for axis in range(len(shape))])
    return level


def normal_values(own_key, dims, spread, limit, cuts=(), held_as=jnp.bfloat16):
    gain = steps_of(own_key, dims, cuts, -0.22, 0.18) if cuts else 1.0
    entries = jax.random.normal(own_key, dims, jnp.float32) * spread * gain
    return jnp.minimum(jnp.maximum(entries, -limit), limit).astype(held_as)


def setup_inputs(seed: int = 0, part: int = 0) -> dict:
    seeds = jax.random.split(jax.random.key(seed), 6)
    own_keys = jax.random.split(jax.random.fold_in(seeds[5], part), 6)
    queries = draw_queries(jax.random.fold_in(jax.random.fold_in(seeds[5], part), 71), part)
    keys = draw_keys(jax.random.fold_in(jax.random.fold_in(seeds[5], part), 71), part)
    values = normal_values(own_keys[2], (TOKENS, HEADS * HDIM), 1.0, 6.0, ((0, 16),))
    tile_lists = draw_tile_lists(jax.random.fold_in(jax.random.fold_in(seeds[5], part), 71), part)
    live_counts = draw_live_counts(jax.random.fold_in(jax.random.fold_in(seeds[5], part), 71), part)
    return dict(queries=queries, keys=keys, values=values, tile_lists=tile_lists, live_counts=live_counts)


def reference(queries, keys, values, tile_lists, live_counts):
    score_scale = HDIM ** -0.5

    def per_heads(array):
        return array.astype(jnp.float32).reshape(NTILES, TILE, HEADS, HDIM).transpose(2, 0, 1, 3)

    positions = jnp.arange(LIST)
    usable = (positions[None, :] < live_counts[:, None]) & (tile_lists >= 0) & (tile_lists < NTILES)
    safe_tiles = jnp.clip(tile_lists, 0, NTILES - 1).astype(jnp.int32)
    visible = jnp.repeat(usable, TILE, axis=1)[:, None, :]

    def per_head(inputs):
        q_head, k_head, v_head = inputs
        k_picked = k_head[safe_tiles].reshape(NTILES, LIST * TILE, HDIM)
        v_picked = v_head[safe_tiles].reshape(NTILES, LIST * TILE, HDIM)
        scores = jnp.einsum("tqd,tkd->tqk", q_head, k_picked, precision=lax.Precision.HIGHEST) * score_scale
        scores = jnp.where(visible, scores, -1e30)
        highest = jnp.max(scores, axis=-1, keepdims=True)
        weights = jnp.where(visible, jnp.exp(scores - highest), 0.0)
        softmax_divisor = jnp.sum(weights, axis=-1, keepdims=True)
        rounded = lax.optimization_barrier(weights.astype(jnp.bfloat16))
        attention_probs = rounded.astype(jnp.float32)
        mixed = jnp.einsum("tqk,tkd->tqd", attention_probs, v_picked, precision=lax.Precision.HIGHEST)
        return (mixed / softmax_divisor).astype(jnp.bfloat16)

    results = lax.map(per_head, (per_heads(queries), per_heads(keys), per_heads(values)))
    return results.transpose(1, 2, 0, 3).reshape(TOKENS, HEADS * HDIM)
```

```python
import functools
import math

import jax
import jax.numpy as jnp
from jax import lax
from jax.experimental import pallas as pl
from jax.experimental.pallas import tpu as pltpu
from jax.sharding import PartitionSpec as P

HDIM = 128
TILE = 128
EDGE = 8
LIST = 16
BLOCK = 3
WINDOW = BLOCK + LIST - 1
HIDDEN = -1e30
EXPONENT_SCALE = HDIM ** (-0.5) * math.log2(math.e)
SMEM = pl.BlockSpec(memory_space=pltpu.SMEM)
VMEM = pl.BlockSpec(memory_space=pltpu.VMEM)


def pack_kernel(heads, q_ref, k_ref, v_ref, q_out, k_out, v_out):
    for source, target in ((k_ref, k_out), (v_ref, v_out), (q_ref, q_out)):
        for head in range(heads):
            target[head] = source[:, head * HDIM : (head + 1) * HDIM]


def pack(queries, keys, values):
    rows, columns = queries.shape
    heads = columns // HDIM
    shape = jax.ShapeDtypeStruct((heads, rows, HDIM), queries.dtype)
    return pl.pallas_call(
        functools.partial(pack_kernel, heads),
        out_shape=[shape] * 3,
        in_specs=[VMEM] * 3,
        out_specs=[VMEM] * 3,
        compiler_params=pltpu.CompilerParams(vmem_limit_bytes=8 << 20),
        name="pack",
    )(queries, keys, values)


def unpack_kernel(heads, parts_ref, out_ref):
    for head in range(heads):
        out_ref[:, head * HDIM : (head + 1) * HDIM] = parts_ref[head]


def unpack(parts):
    heads, rows, _ = parts.shape
    return pl.pallas_call(
        functools.partial(unpack_kernel, heads),
        out_shape=jax.ShapeDtypeStruct((rows, heads * HDIM), parts.dtype),
        in_specs=[VMEM],
        out_specs=VMEM,
        compiler_params=pltpu.CompilerParams(vmem_limit_bytes=8 << 20),
        name="unpack",
    )(parts)


def attend_block(first, total_tiles, lists_ref, counts_ref, q_ref, kbuf, vbuf, bias, scores, probs):
    for tile in range(BLOCK):
        row = first + tile
        own = lists_ref[row, 0]
        count = counts_ref[row]
        for entry in range(LIST):
            listed = lists_ref[row, entry]
            live = (entry < count) & (listed >= 0) & (listed < total_tiles)
            bias[tile * LIST + listed - own + EDGE] = jnp.where(live, 0.0, HIDDEN)

    base = pl.multiple_of(first * TILE, TILE)
    for pair in range(WINDOW // 2):
        low = max(0, 2 * pair - LIST + 1)
        high = min(BLOCK - 1, 2 * pair + 1)
        part = lax.dot_general(
            q_ref[low * TILE : (high + 1) * TILE, :],
            kbuf[pl.ds(base + pair * 2 * TILE, 2 * TILE), :],
            (((1,), (1,)), ((), ())),
            preferred_element_type=jnp.float32,
        )
        for tile in range(low, high + 1):
            for half in range(2):
                place = 2 * pair + half
                if 0 <= place - tile < LIST:
                    rows = slice((tile - low) * TILE, (tile - low + 1) * TILE)
                    scores[tile * TILE : (tile + 1) * TILE, place * TILE : (place + 1) * TILE] = (
                        part[rows, half * TILE : (half + 1) * TILE] + bias[tile * LIST + place - tile]
                    )
    divisors = []
    for tile in range(BLOCK):
        rows = slice(tile * TILE, (tile + 1) * TILE)
        highest = scores[rows, tile * TILE : (tile + 1) * TILE]
        for place in range(tile + 1, tile + LIST):
            highest = jnp.maximum(highest, scores[rows, place * TILE : (place + 1) * TILE])
        highest = jnp.broadcast_to(jnp.max(highest, axis=1, keepdims=True), (TILE, TILE))
        total = jnp.zeros((TILE, TILE), jnp.float32)
        for place in range(WINDOW):
            columns = slice(place * TILE, (place + 1) * TILE)
            if 0 <= place - tile < LIST:
                weights = jnp.exp2((scores[rows, columns] - highest) * EXPONENT_SCALE)
                total += weights
                probs[rows, columns] = weights.astype(jnp.bfloat16)
            else:
                probs[rows, columns] = jnp.zeros((TILE, TILE), jnp.bfloat16)
        divisors.append(jnp.sum(total, axis=1, keepdims=True))
    mixed = jnp.dot(
        probs[...], vbuf[pl.ds(base, WINDOW * TILE), :], preferred_element_type=jnp.float32
    )
    return (mixed / jnp.concatenate(divisors, axis=0)).astype(jnp.bfloat16)


def attend_kernel(
    total_tiles, lists_ref, counts_ref, q_ref, k_own, v_own, k_low, v_low, k_high, v_high, out_ref,
    kbuf, vbuf, bias, scores, probs,
):
    rows = k_own.shape[0]
    for low, own, high, buffer in ((k_low, k_own, k_high, kbuf), (v_low, v_own, v_high, vbuf)):
        buffer[: EDGE * TILE, :] = low[...]
        buffer[EDGE * TILE : EDGE * TILE + rows, :] = own[...]
        buffer[EDGE * TILE + rows :, :] = high[...]

    @pl.loop(0, q_ref.shape[0] // (BLOCK * TILE))
    def _(block):
        place = pl.ds(pl.multiple_of(block * BLOCK * TILE, TILE), BLOCK * TILE)
        out_ref[place, :] = attend_block(
            block * BLOCK, total_tiles, lists_ref, counts_ref, q_ref.at[place, :],
            kbuf, vbuf, bias, scores, probs,
        )


def attend(queries, own, low, high, tile_lists, live_counts, total_tiles):
    rows = queries.shape[0]
    padded = rows + (LIST - 1) * TILE
    block_rows = BLOCK * TILE
    return pl.pallas_call(
        functools.partial(attend_kernel, total_tiles),
        out_shape=jax.ShapeDtypeStruct(queries.shape, queries.dtype),
        in_specs=[SMEM, SMEM] + [VMEM] * 7,
        out_specs=VMEM,
        scratch_shapes=[
            pltpu.VMEM((padded, HDIM), jnp.bfloat16),
            pltpu.VMEM((padded, HDIM), jnp.bfloat16),
            pltpu.SMEM((BLOCK * LIST,), jnp.float32),
            pltpu.VMEM((block_rows, WINDOW * TILE), jnp.float32),
            pltpu.VMEM((block_rows, WINDOW * TILE), jnp.bfloat16),
        ],
        compiler_params=pltpu.CompilerParams(vmem_limit_bytes=24 << 20),
        name="attend",
    )(tile_lists, live_counts, queries, own[0], own[1], low[0], low[1], high[0], high[1])


def to_heads(array):
    heads, rows, _ = array.shape
    return lax.all_to_all(array, "head", split_axis=0, concat_axis=0, tiled=True).reshape(heads * rows, HDIM)


def on_device(queries, keys, values, tile_lists, live_counts):
    ctx = lax.axis_size("ctx")
    total_tiles = tile_lists.shape[0] * ctx
    forward = [(i, i + 1) for i in range(ctx - 1)]
    backward = [(i + 1, i) for i in range(ctx - 1)]
    q_parts, k_parts, v_parts = pack(queries, keys, values)
    own = to_heads(k_parts), to_heads(v_parts)
    low = [lax.ppermute(array[-EDGE * TILE :], "ctx", forward) for array in own]
    high = [lax.ppermute(array[: (EDGE - 1) * TILE], "ctx", backward) for array in own]
    local_q = to_heads(q_parts)
    head_out = attend(local_q, own, low, high, tile_lists, live_counts, total_tiles)
    back = lax.all_to_all(
        head_out.reshape(q_parts.shape), "head", split_axis=0, concat_axis=0, tiled=True
    )
    return unpack(back)


def solution(mesh):
    return jax.shard_map(
        on_device,
        mesh=mesh,
        in_specs=(
            P(("groups", "ctx", "head"), None),
            P(("groups", "ctx", "head"), None),
            P(("groups", "ctx", "head"), None),
            P(("groups", "ctx"), None),
            P(("groups", "ctx")),
        ),
        out_specs=P(("groups", "ctx", "head"), None),
        check_vma=False,
    )
```

```python
import functools
import math

import jax
import jax.numpy as jnp
from jax import lax
from jax.experimental import pallas as pl
from jax.experimental.pallas import tpu as pltpu
from jax.sharding import PartitionSpec as P

HDIM = 128
TILE = 128
EDGE = 8
LIST = 16
BLOCK = 3
WINDOW = BLOCK + LIST - 1
HIDDEN = -1e30
EXPONENT_SCALE = HDIM ** (-0.5) * math.log2(math.e)
SMEM = pl.BlockSpec(memory_space=pltpu.SMEM)
VMEM = pl.BlockSpec(memory_space=pltpu.VMEM)


def pack_kernel(heads, q_ref, k_ref, v_ref, q_out, k_out, v_out):
    for source, target in ((k_ref, k_out), (v_ref, v_out), (q_ref, q_out)):
        for head in range(heads):
            target[head] = source[:, head * HDIM : (head + 1) * HDIM]


def pack(queries, keys, values):
    rows, columns = queries.shape
    heads = columns // HDIM
    shape = jax.ShapeDtypeStruct((heads, rows, HDIM), queries.dtype)
    return pl.pallas_call(
        functools.partial(pack_kernel, heads),
        out_shape=[shape] * 3,
        in_specs=[VMEM] * 3,
        out_specs=[VMEM] * 3,
        compiler_params=pltpu.CompilerParams(vmem_limit_bytes=8 << 20),
        name="pack",
    )(queries, keys, values)


def unpack_kernel(heads, parts_ref, out_ref):
    for head in range(heads):
        out_ref[:, head * HDIM : (head + 1) * HDIM] = parts_ref[head]


def unpack(parts):
    heads, rows, _ = parts.shape
    return pl.pallas_call(
        functools.partial(unpack_kernel, heads),
        out_shape=jax.ShapeDtypeStruct((rows, heads * HDIM), parts.dtype),
        in_specs=[VMEM],
        out_specs=VMEM,
        compiler_params=pltpu.CompilerParams(vmem_limit_bytes=8 << 20),
        name="unpack",
    )(parts)


def attend_block(first, total_tiles, lists_ref, counts_ref, q_ref, kbuf, vbuf, bias, scores, probs):
    for tile in range(BLOCK):
        row = first + tile
        own = lists_ref[row, 0]
        count = counts_ref[row]
        for entry in range(LIST):
            listed = lists_ref[row, entry]
            live = (entry < count) & (listed >= 0) & (listed < total_tiles)
            bias[tile * LIST + listed - own + EDGE] = jnp.where(live, 0.0, HIDDEN)

    base = pl.multiple_of(first * TILE, TILE)
    for pair in range(WINDOW // 2):
        low = max(0, 2 * pair - LIST + 1)
        high = min(BLOCK - 1, 2 * pair + 1)
        part = lax.dot_general(
            q_ref[low * TILE : (high + 1) * TILE, :],
            kbuf[pl.ds(base + pair * 2 * TILE, 2 * TILE), :],
            (((1,), (1,)), ((), ())),
            preferred_element_type=jnp.float32,
        )
        for tile in range(low, high + 1):
            for half in range(2):
                place = 2 * pair + half
                if 0 <= place - tile < LIST:
                    rows = slice((tile - low) * TILE, (tile - low + 1) * TILE)
                    scores[tile * TILE : (tile + 1) * TILE, place * TILE : (place + 1) * TILE] = (
                        part[rows, half * TILE : (half + 1) * TILE] + bias[tile * LIST + place - tile]
                    )
    divisors = []
    for tile in range(BLOCK):
        rows = slice(tile * TILE, (tile + 1) * TILE)
        highest = scores[rows, tile * TILE : (tile + 1) * TILE]
        for place in range(tile + 1, tile + LIST):
            highest = jnp.maximum(highest, scores[rows, place * TILE : (place + 1) * TILE])
        highest = jnp.broadcast_to(jnp.max(highest, axis=1, keepdims=True), (TILE, TILE))
        total = jnp.zeros((TILE, TILE), jnp.float32)
        for place in range(WINDOW):
            columns = slice(place * TILE, (place + 1) * TILE)
            if 0 <= place - tile < LIST:
                weights = jnp.exp2((scores[rows, columns] - highest) * EXPONENT_SCALE)
                total += weights
                probs[rows, columns] = weights.astype(jnp.bfloat16)
            else:
                probs[rows, columns] = jnp.zeros((TILE, TILE), jnp.bfloat16)
        divisors.append(jnp.sum(total, axis=1, keepdims=True))
    mixed = jnp.dot(
        probs[...], vbuf[pl.ds(base, WINDOW * TILE), :], preferred_element_type=jnp.float32
    )
    return (mixed / jnp.concatenate(divisors, axis=0)).astype(jnp.bfloat16)


def attend_kernel(
    total_tiles, lists_ref, counts_ref, q_ref, k_own, v_own, k_low, v_low, k_high, v_high, out_ref,
    kbuf, vbuf, bias, scores, probs,
):
    rows = k_own.shape[0]
    for low, own, high, buffer in ((k_low, k_own, k_high, kbuf), (v_low, v_own, v_high, vbuf)):
        buffer[: EDGE * TILE, :] = low[...]
        buffer[EDGE * TILE : EDGE * TILE + rows, :] = own[...]
        buffer[EDGE * TILE + rows :, :] = high[...]

    @pl.loop(0, q_ref.shape[0] // (BLOCK * TILE))
    def _(block):
        place = pl.ds(pl.multiple_of(block * BLOCK * TILE, TILE), BLOCK * TILE)
        out_ref[place, :] = attend_block(
            block * BLOCK, total_tiles, lists_ref, counts_ref, q_ref.at[place, :],
            kbuf, vbuf, bias, scores, probs,
        )


def attend(queries, own, low, high, tile_lists, live_counts, total_tiles):
    rows = queries.shape[0]
    padded = rows + (LIST - 1) * TILE
    block_rows = BLOCK * TILE
    return pl.pallas_call(
        functools.partial(attend_kernel, total_tiles),
        out_shape=jax.ShapeDtypeStruct(queries.shape, queries.dtype),
        in_specs=[SMEM, SMEM] + [VMEM] * 7,
        out_specs=VMEM,
        scratch_shapes=[
            pltpu.VMEM((padded, HDIM), jnp.bfloat16),
            pltpu.VMEM((padded, HDIM), jnp.bfloat16),
            pltpu.SMEM((BLOCK * LIST,), jnp.float32),
            pltpu.VMEM((block_rows, WINDOW * TILE), jnp.float32),
            pltpu.VMEM((block_rows, WINDOW * TILE), jnp.bfloat16),
        ],
        compiler_params=pltpu.CompilerParams(vmem_limit_bytes=24 << 20),
        name="attend",
    )(tile_lists, live_counts, queries, own[0], own[1], low[0], low[1], high[0], high[1])


def to_heads(array):
    heads, rows, _ = array.shape
    return lax.all_to_all(array, "head", split_axis=0, concat_axis=0, tiled=True).reshape(heads * rows, HDIM)


def halo(array, dim):
    ctx = lax.axis_size("ctx")
    count = array.shape[dim]
    tail = lax.slice_in_dim(array, count - EDGE * TILE, count, axis=dim)
    head = lax.slice_in_dim(array, 0, (EDGE - 1) * TILE, axis=dim)
    low = lax.ppermute(tail, "ctx", [(i, i + 1) for i in range(ctx - 1)])
    high = lax.ppermute(head, "ctx", [(i + 1, i) for i in range(ctx - 1)])
    return low, high


def whole_range(queries, keys, values, tile_lists, live_counts, total_tiles):
    q_parts, k_parts, v_parts = pack(queries, keys, values)
    own = to_heads(k_parts), to_heads(v_parts)
    low, high = zip(*(halo(array, 0) for array in own))
    local_q = to_heads(q_parts)
    head_out = attend(local_q, own, low, high, tile_lists, live_counts, total_tiles)
    back = lax.all_to_all(
        head_out.reshape(q_parts.shape), "head", split_axis=0, concat_axis=0, tiled=True
    )
    return unpack(back)


def column_of(head):
    return pl.ds(pl.multiple_of(head * HDIM, HDIM), HDIM)


def shift_pack_kernel(heads, q_ref, k_ref, v_ref, *out_refs):
    me = lax.axis_index("head")
    for shift in range(heads):
        columns = column_of(lax.rem(me + shift, heads))
        kv_out, q_out = out_refs[2 * shift], out_refs[2 * shift + 1]
        kv_out[0] = k_ref[:, columns]
        kv_out[1] = v_ref[:, columns]
        q_out[...] = q_ref[:, columns]


def shift_pack(queries, keys, values, heads):
    rows = queries.shape[0]
    kv = jax.ShapeDtypeStruct((2, rows, HDIM), keys.dtype)
    q = jax.ShapeDtypeStruct((rows, HDIM), queries.dtype)
    parts = pl.pallas_call(
        functools.partial(shift_pack_kernel, heads),
        out_shape=[kv, q] * heads,
        in_specs=[VMEM] * 3,
        out_specs=[VMEM] * 2 * heads,
        compiler_params=pltpu.CompilerParams(vmem_limit_bytes=8 << 20),
        name="shift_pack",
    )(queries, keys, values)
    return list(parts[0::2]), list(parts[1::2])


def gather_kernel(heads, *refs):
    out_ref = refs[-1]
    me = lax.axis_index("head")
    for shift in range(heads):
        rows = refs[shift].shape[1]
        source = lax.rem(me + heads - shift, heads)
        out_ref[:, pl.ds(pl.multiple_of(source * rows, TILE), rows), :] = refs[shift][...]


def gather(parts):
    heads, (_, rows, _) = len(parts), parts[0].shape
    return pl.pallas_call(
        functools.partial(gather_kernel, heads),
        out_shape=jax.ShapeDtypeStruct((2, heads * rows, HDIM), parts[0].dtype),
        in_specs=[VMEM] * heads,
        out_specs=VMEM,
        compiler_params=pltpu.CompilerParams(vmem_limit_bytes=8 << 20),
        name="gather",
    )(*parts)


def pad_kernel(low_ref, own_ref, high_ref, out_ref):
    at = 0
    for ref in (low_ref, own_ref, high_ref):
        rows = ref.shape[1]
        out_ref[:, at : at + rows, :] = ref[...]
        at += rows


def pad(low, own, high):
    rows = low.shape[1] + own.shape[1] + high.shape[1]
    return pl.pallas_call(
        pad_kernel,
        out_shape=jax.ShapeDtypeStruct((2, rows, HDIM), own.dtype),
        in_specs=[VMEM] * 3,
        out_specs=VMEM,
        compiler_params=pltpu.CompilerParams(vmem_limit_bytes=8 << 20),
        name="pad",
    )(low, own, high)


def attend_chunk_kernel(
    shift, heads, total_tiles, lists_ref, counts_ref, q_ref, kv_ref, out_ref, bias, scores, probs
):
    source = lax.rem(lax.axis_index("head") + heads - shift, heads)
    out_ref[...] = attend_block(
        source * BLOCK, total_tiles, lists_ref, counts_ref, q_ref, kv_ref.at[0], kv_ref.at[1],
        bias, scores, probs,
    )


def attend_chunk(shift, heads, queries, padded, tile_lists, live_counts, total_tiles):
    rows = queries.shape[0]
    pairs = BLOCK * LIST * TILE * TILE
    return pl.pallas_call(
        functools.partial(attend_chunk_kernel, shift, heads, total_tiles),
        out_shape=jax.ShapeDtypeStruct(queries.shape, queries.dtype),
        in_specs=[SMEM, SMEM, VMEM, VMEM],
        out_specs=VMEM,
        scratch_shapes=[
            pltpu.SMEM((BLOCK * LIST,), jnp.float32),
            pltpu.VMEM((rows, WINDOW * TILE), jnp.float32),
            pltpu.VMEM((rows, WINDOW * TILE), jnp.bfloat16),
        ],
        compiler_params=pltpu.CompilerParams(vmem_limit_bytes=16 << 20),
        cost_estimate=pl.CostEstimate(
            flops=4 * pairs * HDIM, bytes_accessed=padded.size * 2, transcendentals=pairs
        ),
        name="attend_chunk",
    )(tile_lists, live_counts, queries, padded)


def shift_unpack_kernel(heads, *refs):
    out_ref = refs[-1]
    me = lax.axis_index("head")
    for shift in range(heads):
        out_ref[:, column_of(lax.rem(me + shift, heads))] = refs[shift][...]


def shift_unpack(parts):
    heads, (rows, _) = len(parts), parts[0].shape
    return pl.pallas_call(
        functools.partial(shift_unpack_kernel, heads),
        out_shape=jax.ShapeDtypeStruct((rows, heads * HDIM), parts[0].dtype),
        in_specs=[VMEM] * heads,
        out_specs=VMEM,
        compiler_params=pltpu.CompilerParams(vmem_limit_bytes=8 << 20),
        name="shift_unpack",
    )(*parts)


def by_shifts(queries, keys, values, tile_lists, live_counts, total_tiles):
    heads = lax.axis_size("head")
    order = sorted(range(1, heads), key=lambda shift: -min(shift, heads - shift))

    def send(array, shift):
        return lax.ppermute(array, "head", [(i, (i + shift) % heads) for i in range(heads)])

    kv_parts, q_parts = shift_pack(queries, keys, values, heads)
    for shift in order:
        kv_parts[shift] = send(kv_parts[shift], shift)
    for shift in order:
        q_parts[shift] = send(q_parts[shift], shift)
    own = gather(kv_parts)
    low, high = halo(own, 1)
    padded = pad(low, own, high)
    outs = [None] * heads
    for shift in order + [0]:
        outs[shift] = attend_chunk(
            shift, heads, q_parts[shift], padded, tile_lists, live_counts, total_tiles
        )
        if shift:
            outs[shift] = send(outs[shift], -shift)
    return shift_unpack(outs)


def on_device(queries, keys, values, tile_lists, live_counts):
    total_tiles = tile_lists.shape[0] * lax.axis_size("ctx")
    one_block = queries.shape[0] == BLOCK * TILE
    form = by_shifts if one_block and lax.axis_size("head") <= 8 else whole_range
    return form(queries, keys, values, tile_lists, live_counts, total_tiles)


def solution(mesh):
    return jax.shard_map(
        on_device,
        mesh=mesh,
        in_specs=(
            P(("groups", "ctx", "head"), None),
            P(("groups", "ctx", "head"), None),
            P(("groups", "ctx", "head"), None),
            P(("groups", "ctx"), None),
            P(("groups", "ctx")),
        ),
        out_specs=P(("groups", "ctx", "head"), None),
        check_vma=False,
    )
```

```python
import functools
import math

import jax
import jax.numpy as jnp
from jax import lax
from jax.experimental import pallas as pl
from jax.experimental.pallas import tpu as pltpu
from jax.sharding import PartitionSpec as P

HDIM = 128
TILE = 128
EDGE = 8
LIST = 16
BLOCK = 3
WINDOW = BLOCK + LIST - 1
HIDDEN = -1e30
EXPONENT_SCALE = HDIM ** (-0.5) * math.log2(math.e)
SMEM = pl.BlockSpec(memory_space=pltpu.SMEM)
VMEM = pl.BlockSpec(memory_space=pltpu.VMEM)


def call(kernel, name, operands, in_specs, shapes, scratch=(), limit=8, cost=None):
    out_shape = jax.tree.map(
        lambda shape: shape if hasattr(shape, "dtype") else jax.ShapeDtypeStruct(shape, jnp.bfloat16),
        shapes,
        is_leaf=lambda node: isinstance(node, tuple) or hasattr(node, "dtype"),
    )
    return pl.pallas_call(
        kernel,
        out_shape=out_shape,
        in_specs=in_specs,
        out_specs=jax.tree.map(lambda _: VMEM, out_shape),
        scratch_shapes=scratch,
        compiler_params=pltpu.CompilerParams(vmem_limit_bytes=limit << 20),
        cost_estimate=cost,
        name=name,
    )(*operands)


def column_of(head):
    return pl.ds(pl.multiple_of(head * HDIM, HDIM), HDIM)


def bias_kernel(total_tiles, lists_ref, counts_ref, bias_ref):
    @pl.loop(0, lists_ref.shape[0])
    def _(row):
        own = lists_ref[row, 0]
        count = counts_ref[row]
        for entry in range(LIST):
            listed = lists_ref[row, entry]
            live = (entry < count) & (listed >= 0) & (listed < total_tiles)
            value = jnp.where(live, 0.0, HIDDEN)
            bias_ref[row, pl.ds(listed - own + EDGE, 1), :] = jnp.full((1, TILE), value, jnp.float32)


def mask_bias(tile_lists, live_counts, total_tiles):
    shape = jax.ShapeDtypeStruct((tile_lists.shape[0], LIST, TILE), jnp.float32)
    kernel = functools.partial(bias_kernel, total_tiles)
    return call(kernel, "mask_bias", (tile_lists, live_counts), [SMEM, SMEM], shape)


def attend_block(first, q_ref, kt_ref, v_ref, bias_ref, scores, probs):
    base = pl.multiple_of(first * TILE, TILE)
    for pair in range(WINDOW // 2):
        low = max(0, 2 * pair - LIST + 1)
        high = min(BLOCK - 1, 2 * pair + 1)
        part = jnp.dot(
            q_ref[low * TILE : (high + 1) * TILE, :],
            kt_ref[:, pl.ds(base + pair * 2 * TILE, 2 * TILE)],
            preferred_element_type=jnp.float32,
        )
        for tile in range(low, high + 1):
            for half in range(2):
                place = 2 * pair + half
                offset = place - tile
                if 0 <= offset < LIST:
                    rows = slice((tile - low) * TILE, (tile - low + 1) * TILE)
                    scores[tile * TILE : (tile + 1) * TILE, place * TILE : (place + 1) * TILE] = (
                        part[rows, half * TILE : (half + 1) * TILE]
                        + bias_ref[first + tile, offset : offset + 1, :]
                    )
    divisors = []
    for tile in range(BLOCK):
        rows = slice(tile * TILE, (tile + 1) * TILE)
        highest = scores[rows, tile * TILE : (tile + 1) * TILE]
        for place in range(tile + 1, tile + LIST):
            highest = jnp.maximum(highest, scores[rows, place * TILE : (place + 1) * TILE])
        highest = jnp.broadcast_to(jnp.max(highest, axis=1, keepdims=True), (TILE, TILE))
        total = jnp.zeros((TILE, TILE), jnp.float32)
        for place in range(WINDOW):
            columns = slice(place * TILE, (place + 1) * TILE)
            if 0 <= place - tile < LIST:
                weights = jnp.exp2((scores[rows, columns] - highest) * EXPONENT_SCALE)
                total += weights
                probs[rows, columns] = weights.astype(jnp.bfloat16)
            else:
                probs[rows, columns] = jnp.zeros((TILE, TILE), jnp.bfloat16)
        divisors.append(jnp.sum(total, axis=1, keepdims=True))
    mixed = jnp.dot(
        probs[...], v_ref[pl.ds(base, WINDOW * TILE), :], preferred_element_type=jnp.float32
    )
    return (mixed / jnp.concatenate(divisors, axis=0)).astype(jnp.bfloat16)


def block_scratch():
    rows = BLOCK * TILE
    return [
        pltpu.VMEM((rows, WINDOW * TILE), jnp.float32),
        pltpu.VMEM((rows, WINDOW * TILE), jnp.bfloat16),
    ]


def halo(array, dim):
    ctx = lax.axis_size("ctx")
    count = array.shape[dim]
    tail = lax.slice_in_dim(array, count - EDGE * TILE, count, axis=dim)
    head = lax.slice_in_dim(array, 0, (EDGE - 1) * TILE, axis=dim)
    low = lax.ppermute(tail, "ctx", [(i, i + 1) for i in range(ctx - 1)])
    high = lax.ppermute(head, "ctx", [(i + 1, i) for i in range(ctx - 1)])
    return low, array, high


def pack_kernel(heads, q_ref, k_ref, v_ref, q_out, k_out, v_out):
    for source, target in ((k_ref, k_out), (v_ref, v_out), (q_ref, q_out)):
        for head in range(heads):
            target[head] = source[:, head * HDIM : (head + 1) * HDIM]


def unpack_kernel(heads, parts_ref, out_ref):
    for head in range(heads):
        out_ref[:, head * HDIM : (head + 1) * HDIM] = parts_ref[head]


def attend_range_kernel(q_ref, k_low, k_own, k_high, v_low, v_own, v_high, bias_ref, out_ref, kt, v, *scratch):
    at = 0
    for k_part, v_part in ((k_low, v_low), (k_own, v_own), (k_high, v_high)):
        rows = k_part.shape[0]
        kt[:, at : at + rows] = k_part[...].T
        v[at : at + rows, :] = v_part[...]
        at += rows

    @pl.loop(0, q_ref.shape[0] // (BLOCK * TILE))
    def _(block):
        place = pl.ds(pl.multiple_of(block * BLOCK * TILE, TILE), BLOCK * TILE)
        out_ref[place, :] = attend_block(block * BLOCK, q_ref.at[place, :], kt, v, bias_ref, *scratch)


def to_heads(array):
    heads, rows, _ = array.shape
    return lax.all_to_all(array, "head", split_axis=0, concat_axis=0, tiled=True).reshape(heads * rows, HDIM)


def whole_range(queries, keys, values, bias):
    rows, columns = queries.shape
    heads = columns // HDIM
    parts = (heads, rows, HDIM)
    q_parts, k_parts, v_parts = call(
        functools.partial(pack_kernel, heads), "pack", (queries, keys, values), [VMEM] * 3, [parts] * 3
    )
    k_own, v_own = to_heads(k_parts), to_heads(v_parts)
    local_q = to_heads(q_parts)
    padded = heads * rows + (LIST - 1) * TILE
    head_out = call(
        attend_range_kernel,
        "attend_range",
        (local_q, *halo(k_own, 0), *halo(v_own, 0), bias),
        [VMEM] * 8,
        (heads * rows, HDIM),
        [pltpu.VMEM((HDIM, padded), jnp.bfloat16), pltpu.VMEM((padded, HDIM), jnp.bfloat16)] + block_scratch(),
        24,
    )
    back = lax.all_to_all(head_out.reshape(parts), "head", split_axis=0, concat_axis=0, tiled=True)
    return call(functools.partial(unpack_kernel, heads), "unpack", (back,), [VMEM], (rows, columns))


def load_kernel(heads, array_ref, *out_refs):
    me = lax.axis_index("head")
    for shift in range(heads):
        out_refs[shift][...] = array_ref[:, column_of(lax.rem(me + shift, heads))]


def load(array, heads):
    shapes = [(array.shape[0], HDIM)] * heads
    return list(call(functools.partial(load_kernel, heads), "load", (array,), [VMEM], shapes))


def turn_kernel(array_ref, *refs):
    refs[-1][...] = array_ref[...].T


def pass_kernel(array_ref, *refs):
    refs[-1][...] = array_ref[...]


def turned(array, *after):
    operands = (array, *after)
    return call(turn_kernel, "turned", operands, [VMEM] * len(operands), array.shape[::-1])


def passed(array, *after):
    operands = (array, *after)
    return call(pass_kernel, "passed", operands, [VMEM] * len(operands), array.shape)


def gather_kernel(dim, *refs):
    heads, out_ref = len(refs) - 1, refs[-1]
    me = lax.axis_index("head")
    for shift in range(heads):
        count = refs[shift].shape[dim]
        source = lax.rem(me + heads - shift, heads)
        place = pl.ds(pl.multiple_of(source * count, TILE), count)
        if dim == 0:
            out_ref[place, :] = refs[shift][...]
        else:
            out_ref[:, place] = refs[shift][...]


def gathered(parts, dim):
    shape = list(parts[0].shape)
    shape[dim] *= len(parts)
    kernel = functools.partial(gather_kernel, dim)
    return call(kernel, "gathered", parts, [VMEM] * len(parts), tuple(shape))


def pad_kernel(dim, low_ref, own_ref, high_ref, out_ref):
    at = 0
    for ref in (low_ref, own_ref, high_ref):
        count = ref.shape[dim]
        if dim == 0:
            out_ref[at : at + count, :] = ref[...]
        else:
            out_ref[:, at : at + count] = ref[...]
        at += count


def padded_range(parts, dim):
    parts = halo(gathered(parts, dim), dim)
    shape = list(parts[1].shape)
    shape[dim] += (LIST - 1) * TILE
    return call(functools.partial(pad_kernel, dim), "padded", parts, [VMEM] * 3, tuple(shape))


def attend_chunk_kernel(shift, heads, q_ref, kt_ref, v_ref, bias_ref, out_ref, *scratch):
    source = lax.rem(lax.axis_index("head") + heads - shift, heads)
    out_ref[...] = attend_block(source * BLOCK, q_ref, kt_ref, v_ref, bias_ref, *scratch)


def attend_chunk(shift, heads, queries, keys, values, bias):
    pairs = BLOCK * LIST * TILE * TILE
    return call(
        functools.partial(attend_chunk_kernel, shift, heads),
        "attend_chunk",
        (queries, keys, values, bias),
        [VMEM] * 4,
        queries.shape,
        block_scratch(),
        16,
        pl.CostEstimate(flops=4 * pairs * HDIM, bytes_accessed=1 << 20, transcendentals=pairs),
    )


def spread_kernel(heads, *refs):
    out_ref = refs[-1]
    me = lax.axis_index("head")
    for shift in range(heads):
        out_ref[:, column_of(lax.rem(me + shift, heads))] = refs[shift][...]


def by_shifts(queries, keys, values, bias):
    heads = lax.axis_size("head")
    order = sorted(range(1, heads), key=lambda shift: -min(shift, heads - shift))

    def send(array, shift):
        return lax.ppermute(array, "head", [(i, (i + shift) % heads) for i in range(heads)])

    v_parts, k_parts, q_parts = (load(array, heads) for array in (values, keys, queries))
    k_parts[0] = turned(k_parts[0])
    for shift in order:
        v_parts[shift] = send(v_parts[shift], shift)
    for shift in order:
        k_parts[shift] = send(turned(k_parts[shift], v_parts[shift]), shift)
    all_values = padded_range(v_parts, 0)
    for shift in order:
        q_parts[shift] = send(passed(q_parts[shift], k_parts[shift]), shift)
    all_keys = padded_range(k_parts, 1)
    outs = [None] * heads
    for shift in order + [0]:
        outs[shift] = attend_chunk(shift, heads, q_parts[shift], all_keys, all_values, bias)
        if shift:
            outs[shift] = send(outs[shift], -shift)
    return call(functools.partial(spread_kernel, heads), "spread", outs, [VMEM] * heads, queries.shape)


def on_device(queries, keys, values, tile_lists, live_counts):
    bias = mask_bias(tile_lists, live_counts, tile_lists.shape[0] * lax.axis_size("ctx"))
    one_block = queries.shape[0] == BLOCK * TILE
    form = by_shifts if one_block and lax.axis_size("head") <= 8 else whole_range
    return form(queries, keys, values, bias)


def solution(mesh):
    return jax.shard_map(
        on_device,
        mesh=mesh,
        in_specs=(
            P(("groups", "ctx", "head"), None),
            P(("groups", "ctx", "head"), None),
            P(("groups", "ctx", "head"), None),
            P(("groups", "ctx"), None),
            P(("groups", "ctx")),
        ),
        out_specs=P(("groups", "ctx", "head"), None),
        check_vma=False,
    )
```

```python
import functools
import math

import jax
import jax.numpy as jnp
from jax import lax
from jax.experimental import pallas as pl
from jax.experimental.pallas import tpu as pltpu
from jax.sharding import PartitionSpec as P

HDIM = 128
TILE = 128
EDGE = 8
LIST = 16
BLOCK = 3
WINDOW = BLOCK + LIST - 1
HIDDEN = -1e30
EXPONENT_SCALE = HDIM ** (-0.5) * math.log2(math.e)
SMEM = pl.BlockSpec(memory_space=pltpu.SMEM)
VMEM = pl.BlockSpec(memory_space=pltpu.VMEM)


def call(kernel, name, operands, in_specs, shapes, scratch=(), limit=8, cost=None):
    out_shape = jax.tree.map(
        lambda shape: shape if hasattr(shape, "dtype") else jax.ShapeDtypeStruct(shape, jnp.bfloat16),
        shapes,
        is_leaf=lambda node: isinstance(node, tuple) or hasattr(node, "dtype"),
    )
    return pl.pallas_call(
        kernel,
        out_shape=out_shape,
        in_specs=in_specs,
        out_specs=jax.tree.map(lambda _: VMEM, out_shape),
        scratch_shapes=scratch,
        compiler_params=pltpu.CompilerParams(vmem_limit_bytes=limit << 20),
        cost_estimate=cost,
        name=name,
    )(*operands)


def column_of(head):
    return pl.ds(pl.multiple_of(head * HDIM, HDIM), HDIM)


def rows_of(tile):
    return slice(tile * TILE, (tile + 1) * TILE)


def bias_kernel(total_tiles, lists_ref, counts_ref, bias_ref):
    bias_ref[...] = jnp.full(bias_ref.shape, HIDDEN, jnp.float32)

    @pl.loop(0, lists_ref.shape[0])
    def _(row):
        own = lists_ref[row, 0]
        count = counts_ref[row]
        for entry in range(LIST):
            listed = lists_ref[row, entry]
            live = (entry < count) & (listed >= 0) & (listed < total_tiles)
            value = jnp.where(live, 0.0, HIDDEN)
            bias_ref[row, pl.ds(row + listed - own + EDGE, 1), :] = jnp.full((1, TILE), value, jnp.float32)


def mask_bias(tile_lists, live_counts, total_tiles):
    tiles = tile_lists.shape[0]
    shape = jax.ShapeDtypeStruct((tiles, tiles + LIST - 1, TILE), jnp.float32)
    kernel = functools.partial(bias_kernel, total_tiles)
    return call(kernel, "mask_bias", (tile_lists, live_counts), [SMEM, SMEM], shape)


def attend_tiles(q_ref, kv_ref, at, count, bias_ref, row, place_of, scores, probs, before=None):
    for pair in range(count // 2):
        keys = jnp.concatenate([kv_ref[0, at + 2 * pair], kv_ref[0, at + 2 * pair + 1]], axis=1)
        part = jnp.dot(q_ref[...], keys, preferred_element_type=jnp.float32)
        for half in range(2):
            place = pl.ds(place_of(2 * pair + half), 1)
            columns = rows_of(2 * pair + half)
            for tile in range(BLOCK):
                scores[rows_of(tile), columns] = part[rows_of(tile), rows_of(half)] + bias_ref[row + tile, place, :]
    maxima, divisors, factors = [], [], []
    for tile in range(BLOCK):
        rows = rows_of(tile)
        highest = scores[rows, rows_of(0)]
        for key_tile in range(1, count):
            highest = jnp.maximum(highest, scores[rows, rows_of(key_tile)])
        highest = jnp.broadcast_to(jnp.max(highest, axis=1, keepdims=True), (TILE, TILE))
        if before:
            highest = jnp.maximum(highest, before[0][rows, :])
        total = jnp.zeros((TILE, TILE), jnp.float32)
        for key_tile in range(count):
            columns = rows_of(key_tile)
            weights = jnp.exp2((scores[rows, columns] - highest) * EXPONENT_SCALE)
            total += weights
            probs[rows, columns] = weights.astype(jnp.bfloat16)
        divisor = jnp.broadcast_to(jnp.sum(total, axis=1, keepdims=True), (TILE, TILE))
        if before:
            factors.append(jnp.exp2((before[0][rows, :] - highest) * EXPONENT_SCALE))
            divisor += before[1][rows, :] * factors[-1]
        maxima.append(highest)
        divisors.append(divisor)
    values = kv_ref[1, pl.ds(at, count)].reshape(count * TILE, HDIM)
    mixed = jnp.dot(probs[...], values, preferred_element_type=jnp.float32)
    if before:
        mixed += before[2][...] * jnp.concatenate(factors, axis=0)
    return jnp.concatenate(maxima, axis=0), jnp.concatenate(divisors, axis=0), mixed


def tile_scratch(count):
    shape = (BLOCK * TILE, count * TILE)
    return [pltpu.VMEM(shape, jnp.float32), pltpu.VMEM(shape, jnp.bfloat16)]


def attend_cost(count):
    pairs = BLOCK * count * TILE * TILE
    return pl.CostEstimate(flops=4 * pairs * HDIM, bytes_accessed=1 << 20, transcendentals=pairs)


def halo(array, dim, unit):
    ctx = lax.axis_size("ctx")
    count = array.shape[dim]
    tail = lax.slice_in_dim(array, count - EDGE * unit, count, axis=dim)
    head = lax.slice_in_dim(array, 0, (EDGE - 1) * unit, axis=dim)
    low = lax.ppermute(tail, "ctx", [(i, i + 1) for i in range(ctx - 1)])
    high = lax.ppermute(head, "ctx", [(i + 1, i) for i in range(ctx - 1)])
    return low, high


def pack_kernel(heads, q_ref, k_ref, v_ref, q_out, k_out, v_out):
    for source, target in ((k_ref, k_out), (v_ref, v_out), (q_ref, q_out)):
        for head in range(heads):
            target[head] = source[:, head * HDIM : (head + 1) * HDIM]


def unpack_kernel(heads, parts_ref, out_ref):
    for head in range(heads):
        out_ref[:, head * HDIM : (head + 1) * HDIM] = parts_ref[head]


def attend_range_kernel(q_ref, k_low, k_own, k_high, v_low, v_own, v_high, bias_ref, out_ref, kv, *scratch):
    at = 0
    for k_part, v_part in ((k_low, v_low), (k_own, v_own), (k_high, v_high)):
        for tile in range(k_part.shape[0] // TILE):
            kv[0, at] = k_part[rows_of(tile), :].T
            kv[1, at] = v_part[rows_of(tile), :]
            at += 1

    @pl.loop(0, q_ref.shape[0] // (BLOCK * TILE))
    def _(block):
        place = pl.ds(pl.multiple_of(block * BLOCK * TILE, TILE), BLOCK * TILE)
        first = block * BLOCK
        _, divisor, mixed = attend_tiles(
            q_ref.at[place, :], kv, first, WINDOW, bias_ref, first, lambda tile: first + tile, *scratch
        )
        out_ref[place, :] = (mixed / divisor).astype(jnp.bfloat16)


def to_heads(array):
    heads, rows, _ = array.shape
    return lax.all_to_all(array, "head", split_axis=0, concat_axis=0, tiled=True).reshape(heads * rows, HDIM)


def whole_range(queries, keys, values, bias):
    rows, columns = queries.shape
    heads = columns // HDIM
    parts = (heads, rows, HDIM)
    q_parts, k_parts, v_parts = call(
        functools.partial(pack_kernel, heads), "pack", (queries, keys, values), [VMEM] * 3, [parts] * 3
    )
    k_own, v_own = to_heads(k_parts), to_heads(v_parts)
    (k_low, k_high), (v_low, v_high) = halo(k_own, 0, TILE), halo(v_own, 0, TILE)
    local_q = to_heads(q_parts)
    padded = heads * rows // TILE + LIST - 1
    head_out = call(
        attend_range_kernel,
        "attend_range",
        (local_q, k_low, k_own, k_high, v_low, v_own, v_high, bias),
        [VMEM] * 8,
        (heads * rows, HDIM),
        [pltpu.VMEM((2, padded, TILE, HDIM), jnp.bfloat16)] + tile_scratch(WINDOW),
        24,
    )
    back = lax.all_to_all(head_out.reshape(parts), "head", split_axis=0, concat_axis=0, tiled=True)
    return call(functools.partial(unpack_kernel, heads), "unpack", (back,), [VMEM], (rows, columns))


def load_kv_kernel(heads, shift, k_ref, v_ref, out_ref):
    columns = column_of(lax.rem(lax.axis_index("head") + shift, heads))
    for tile in range(BLOCK):
        out_ref[0, tile] = k_ref[rows_of(tile), columns].T
        out_ref[1, tile] = v_ref[rows_of(tile), columns]


def load_q_kernel(heads, shift, q_ref, *refs):
    refs[-1][...] = q_ref[:, column_of(lax.rem(lax.axis_index("head") + shift, heads))]


def gather_kernel(*refs):
    heads, out_ref = len(refs) - 1, refs[-1]
    me = lax.axis_index("head")
    for shift in range(heads):
        out_ref[:, pl.ds(lax.rem(me + heads - shift, heads) * BLOCK, BLOCK)] = refs[shift][...]


def join_kernel(low_ref, high_ref, out_ref):
    out_ref[:, : low_ref.shape[1]] = low_ref[...]
    out_ref[:, low_ref.shape[1] :] = high_ref[...]


def first_row(shift, heads):
    return lax.rem(lax.axis_index("head") + heads - shift, heads) * BLOCK


def attend_own_kernel(shift, heads, q_ref, kv_ref, bias_ref, max_ref, divisor_ref, mixed_ref, *scratch):
    max_ref[...], divisor_ref[...], mixed_ref[...] = attend_tiles(
        q_ref, kv_ref, 0, kv_ref.shape[1], bias_ref, first_row(shift, heads), lambda tile: EDGE + tile, *scratch
    )


def attend_halo_kernel(shift, heads, own, q_ref, kv_ref, bias_ref, *refs):
    before, out_ref, scratch = refs[:3], refs[3], refs[4:]
    row = first_row(shift, heads)
    at = jnp.minimum(row, kv_ref.shape[1] - EDGE)

    def place_of(tile):
        return at + tile + jnp.where(at + tile < EDGE, 0, own)

    _, divisor, mixed = attend_tiles(
        q_ref, kv_ref, at, EDGE, bias_ref, row, place_of, *scratch, before=before
    )
    out_ref[...] = (mixed / divisor).astype(jnp.bfloat16)


def spread_kernel(heads, *refs):
    out_ref = refs[-1]
    me = lax.axis_index("head")
    for shift in range(heads):
        out_ref[:, column_of(lax.rem(me + shift, heads))] = refs[shift][...]


def by_shifts(queries, keys, values, bias):
    heads = lax.axis_size("head")
    tiles = heads * BLOCK
    order = sorted(range(1, heads), key=lambda shift: -min(shift, heads - shift))
    chunk = (queries.shape[0], HDIM)
    sums = jax.ShapeDtypeStruct(chunk, jnp.float32)

    def send(array, shift):
        return lax.ppermute(array, "head", [(i, (i + shift) % heads) for i in range(heads)])

    def kernel_of(kernel, *settings):
        return functools.partial(kernel, *settings)

    kv_parts, q_parts = [None] * heads, [None] * heads
    for shift in order + [0]:
        part = call(
            kernel_of(load_kv_kernel, heads, shift), "load_kv", (keys, values), [VMEM] * 2, (2, BLOCK, TILE, HDIM)
        )
        kv_parts[shift] = send(part, shift) if shift else part
    for shift in order + [0]:
        after = (kv_parts[shift],) if shift else ()
        part = call(
            kernel_of(load_q_kernel, heads, shift), "load_q", (queries, *after), [VMEM] * (1 + len(after)), chunk
        )
        q_parts[shift] = send(part, shift) if shift else part
    own = call(gather_kernel, "gather", kv_parts, [VMEM] * heads, (2, tiles, TILE, HDIM))
    low_high = halo(own, 1, 1)
    partial = [None] * heads
    for shift in order + [0]:
        partial[shift] = call(
            kernel_of(attend_own_kernel, shift, heads),
            "attend_own",
            (q_parts[shift], own, bias),
            [VMEM] * 3,
            [sums] * 3,
            tile_scratch(tiles),
            16,
            attend_cost(tiles),
        )
    around = call(join_kernel, "join", low_high, [VMEM] * 2, (2, LIST - 1, TILE, HDIM))
    outs = [None] * heads
    for shift in order + [0]:
        outs[shift] = call(
            kernel_of(attend_halo_kernel, shift, heads, tiles),
            "attend_halo",
            (q_parts[shift], around, bias, *partial[shift]),
            [VMEM] * 6,
            chunk,
            tile_scratch(EDGE),
            16,
            attend_cost(EDGE),
        )
        if shift:
            outs[shift] = send(outs[shift], -shift)
    return call(kernel_of(spread_kernel, heads), "spread", outs, [VMEM] * heads, queries.shape)


def on_device(queries, keys, values, tile_lists, live_counts):
    bias = mask_bias(tile_lists, live_counts, tile_lists.shape[0] * lax.axis_size("ctx"))
    heads = lax.axis_size("head")
    in_chunks = queries.shape[0] == BLOCK * TILE and heads <= 8 and heads % 2 == 0
    form = by_shifts if in_chunks and heads * BLOCK >= EDGE else whole_range
    return form(queries, keys, values, bias)


def solution(mesh):
    return jax.shard_map(
        on_device,
        mesh=mesh,
        in_specs=(
            P(("groups", "ctx", "head"), None),
            P(("groups", "ctx", "head"), None),
            P(("groups", "ctx", "head"), None),
            P(("groups", "ctx"), None),
            P(("groups", "ctx")),
        ),
        out_specs=P(("groups", "ctx", "head"), None),
        check_vma=False,
    )
```

```python
import functools
import math

import jax
import jax.numpy as jnp
from jax import lax
from jax.experimental import pallas as pl
from jax.experimental.pallas import tpu as pltpu
from jax.sharding import PartitionSpec as P

HDIM = 128
TILE = 128
EDGE = 8
LIST = 16
BLOCK = 3
WINDOW = BLOCK + LIST - 1
HIDDEN = -1e30
EXPONENT_SCALE = HDIM ** (-0.5) * math.log2(math.e)
SMEM = pl.BlockSpec(memory_space=pltpu.SMEM)
VMEM = pl.BlockSpec(memory_space=pltpu.VMEM)


def call(kernel, name, operands, in_specs, shapes, scratch=(), limit=8, cost=None):
    out_shape = jax.tree.map(
        lambda shape: shape if hasattr(shape, "dtype") else jax.ShapeDtypeStruct(shape, jnp.bfloat16),
        shapes,
        is_leaf=lambda node: isinstance(node, tuple) or hasattr(node, "dtype"),
    )
    return pl.pallas_call(
        kernel,
        out_shape=out_shape,
        in_specs=in_specs,
        out_specs=jax.tree.map(lambda _: VMEM, out_shape),
        scratch_shapes=scratch,
        compiler_params=pltpu.CompilerParams(vmem_limit_bytes=limit << 20),
        cost_estimate=cost,
        name=name,
    )(*operands)


def column_of(head):
    return pl.ds(pl.multiple_of(head * HDIM, HDIM), HDIM)


def rows_of(tile):
    return slice(tile * TILE, (tile + 1) * TILE)


def bias_kernel(total_tiles, lists_ref, counts_ref, bias_ref):
    bias_ref[...] = jnp.full(bias_ref.shape, HIDDEN, jnp.float32)

    @pl.loop(0, lists_ref.shape[0])
    def _(row):
        own = lists_ref[row, 0]
        count = counts_ref[row]
        for entry in range(LIST):
            listed = lists_ref[row, entry]
            live = (entry < count) & (listed >= 0) & (listed < total_tiles)
            value = jnp.where(live, 0.0, HIDDEN)
            bias_ref[row, pl.ds(row + listed - own + EDGE, 1), :] = jnp.full((1, TILE), value, jnp.float32)


def mask_bias(tile_lists, live_counts, total_tiles):
    tiles = tile_lists.shape[0]
    shape = jax.ShapeDtypeStruct((tiles, tiles + LIST - 1, TILE), jnp.float32)
    kernel = functools.partial(bias_kernel, total_tiles)
    return call(kernel, "mask_bias", (tile_lists, live_counts), [SMEM, SMEM], shape)


def attend_tiles(q_ref, kv_ref, at, count, bias_ref, row, place_of, scores, probs, before=None):
    for pair in range(count // 2):
        keys = jnp.concatenate([kv_ref[0, at + 2 * pair], kv_ref[0, at + 2 * pair + 1]], axis=1)
        part = jnp.dot(q_ref[...], keys, preferred_element_type=jnp.float32)
        for half in range(2):
            place = pl.ds(place_of(2 * pair + half), 1)
            columns = rows_of(2 * pair + half)
            for tile in range(BLOCK):
                scores[rows_of(tile), columns] = part[rows_of(tile), rows_of(half)] + bias_ref[row + tile, place, :]
    maxima, divisors, factors = [], [], []
    for tile in range(BLOCK):
        rows = rows_of(tile)
        highest = scores[rows, rows_of(0)]
        for key_tile in range(1, count):
            highest = jnp.maximum(highest, scores[rows, rows_of(key_tile)])
        highest = jnp.broadcast_to(jnp.max(highest, axis=1, keepdims=True), (TILE, TILE))
        if before:
            highest = jnp.maximum(highest, before[0][rows, :])
        total = jnp.zeros((TILE, TILE), jnp.float32)
        for key_tile in range(count):
            columns = rows_of(key_tile)
            weights = jnp.exp2((scores[rows, columns] - highest) * EXPONENT_SCALE)
            total += weights
            probs[rows, columns] = weights.astype(jnp.bfloat16)
        divisor = jnp.broadcast_to(jnp.sum(total, axis=1, keepdims=True), (TILE, TILE))
        if before:
            factors.append(jnp.exp2((before[0][rows, :] - highest) * EXPONENT_SCALE))
            divisor += before[1][rows, :] * factors[-1]
        maxima.append(highest)
        divisors.append(divisor)
    values = kv_ref[1, pl.ds(at, count)].reshape(count * TILE, HDIM)
    mixed = jnp.dot(probs[...], values, preferred_element_type=jnp.float32)
    if before:
        mixed += before[2][...] * jnp.concatenate(factors, axis=0)
    return jnp.concatenate(maxima, axis=0), jnp.concatenate(divisors, axis=0), mixed


def tile_scratch(count):
    shape = (BLOCK * TILE, count * TILE)
    return [pltpu.VMEM(shape, jnp.float32), pltpu.VMEM(shape, jnp.bfloat16)]


def attend_cost(count, weight=1):
    pairs = BLOCK * count * TILE * TILE * weight
    return pl.CostEstimate(flops=4 * pairs * HDIM, bytes_accessed=weight << 20, transcendentals=pairs)


def halo(array, dim, unit):
    ctx = lax.axis_size("ctx")
    count = array.shape[dim]
    tail = lax.slice_in_dim(array, count - EDGE * unit, count, axis=dim)
    head = lax.slice_in_dim(array, 0, (EDGE - 1) * unit, axis=dim)
    low = lax.ppermute(tail, "ctx", [(i, i + 1) for i in range(ctx - 1)])
    high = lax.ppermute(head, "ctx", [(i + 1, i) for i in range(ctx - 1)])
    return low, high


def pack_kernel(heads, q_ref, k_ref, v_ref, q_out, k_out, v_out):
    for source, target in ((k_ref, k_out), (v_ref, v_out), (q_ref, q_out)):
        for head in range(heads):
            target[head] = source[:, head * HDIM : (head + 1) * HDIM]


def unpack_kernel(heads, parts_ref, out_ref):
    for head in range(heads):
        out_ref[:, head * HDIM : (head + 1) * HDIM] = parts_ref[head]


def attend_range_kernel(q_ref, k_low, k_own, k_high, v_low, v_own, v_high, bias_ref, out_ref, kv, *scratch):
    at = 0
    for k_part, v_part in ((k_low, v_low), (k_own, v_own), (k_high, v_high)):
        for tile in range(k_part.shape[0] // TILE):
            kv[0, at] = k_part[rows_of(tile), :].T
            kv[1, at] = v_part[rows_of(tile), :]
            at += 1

    @pl.loop(0, q_ref.shape[0] // (BLOCK * TILE))
    def _(block):
        place = pl.ds(pl.multiple_of(block * BLOCK * TILE, TILE), BLOCK * TILE)
        first = block * BLOCK
        _, divisor, mixed = attend_tiles(
            q_ref.at[place, :], kv, first, WINDOW, bias_ref, first, lambda tile: first + tile, *scratch
        )
        out_ref[place, :] = (mixed / divisor).astype(jnp.bfloat16)


def to_heads(array):
    heads, rows, _ = array.shape
    return lax.all_to_all(array, "head", split_axis=0, concat_axis=0, tiled=True).reshape(heads * rows, HDIM)


def whole_range(queries, keys, values, bias):
    rows, columns = queries.shape
    heads = columns // HDIM
    parts = (heads, rows, HDIM)
    q_parts, k_parts, v_parts = call(
        functools.partial(pack_kernel, heads), "pack", (queries, keys, values), [VMEM] * 3, [parts] * 3
    )
    k_own, v_own = to_heads(k_parts), to_heads(v_parts)
    (k_low, k_high), (v_low, v_high) = halo(k_own, 0, TILE), halo(v_own, 0, TILE)
    local_q = to_heads(q_parts)
    padded = heads * rows // TILE + LIST - 1
    head_out = call(
        attend_range_kernel,
        "attend_range",
        (local_q, k_low, k_own, k_high, v_low, v_own, v_high, bias),
        [VMEM] * 8,
        (heads * rows, HDIM),
        [pltpu.VMEM((2, padded, TILE, HDIM), jnp.bfloat16)] + tile_scratch(WINDOW),
        24,
    )
    back = lax.all_to_all(head_out.reshape(parts), "head", split_axis=0, concat_axis=0, tiled=True)
    return call(functools.partial(unpack_kernel, heads), "unpack", (back,), [VMEM], (rows, columns))


def load_kv_kernel(heads, shift, k_ref, v_ref, out_ref):
    columns = column_of(lax.rem(lax.axis_index("head") + shift, heads))
    for tile in range(BLOCK):
        out_ref[0, tile] = k_ref[rows_of(tile), columns].T
        out_ref[1, tile] = v_ref[rows_of(tile), columns]


def load_q_kernel(heads, shift, q_ref, *refs):
    refs[-1][...] = q_ref[:, column_of(lax.rem(lax.axis_index("head") + shift, heads))]


def gather_kernel(*refs):
    heads, out_ref = len(refs) - 1, refs[-1]
    me = lax.axis_index("head")
    for shift in range(heads):
        out_ref[:, pl.ds(lax.rem(me + heads - shift, heads) * BLOCK, BLOCK)] = refs[shift][...]


def join_kernel(low_ref, high_ref, out_ref):
    out_ref[:, : low_ref.shape[1]] = low_ref[...]
    out_ref[:, low_ref.shape[1] :] = high_ref[...]


def first_row(shift, heads):
    return lax.rem(lax.axis_index("head") + heads - shift, heads) * BLOCK


def attend_own_kernel(shift, heads, q_ref, kv_ref, bias_ref, *refs):
    max_ref, divisor_ref, mixed_ref, *scratch = refs[-5:]
    max_ref[...], divisor_ref[...], mixed_ref[...] = attend_tiles(
        q_ref, kv_ref, 0, kv_ref.shape[1], bias_ref, first_row(shift, heads), lambda tile: EDGE + tile, *scratch
    )


def attend_halo_kernel(shift, heads, own, q_ref, kv_ref, bias_ref, *refs):
    before, out_ref, scratch = refs[:3], refs[3], refs[4:]
    row = first_row(shift, heads)
    at = jnp.minimum(row, kv_ref.shape[1] - EDGE)

    def place_of(tile):
        return at + tile + jnp.where(at + tile < EDGE, 0, own)

    _, divisor, mixed = attend_tiles(
        q_ref, kv_ref, at, EDGE, bias_ref, row, place_of, *scratch, before=before
    )
    out_ref[...] = (mixed / divisor).astype(jnp.bfloat16)


def spread_kernel(heads, *refs):
    out_ref = refs[-1]
    me = lax.axis_index("head")
    for shift in range(heads):
        out_ref[:, column_of(lax.rem(me + shift, heads))] = refs[shift][...]


def by_shifts(queries, keys, values, bias):
    heads = lax.axis_size("head")
    tiles = heads * BLOCK
    order = sorted(range(1, heads), key=lambda shift: -min(shift, heads - shift))
    chunk = (queries.shape[0], HDIM)
    sums = jax.ShapeDtypeStruct(chunk, jnp.float32)

    def send(array, shift):
        return lax.ppermute(array, "head", [(i, (i + shift) % heads) for i in range(heads)])

    def kernel_of(kernel, *settings):
        return functools.partial(kernel, *settings)

    kv_parts, q_parts = [None] * heads, [None] * heads
    for shift in order + [0]:
        part = call(
            kernel_of(load_kv_kernel, heads, shift), "load_kv", (keys, values), [VMEM] * 2, (2, BLOCK, TILE, HDIM)
        )
        kv_parts[shift] = send(part, shift) if shift else part
    for shift in order + [0]:
        after = (kv_parts[order[0]],) if shift else ()
        part = call(
            kernel_of(load_q_kernel, heads, shift), "load_q", (queries, *after), [VMEM] * (1 + len(after)), chunk
        )
        q_parts[shift] = send(part, shift) if shift else part
    own = call(gather_kernel, "gather", kv_parts, [VMEM] * heads, (2, tiles, TILE, HDIM))
    low_high = halo(own, 1, 1)
    partial = [None] * heads
    for shift in [0] + order:
        after = (partial[last][0],) if shift else ()
        if shift == order[0]:
            after += tuple(q_parts[other] for other in order[1:])
        last = shift
        partial[shift] = call(
            kernel_of(attend_own_kernel, shift, heads),
            "attend_own",
            (q_parts[shift], own, bias, *after),
            [VMEM] * (3 + len(after)),
            [sums] * 3,
            tile_scratch(tiles),
            16,
            attend_cost(tiles, 100 if shift else 1),
        )
    around = call(join_kernel, "join", low_high, [VMEM] * 2, (2, LIST - 1, TILE, HDIM))
    outs = [None] * heads
    for shift in order + [0]:
        outs[shift] = call(
            kernel_of(attend_halo_kernel, shift, heads, tiles),
            "attend_halo",
            (q_parts[shift], around, bias, *partial[shift]),
            [VMEM] * 6,
            chunk,
            tile_scratch(EDGE),
            16,
            attend_cost(EDGE),
        )
        if shift:
            outs[shift] = send(outs[shift], -shift)
    return call(kernel_of(spread_kernel, heads), "spread", outs, [VMEM] * heads, queries.shape)


def on_device(queries, keys, values, tile_lists, live_counts):
    bias = mask_bias(tile_lists, live_counts, tile_lists.shape[0] * lax.axis_size("ctx"))
    heads = lax.axis_size("head")
    in_chunks = queries.shape[0] == BLOCK * TILE and heads <= 8 and heads % 2 == 0
    form = by_shifts if in_chunks and heads * BLOCK >= EDGE else whole_range
    return form(queries, keys, values, bias)


def solution(mesh):
    return jax.shard_map(
        on_device,
        mesh=mesh,
        in_specs=(
            P(("groups", "ctx", "head"), None),
            P(("groups", "ctx", "head"), None),
            P(("groups", "ctx", "head"), None),
            P(("groups", "ctx"), None),
            P(("groups", "ctx")),
        ),
        out_specs=P(("groups", "ctx", "head"), None),
        check_vma=False,
    )
```

```python
import functools
import math

import jax
import jax.numpy as jnp
from jax import lax
from jax.experimental import pallas as pl
from jax.experimental.pallas import tpu as pltpu
from jax.sharding import PartitionSpec as P

HDIM = 128
TILE = 128
EDGE = 8
LIST = 16
BLOCK = 3
WINDOW = BLOCK + LIST - 1
HIDDEN = -1e30
EXPONENT_SCALE = HDIM ** (-0.5) * math.log2(math.e)
SMEM = pl.BlockSpec(memory_space=pltpu.SMEM)
VMEM = pl.BlockSpec(memory_space=pltpu.VMEM)


def call(kernel, name, operands, in_specs, shapes, scratch=(), limit=8, cost=None):
    out_shape = jax.tree.map(
        lambda shape: shape if hasattr(shape, "dtype") else jax.ShapeDtypeStruct(shape, jnp.bfloat16),
        shapes,
        is_leaf=lambda node: isinstance(node, tuple) or hasattr(node, "dtype"),
    )
    return pl.pallas_call(
        kernel,
        out_shape=out_shape,
        in_specs=in_specs,
        out_specs=jax.tree.map(lambda _: VMEM, out_shape),
        scratch_shapes=scratch,
        compiler_params=pltpu.CompilerParams(vmem_limit_bytes=limit << 20),
        cost_estimate=cost,
        name=name,
    )(*operands)


def column_of(head):
    return pl.ds(pl.multiple_of(head * HDIM, HDIM), HDIM)


def rows_of(tile):
    return slice(tile * TILE, (tile + 1) * TILE)


def bias_kernel(total_tiles, lists_ref, counts_ref, bias_ref):
    tiles, entries = lists_ref.shape
    lists = lists_ref[...]
    entry = lax.broadcasted_iota(jnp.int32, lists.shape, 1)
    row = lax.broadcasted_iota(jnp.int32, lists.shape, 0)
    live = (entry < counts_ref[...]) & (lists >= 0) & (lists < total_tiles)
    places = jnp.where(live, lists - lists[:, :1] + row + EDGE, -1)
    listed = [jnp.broadcast_to(places[:, at : at + 1], (tiles, TILE)) for at in range(entries)]
    for place in range(bias_ref.shape[0]):
        visible = listed[0] == place
        for at in range(1, entries):
            visible |= listed[at] == place
        bias_ref[place] = jnp.where(visible, 0.0, HIDDEN)


def mask_bias(tile_lists, live_counts, total_tiles):
    tiles = tile_lists.shape[0]
    shape = jax.ShapeDtypeStruct((tiles + LIST - 1, tiles, TILE), jnp.float32)
    kernel = functools.partial(bias_kernel, total_tiles)
    return call(kernel, "mask_bias", (tile_lists, live_counts[:, None]), [VMEM] * 2, shape)


def attend_block(first, q_ref, kv_ref, bias_ref, out_ref, scores, probs):
    for pair in range(WINDOW // 2):
        low = max(0, 2 * pair - LIST + 1)
        high = min(BLOCK - 1, 2 * pair + 1)
        at = first + 2 * pair
        keys = jnp.concatenate([kv_ref[0, at], kv_ref[0, at + 1]], axis=1)
        part = jnp.dot(
            q_ref[low * TILE : (high + 1) * TILE, :], keys, preferred_element_type=jnp.float32
        )
        for half in range(2):
            for tile in range(low, high + 1):
                offset = 2 * pair + half - tile
                if 0 <= offset < LIST:
                    bias = bias_ref[at + half, pl.ds(first + tile, 1), :]
                    scores[tile, :, rows_of(offset)] = part[rows_of(tile - low), rows_of(half)] + bias
    for tile in range(BLOCK):
        highest = scores[tile, :, rows_of(0)]
        for offset in range(1, LIST):
            highest = jnp.maximum(highest, scores[tile, :, rows_of(offset)])
        highest = jnp.broadcast_to(jnp.max(highest, axis=1, keepdims=True), (TILE, TILE))
        total = jnp.zeros((TILE, TILE), jnp.float32)
        for offset in range(LIST):
            weights = jnp.exp2((scores[tile, :, rows_of(offset)] - highest) * EXPONENT_SCALE)
            total += weights
            probs[tile, :, rows_of(offset)] = weights.astype(jnp.bfloat16)
        values = kv_ref[1, pl.ds(first + tile, LIST)].reshape(LIST * TILE, HDIM)
        mixed = jnp.dot(probs[tile], values, preferred_element_type=jnp.float32)
        out_ref[rows_of(tile), :] = (mixed / jnp.sum(total, axis=1, keepdims=True)).astype(jnp.bfloat16)


def block_scratch():
    shape = (BLOCK, TILE, LIST * TILE)
    return [pltpu.VMEM(shape, jnp.float32), pltpu.VMEM(shape, jnp.bfloat16)]


def cost(tile_pairs):
    pairs = tile_pairs * TILE * TILE
    return pl.CostEstimate(flops=4 * pairs * HDIM, bytes_accessed=pairs, transcendentals=pairs)


def halo(array, dim, unit):
    ctx = lax.axis_size("ctx")
    count = array.shape[dim]
    tail = lax.slice_in_dim(array, count - EDGE * unit, count, axis=dim)
    head = lax.slice_in_dim(array, 0, (EDGE - 1) * unit, axis=dim)
    low = lax.ppermute(tail, "ctx", [(i, i + 1) for i in range(ctx - 1)])
    high = lax.ppermute(head, "ctx", [(i + 1, i) for i in range(ctx - 1)])
    return low, high


def pack_kernel(heads, q_ref, k_ref, v_ref, q_out, k_out, v_out):
    for source, target in ((k_ref, k_out), (v_ref, v_out), (q_ref, q_out)):
        for head in range(heads):
            target[head] = source[:, head * HDIM : (head + 1) * HDIM]


def unpack_kernel(heads, parts_ref, out_ref):
    for head in range(heads):
        out_ref[:, head * HDIM : (head + 1) * HDIM] = parts_ref[head]


def attend_range_kernel(q_ref, k_low, k_own, k_high, v_low, v_own, v_high, bias_ref, out_ref, kv, *scratch):
    at = 0
    for k_part, v_part in ((k_low, v_low), (k_own, v_own), (k_high, v_high)):
        for tile in range(k_part.shape[0] // TILE):
            kv[0, at] = k_part[rows_of(tile), :].T
            kv[1, at] = v_part[rows_of(tile), :]
            at += 1

    @pl.loop(0, q_ref.shape[0] // (BLOCK * TILE))
    def _(block):
        place = pl.ds(pl.multiple_of(block * BLOCK * TILE, TILE), BLOCK * TILE)
        attend_block(block * BLOCK, q_ref.at[place, :], kv, bias_ref, out_ref.at[place, :], *scratch)


def to_heads(array):
    heads, rows, _ = array.shape
    return lax.all_to_all(array, "head", split_axis=0, concat_axis=0, tiled=True).reshape(heads * rows, HDIM)


def whole_range(queries, keys, values, bias):
    rows, columns = queries.shape
    heads = columns // HDIM
    parts = (heads, rows, HDIM)
    q_parts, k_parts, v_parts = call(
        functools.partial(pack_kernel, heads), "pack", (queries, keys, values), [VMEM] * 3, [parts] * 3
    )
    k_own, v_own = to_heads(k_parts), to_heads(v_parts)
    (k_low, k_high), (v_low, v_high) = halo(k_own, 0, TILE), halo(v_own, 0, TILE)
    local_q = to_heads(q_parts)
    padded = heads * rows // TILE + LIST - 1
    head_out = call(
        attend_range_kernel,
        "attend_range",
        (local_q, k_low, k_own, k_high, v_low, v_own, v_high, bias),
        [VMEM] * 8,
        (heads * rows, HDIM),
        [pltpu.VMEM((2, padded, TILE, HDIM), jnp.bfloat16)] + block_scratch(),
        24,
    )
    back = lax.all_to_all(head_out.reshape(parts), "head", split_axis=0, concat_axis=0, tiled=True)
    return call(functools.partial(unpack_kernel, heads), "unpack", (back,), [VMEM], (rows, columns))


def load_kv_kernel(heads, shift, k_ref, v_ref, out_ref):
    columns = column_of(lax.rem(lax.axis_index("head") + shift, heads))
    for tile in range(BLOCK):
        out_ref[0, tile] = k_ref[rows_of(tile), columns].T
        out_ref[1, tile] = v_ref[rows_of(tile), columns]


def load_q_kernel(heads, shift, q_ref, *refs):
    refs[-1][...] = q_ref[:, column_of(lax.rem(lax.axis_index("head") + shift, heads))]


def gather_kernel(*refs):
    heads, out_ref = len(refs) - 1, refs[-1]
    me = lax.axis_index("head")
    for shift in range(heads):
        out_ref[:, pl.ds(lax.rem(me + heads - shift, heads) * BLOCK, BLOCK)] = refs[shift][...]


def join_kernel(*refs):
    at = 0
    for ref in refs[:-1]:
        refs[-1][:, at : at + ref.shape[1]] = ref[...]
        at += ref.shape[1]


def pass_kernel(array_ref, *refs):
    refs[-1][...] = array_ref[...]


def stack_kernel(*refs):
    for at, ref in enumerate(refs[:-1]):
        refs[-1][at] = ref[...]


def attend_chunk_kernel(shift, heads, q_ref, kv_ref, bias_ref, *refs):
    out_ref, *scratch = refs[-3:]
    source = lax.rem(lax.axis_index("head") + heads - shift, heads)
    attend_block(source * BLOCK, q_ref.at[shift], kv_ref, bias_ref, out_ref, *scratch)


def spread_kernel(heads, *refs):
    out_ref = refs[-1]
    me = lax.axis_index("head")
    for shift in range(heads):
        out_ref[:, column_of(lax.rem(me + shift, heads))] = refs[shift][...]


def by_shifts(queries, keys, values, bias):
    heads = lax.axis_size("head")
    tiles = heads * BLOCK
    order = sorted(range(1, heads), key=lambda shift: -min(shift, heads - shift))
    chunk = (queries.shape[0], HDIM)

    def send(array, shift):
        return lax.ppermute(array, "head", [(i, (i + shift) % heads) for i in range(heads)])

    def kernel_of(kernel, *settings):
        return functools.partial(kernel, *settings)

    kv_parts, q_parts = [None] * heads, [None] * heads
    for shift in order + [0]:
        part = call(
            kernel_of(load_kv_kernel, heads, shift), "load_kv", (keys, values), [VMEM] * 2, (2, BLOCK, TILE, HDIM)
        )
        kv_parts[shift] = send(part, shift) if shift else part
    for shift in order + [0]:
        after = (kv_parts[order[0]],) if shift else ()
        part = call(
            kernel_of(load_q_kernel, heads, shift), "load_q", (queries, *after), [VMEM] * (1 + len(after)), chunk
        )
        q_parts[shift] = send(part, shift) if shift else part
    own = call(gather_kernel, "gather", kv_parts, [VMEM] * heads, (2, tiles, TILE, HDIM))
    low, high = halo(own, 1, 1)
    local_q = call(stack_kernel, "stack", q_parts, [VMEM] * heads, (heads, *chunk), cost=cost(1 << 14))
    padded = call(join_kernel, "join", (low, own, high), [VMEM] * 3, (2, tiles + LIST - 1, TILE, HDIM))
    outs = [None] * heads
    after = ()
    for shift in order + [0]:
        outs[shift] = call(
            kernel_of(attend_chunk_kernel, shift, heads),
            "attend_chunk",
            (local_q, padded, bias, *after),
            [VMEM] * (3 + len(after)),
            chunk,
            block_scratch(),
            16,
            cost(BLOCK * LIST // 2 if shift else 1),
        )
        after = (outs[shift],)
        if shift:
            outs[shift] = send(outs[shift], -shift)
    after = ()
    for shift in order:
        operands = (outs[shift], *after)
        outs[shift] = call(
            pass_kernel, "landed", operands, [VMEM] * len(operands), chunk, cost=cost(BLOCK * LIST // 2)
        )
        after = (outs[shift],)
    return call(kernel_of(spread_kernel, heads), "spread", outs, [VMEM] * heads, queries.shape)


def on_device(queries, keys, values, tile_lists, live_counts):
    bias = mask_bias(tile_lists, live_counts, tile_lists.shape[0] * lax.axis_size("ctx"))
    heads = lax.axis_size("head")
    in_chunks = queries.shape[0] == BLOCK * TILE and heads <= 8 and heads % 2 == 0
    form = by_shifts if in_chunks and heads * BLOCK >= EDGE else whole_range
    return form(queries, keys, values, bias)


def solution(mesh):
    return jax.shard_map(
        on_device,
        mesh=mesh,
        in_specs=(
            P(("groups", "ctx", "head"), None),
            P(("groups", "ctx", "head"), None),
            P(("groups", "ctx", "head"), None),
            P(("groups", "ctx"), None),
            P(("groups", "ctx")),
        ),
        out_specs=P(("groups", "ctx", "head"), None),
        check_vma=False,
    )
```

```python
import functools
import math

import jax
import jax.numpy as jnp
from jax import lax
from jax.experimental import pallas as pl
from jax.experimental.pallas import tpu as pltpu
from jax.sharding import PartitionSpec as P

HDIM = 128
TILE = 128
EDGE = 8
LIST = 16
BLOCK = 3
WINDOW = BLOCK + LIST - 1
HIDDEN = -1e30
EXPONENT_SCALE = HDIM ** (-0.5) * math.log2(math.e)
SMEM = pl.BlockSpec(memory_space=pltpu.SMEM)
VMEM = pl.BlockSpec(memory_space=pltpu.VMEM)


def call(kernel, name, operands, in_specs, shapes, scratch=(), limit=8, cost=None):
    out_shape = jax.tree.map(
        lambda shape: shape if hasattr(shape, "dtype") else jax.ShapeDtypeStruct(shape, jnp.bfloat16),
        shapes,
        is_leaf=lambda node: isinstance(node, tuple) or hasattr(node, "dtype"),
    )
    return pl.pallas_call(
        kernel,
        out_shape=out_shape,
        in_specs=in_specs,
        out_specs=jax.tree.map(lambda _: VMEM, out_shape),
        scratch_shapes=scratch,
        compiler_params=pltpu.CompilerParams(vmem_limit_bytes=limit << 20),
        cost_estimate=cost,
        name=name,
    )(*operands)


def column_of(head):
    return pl.ds(pl.multiple_of(head * HDIM, HDIM), HDIM)


def rows_of(tile):
    return slice(tile * TILE, (tile + 1) * TILE)


def bias_kernel(total_tiles, lists_ref, counts_ref, bias_ref):
    tiles, entries = lists_ref.shape
    lists = lists_ref[...]
    entry = lax.broadcasted_iota(jnp.int32, lists.shape, 1)
    row = lax.broadcasted_iota(jnp.int32, lists.shape, 0)
    live = (entry < counts_ref[...]) & (lists >= 0) & (lists < total_tiles)
    places = jnp.where(live, lists - lists[:, :1] + row + EDGE, -1)
    listed = [jnp.broadcast_to(places[:, at : at + 1], (tiles, TILE)) for at in range(entries)]
    for place in range(bias_ref.shape[0]):
        visible = listed[0] == place
        for at in range(1, entries):
            visible |= listed[at] == place
        bias_ref[place] = jnp.where(visible, 0.0, HIDDEN)


def mask_bias(tile_lists, live_counts, total_tiles):
    tiles = tile_lists.shape[0]
    shape = jax.ShapeDtypeStruct((tiles + LIST - 1, tiles, TILE), jnp.float32)
    kernel = functools.partial(bias_kernel, total_tiles)
    return call(kernel, "mask_bias", (tile_lists, live_counts[:, None]), [VMEM] * 2, shape)


def attend_block(first, q_ref, kt_ref, v_ref, bias_ref, out_ref, scores, probs):
    for pair in range(WINDOW // 2):
        low = max(0, 2 * pair - LIST + 1)
        high = min(BLOCK - 1, 2 * pair + 1)
        at = first + 2 * pair
        keys = jnp.concatenate([kt_ref[at], kt_ref[at + 1]], axis=1)
        part = jnp.dot(
            q_ref[low * TILE : (high + 1) * TILE, :], keys, preferred_element_type=jnp.float32
        )
        for half in range(2):
            for tile in range(low, high + 1):
                offset = 2 * pair + half - tile
                if 0 <= offset < LIST:
                    bias = bias_ref[at + half, pl.ds(first + tile, 1), :]
                    scores[tile, :, rows_of(offset)] = part[rows_of(tile - low), rows_of(half)] + bias
    for tile in range(BLOCK):
        highest = scores[tile, :, rows_of(0)]
        for offset in range(1, LIST):
            highest = jnp.maximum(highest, scores[tile, :, rows_of(offset)])
        highest = jnp.broadcast_to(jnp.max(highest, axis=1, keepdims=True), (TILE, TILE))
        total = jnp.zeros((TILE, TILE), jnp.float32)
        for offset in range(LIST):
            weights = jnp.exp2((scores[tile, :, rows_of(offset)] - highest) * EXPONENT_SCALE)
            total += weights
            probs[tile, :, rows_of(offset)] = weights.astype(jnp.bfloat16)
        values = v_ref[pl.ds(first + tile, LIST)].reshape(LIST * TILE, HDIM)
        mixed = jnp.dot(probs[tile], values, preferred_element_type=jnp.float32)
        out_ref[rows_of(tile), :] = (mixed / jnp.sum(total, axis=1, keepdims=True)).astype(jnp.bfloat16)


def block_scratch():
    shape = (BLOCK, TILE, LIST * TILE)
    return [pltpu.VMEM(shape, jnp.float32), pltpu.VMEM(shape, jnp.bfloat16)]


def cost(tile_pairs):
    pairs = tile_pairs * TILE * TILE
    return pl.CostEstimate(flops=4 * pairs * HDIM, bytes_accessed=pairs, transcendentals=pairs)


def halo(array, dim, unit):
    ctx = lax.axis_size("ctx")
    count = array.shape[dim]
    tail = lax.slice_in_dim(array, count - EDGE * unit, count, axis=dim)
    head = lax.slice_in_dim(array, 0, (EDGE - 1) * unit, axis=dim)
    low = lax.ppermute(tail, "ctx", [(i, i + 1) for i in range(ctx - 1)])
    high = lax.ppermute(head, "ctx", [(i + 1, i) for i in range(ctx - 1)])
    return low, high


def pack_kernel(heads, q_ref, k_ref, v_ref, q_out, k_out, v_out):
    for source, target in ((k_ref, k_out), (v_ref, v_out), (q_ref, q_out)):
        for head in range(heads):
            target[head] = source[:, head * HDIM : (head + 1) * HDIM]


def unpack_kernel(heads, parts_ref, out_ref):
    for head in range(heads):
        out_ref[:, head * HDIM : (head + 1) * HDIM] = parts_ref[head]


def attend_range_kernel(q_ref, k_low, k_own, k_high, v_low, v_own, v_high, bias_ref, out_ref, kt, v, *scratch):
    at = 0
    for k_part, v_part in ((k_low, v_low), (k_own, v_own), (k_high, v_high)):
        for tile in range(k_part.shape[0] // TILE):
            kt[at] = k_part[rows_of(tile), :].T
            v[at] = v_part[rows_of(tile), :]
            at += 1

    @pl.loop(0, q_ref.shape[0] // (BLOCK * TILE))
    def _(block):
        place = pl.ds(pl.multiple_of(block * BLOCK * TILE, TILE), BLOCK * TILE)
        attend_block(block * BLOCK, q_ref.at[place, :], kt, v, bias_ref, out_ref.at[place, :], *scratch)


def to_heads(array):
    heads, rows, _ = array.shape
    return lax.all_to_all(array, "head", split_axis=0, concat_axis=0, tiled=True).reshape(heads * rows, HDIM)


def whole_range(queries, keys, values, bias):
    rows, columns = queries.shape
    heads = columns // HDIM
    parts = (heads, rows, HDIM)
    q_parts, k_parts, v_parts = call(
        functools.partial(pack_kernel, heads), "pack", (queries, keys, values), [VMEM] * 3, [parts] * 3
    )
    k_own, v_own = to_heads(k_parts), to_heads(v_parts)
    (k_low, k_high), (v_low, v_high) = halo(k_own, 0, TILE), halo(v_own, 0, TILE)
    local_q = to_heads(q_parts)
    padded = heads * rows // TILE + LIST - 1
    head_out = call(
        attend_range_kernel,
        "attend_range",
        (local_q, k_low, k_own, k_high, v_low, v_own, v_high, bias),
        [VMEM] * 8,
        (heads * rows, HDIM),
        [pltpu.VMEM((padded, TILE, HDIM), jnp.bfloat16)] * 2 + block_scratch(),
        24,
    )
    back = lax.all_to_all(head_out.reshape(parts), "head", split_axis=0, concat_axis=0, tiled=True)
    return call(functools.partial(unpack_kernel, heads), "unpack", (back,), [VMEM], (rows, columns))


def load_tiles_kernel(heads, shift, turn, array_ref, *refs):
    columns = column_of(lax.rem(lax.axis_index("head") + shift, heads))
    for tile in range(BLOCK):
        part = array_ref[rows_of(tile), columns]
        refs[-1][tile] = part.T if turn else part


def load_q_kernel(heads, shift, q_ref, *refs):
    refs[-1][...] = q_ref[:, column_of(lax.rem(lax.axis_index("head") + shift, heads))]


def gather_kernel(*refs):
    heads, out_ref = len(refs) - 1, refs[-1]
    me = lax.axis_index("head")
    for shift in range(heads):
        out_ref[pl.ds(lax.rem(me + heads - shift, heads) * BLOCK, BLOCK)] = refs[shift][...]


def join_kernel(*refs):
    at = 0
    for ref in refs[:-1]:
        refs[-1][at : at + ref.shape[0]] = ref[...]
        at += ref.shape[0]


def with_halo(parts):
    heads = len(parts)
    tiles = heads * BLOCK
    own = call(gather_kernel, "gather", parts, [VMEM] * heads, (tiles, TILE, HDIM))
    low, high = halo(own, 0, 1)
    return call(join_kernel, "join", (low, own, high), [VMEM] * 3, (tiles + LIST - 1, TILE, HDIM))


def pass_kernel(array_ref, *refs):
    refs[-1][...] = array_ref[...]


def attend_chunk_kernel(shift, heads, q_ref, kt_ref, v_ref, bias_ref, *refs):
    out_ref, *scratch = refs[-3:]
    source = lax.rem(lax.axis_index("head") + heads - shift, heads)
    attend_block(source * BLOCK, q_ref, kt_ref, v_ref, bias_ref, out_ref, *scratch)


def spread_kernel(heads, *refs):
    out_ref = refs[-1]
    me = lax.axis_index("head")
    for shift in range(heads):
        out_ref[:, column_of(lax.rem(me + shift, heads))] = refs[shift][...]


def by_shifts(queries, keys, values, bias):
    heads = lax.axis_size("head")
    order = sorted(range(1, heads), key=lambda shift: -min(shift, heads - shift))
    chunk, tiles = (queries.shape[0], HDIM), (BLOCK, TILE, HDIM)

    def kernel_of(kernel, *settings):
        return functools.partial(kernel, *settings)

    def call_after(kernel, name, operands, after, shape):
        operands = (*operands, *after)
        return call(kernel, name, operands, [VMEM] * len(operands), shape)

    def send(array, shift):
        return lax.ppermute(array, "head", [(i, (i + shift) % heads) for i in range(heads)])

    v_parts, k_parts, q_parts = [None] * heads, [None] * heads, [None] * heads
    for shift in order + [0]:
        part = call_after(kernel_of(load_tiles_kernel, heads, shift, False), "load_v", (values,), (), tiles)
        v_parts[shift] = send(part, shift) if shift else part
    for shift in order + [0]:
        after = [v_parts[shift]] if shift else []
        if shift == order[-1]:
            after.append(bias)
        part = call_after(kernel_of(load_tiles_kernel, heads, shift, True), "load_k", (keys,), after, tiles)
        k_parts[shift] = send(part, shift) if shift else part
    for shift in order + [0]:
        after = (k_parts[shift],) if shift else ()
        part = call_after(kernel_of(load_q_kernel, heads, shift), "load_q", (queries,), after, chunk)
        q_parts[shift] = send(part, shift) if shift else part
    all_values, all_keys = with_halo(v_parts), with_halo(k_parts)
    outs = [None] * heads
    after = ()
    for shift in order + [0]:
        operands = (q_parts[shift], all_keys, all_values, bias, *after)
        outs[shift] = call(
            kernel_of(attend_chunk_kernel, shift, heads),
            "attend_chunk",
            operands,
            [VMEM] * len(operands),
            chunk,
            block_scratch(),
            16,
            cost(BLOCK * LIST // 2 if shift else 1),
        )
        after = (outs[shift],)
        if shift:
            outs[shift] = send(outs[shift], -shift)
    after = ()
    for shift in order:
        operands = (outs[shift], *after)
        outs[shift] = call(
            pass_kernel, "landed", operands, [VMEM] * len(operands), chunk, cost=cost(BLOCK * LIST // 2)
        )
        after = (outs[shift],)
    return call(kernel_of(spread_kernel, heads), "spread", outs, [VMEM] * heads, queries.shape)


def on_device(queries, keys, values, tile_lists, live_counts):
    bias = mask_bias(tile_lists, live_counts, tile_lists.shape[0] * lax.axis_size("ctx"))
    heads = lax.axis_size("head")
    in_chunks = queries.shape[0] == BLOCK * TILE and heads <= 8 and heads % 2 == 0
    form = by_shifts if in_chunks and heads * BLOCK >= EDGE else whole_range
    return form(queries, keys, values, bias)


def solution(mesh):
    return jax.shard_map(
        on_device,
        mesh=mesh,
        in_specs=(
            P(("groups", "ctx", "head"), None),
            P(("groups", "ctx", "head"), None),
            P(("groups", "ctx", "head"), None),
            P(("groups", "ctx"), None),
            P(("groups", "ctx")),
        ),
        out_specs=P(("groups", "ctx", "head"), None),
        check_vma=False,
    )
```

```python
import functools
import math

import jax
import jax.numpy as jnp
from jax import lax
from jax.experimental import pallas as pl
from jax.experimental.pallas import tpu as pltpu
from jax.sharding import PartitionSpec as P

HDIM = 128
TILE = 128
EDGE = 8
LIST = 16
BLOCK = 3
WINDOW = BLOCK + LIST - 1
HIDDEN = -1e30
EXPONENT_SCALE = HDIM ** (-0.5) * math.log2(math.e)
SMEM = pl.BlockSpec(memory_space=pltpu.SMEM)
VMEM = pl.BlockSpec(memory_space=pltpu.VMEM)


def call(kernel, name, operands, in_specs, shapes, scratch=(), limit=8, cost=None):
    out_shape = jax.tree.map(
        lambda shape: shape if hasattr(shape, "dtype") else jax.ShapeDtypeStruct(shape, jnp.bfloat16),
        shapes,
        is_leaf=lambda node: isinstance(node, tuple) or hasattr(node, "dtype"),
    )
    return pl.pallas_call(
        kernel,
        out_shape=out_shape,
        in_specs=in_specs,
        out_specs=jax.tree.map(lambda _: VMEM, out_shape),
        scratch_shapes=scratch,
        compiler_params=pltpu.CompilerParams(vmem_limit_bytes=limit << 20),
        cost_estimate=cost,
        name=name,
    )(*operands)


def column_of(head):
    return pl.ds(pl.multiple_of(head * HDIM, HDIM), HDIM)


def rows_of(tile):
    return slice(tile * TILE, (tile + 1) * TILE)


def bias_kernel(total_tiles, lists_ref, counts_ref, bias_ref):
    tiles, entries = lists_ref.shape
    lists = lists_ref[...]
    entry = lax.broadcasted_iota(jnp.int32, lists.shape, 1)
    row = lax.broadcasted_iota(jnp.int32, lists.shape, 0)
    live = (entry < counts_ref[...]) & (lists >= 0) & (lists < total_tiles)
    places = jnp.where(live, lists - lists[:, :1] + row + EDGE, -1)
    listed = [jnp.broadcast_to(places[:, at : at + 1], (tiles, TILE)) for at in range(entries)]
    for place in range(bias_ref.shape[0]):
        visible = listed[0] == place
        for at in range(1, entries):
            visible |= listed[at] == place
        bias_ref[place] = jnp.where(visible, 0.0, HIDDEN)


def mask_bias(tile_lists, live_counts, total_tiles):
    tiles = tile_lists.shape[0]
    shape = jax.ShapeDtypeStruct((tiles + LIST - 1, tiles, TILE), jnp.float32)
    kernel = functools.partial(bias_kernel, total_tiles)
    return call(kernel, "mask_bias", (tile_lists, live_counts[:, None]), [VMEM] * 2, shape)


def attend_block(first, q_ref, kt_ref, v_ref, bias_ref, out_ref, scores, probs):
    for pair in range(WINDOW // 2):
        low = max(0, 2 * pair - LIST + 1)
        high = min(BLOCK - 1, 2 * pair + 1)
        at = first + 2 * pair
        keys = jnp.concatenate([kt_ref[at], kt_ref[at + 1]], axis=1)
        part = jnp.dot(
            q_ref[low * TILE : (high + 1) * TILE, :], keys, preferred_element_type=jnp.float32
        )
        for half in range(2):
            for tile in range(low, high + 1):
                offset = 2 * pair + half - tile
                if 0 <= offset < LIST:
                    bias = bias_ref[at + half, pl.ds(first + tile, 1), :]
                    scores[tile, :, rows_of(offset)] = part[rows_of(tile - low), rows_of(half)] + bias
    for tile in range(BLOCK):
        highest = scores[tile, :, rows_of(0)]
        for offset in range(1, LIST):
            highest = jnp.maximum(highest, scores[tile, :, rows_of(offset)])
        highest = jnp.broadcast_to(jnp.max(highest, axis=1, keepdims=True), (TILE, TILE))
        total = jnp.zeros((TILE, TILE), jnp.float32)
        for offset in range(LIST):
            weights = jnp.exp2((scores[tile, :, rows_of(offset)] - highest) * EXPONENT_SCALE)
            total += weights
            probs[tile, :, rows_of(offset)] = weights.astype(jnp.bfloat16)
        values = v_ref[pl.ds(first + tile, LIST)].reshape(LIST * TILE, HDIM)
        mixed = jnp.dot(probs[tile], values, preferred_element_type=jnp.float32)
        out_ref[rows_of(tile), :] = (mixed / jnp.sum(total, axis=1, keepdims=True)).astype(jnp.bfloat16)


def block_scratch():
    shape = (BLOCK, TILE, LIST * TILE)
    return [pltpu.VMEM(shape, jnp.float32), pltpu.VMEM(shape, jnp.bfloat16)]


def cost(tile_pairs):
    pairs = tile_pairs * TILE * TILE
    return pl.CostEstimate(flops=4 * pairs * HDIM, bytes_accessed=pairs, transcendentals=pairs)


def halo(array, dim, unit):
    ctx = lax.axis_size("ctx")
    count = array.shape[dim]
    tail = lax.slice_in_dim(array, count - EDGE * unit, count, axis=dim)
    head = lax.slice_in_dim(array, 0, (EDGE - 1) * unit, axis=dim)
    low = lax.ppermute(tail, "ctx", [(i, i + 1) for i in range(ctx - 1)])
    high = lax.ppermute(head, "ctx", [(i + 1, i) for i in range(ctx - 1)])
    return low, high


def pack_kernel(heads, q_ref, k_ref, v_ref, q_out, k_out, v_out):
    for source, target in ((k_ref, k_out), (v_ref, v_out), (q_ref, q_out)):
        for head in range(heads):
            target[head] = source[:, head * HDIM : (head + 1) * HDIM]


def unpack_kernel(heads, parts_ref, out_ref):
    for head in range(heads):
        out_ref[:, head * HDIM : (head + 1) * HDIM] = parts_ref[head]


def attend_range_kernel(q_ref, k_low, k_own, k_high, v_low, v_own, v_high, bias_ref, out_ref, kt, v, *scratch):
    at = 0
    for k_part, v_part in ((k_low, v_low), (k_own, v_own), (k_high, v_high)):
        for tile in range(k_part.shape[0] // TILE):
            kt[at] = k_part[rows_of(tile), :].T
            v[at] = v_part[rows_of(tile), :]
            at += 1

    @pl.loop(0, q_ref.shape[0] // (BLOCK * TILE))
    def _(block):
        place = pl.ds(pl.multiple_of(block * BLOCK * TILE, TILE), BLOCK * TILE)
        attend_block(block * BLOCK, q_ref.at[place, :], kt, v, bias_ref, out_ref.at[place, :], *scratch)


def to_heads(array):
    heads, rows, _ = array.shape
    return lax.all_to_all(array, "head", split_axis=0, concat_axis=0, tiled=True).reshape(heads * rows, HDIM)


def whole_range(queries, keys, values, bias):
    rows, columns = queries.shape
    heads = columns // HDIM
    parts = (heads, rows, HDIM)
    q_parts, k_parts, v_parts = call(
        functools.partial(pack_kernel, heads), "pack", (queries, keys, values), [VMEM] * 3, [parts] * 3
    )
    k_own, v_own = to_heads(k_parts), to_heads(v_parts)
    (k_low, k_high), (v_low, v_high) = halo(k_own, 0, TILE), halo(v_own, 0, TILE)
    local_q = to_heads(q_parts)
    padded = heads * rows // TILE + LIST - 1
    head_out = call(
        attend_range_kernel,
        "attend_range",
        (local_q, k_low, k_own, k_high, v_low, v_own, v_high, bias),
        [VMEM] * 8,
        (heads * rows, HDIM),
        [pltpu.VMEM((padded, TILE, HDIM), jnp.bfloat16)] * 2 + block_scratch(),
        24,
    )
    back = lax.all_to_all(head_out.reshape(parts), "head", split_axis=0, concat_axis=0, tiled=True)
    return call(functools.partial(unpack_kernel, heads), "unpack", (back,), [VMEM], (rows, columns))


def load_kernel(heads, shift, k_ref, v_ref, q_ref, out_ref):
    columns = column_of(lax.rem(lax.axis_index("head") + shift, heads))
    for tile in range(BLOCK):
        out_ref[0, tile] = k_ref[rows_of(tile), columns].T
        out_ref[1, tile] = v_ref[rows_of(tile), columns]
        out_ref[2, tile] = q_ref[rows_of(tile), columns]


def gather_kernel(*refs):
    *parts, kv_out, q_out = refs
    me = lax.axis_index("head")
    for shift, part in enumerate(parts):
        place = pl.ds(lax.rem(me + len(parts) - shift, len(parts)) * BLOCK, BLOCK)
        kv_out[:, place] = part[:2]
        for tile in range(BLOCK):
            q_out[shift, rows_of(tile), :] = part[2, tile]


def join_kernel(*refs):
    at = 0
    for ref in refs[:-1]:
        refs[-1][:, at : at + ref.shape[1]] = ref[...]
        at += ref.shape[1]


def pass_kernel(array_ref, *refs):
    refs[-1][...] = array_ref[...]


def attend_chunk_kernel(shift, heads, q_ref, kv_ref, bias_ref, *refs):
    out_ref, *scratch = refs[-3:]
    source = lax.rem(lax.axis_index("head") + heads - shift, heads)
    attend_block(
        source * BLOCK, q_ref.at[shift], kv_ref.at[0], kv_ref.at[1], bias_ref, out_ref, *scratch
    )


def spread_kernel(heads, *refs):
    out_ref = refs[-1]
    me = lax.axis_index("head")
    for shift in range(heads):
        out_ref[:, column_of(lax.rem(me + shift, heads))] = refs[shift][...]


def by_shifts(queries, keys, values, bias):
    heads = lax.axis_size("head")
    order = sorted(range(1, heads), key=lambda shift: -min(shift, heads - shift))
    chunk, tiles = (queries.shape[0], HDIM), heads * BLOCK

    def kernel_of(kernel, *settings):
        return functools.partial(kernel, *settings)

    def send(array, shift):
        return lax.ppermute(array, "head", [(i, (i + shift) % heads) for i in range(heads)])

    parts = [None] * heads
    for shift in order + [0]:
        part = call(
            kernel_of(load_kernel, heads, shift),
            "load",
            (keys, values, queries),
            [VMEM] * 3,
            (3, BLOCK, TILE, HDIM),
        )
        parts[shift] = send(part, shift) if shift else part
    own, local_q = call(
        gather_kernel, "gather", parts, [VMEM] * heads, [(2, tiles, TILE, HDIM), (heads, *chunk)]
    )
    low, high = halo(own, 1, 1)
    padded = call(join_kernel, "join", (low, own, high), [VMEM] * 3, (2, tiles + LIST - 1, TILE, HDIM))
    outs = [None] * heads
    after = ()
    for shift in order + [0]:
        operands = (local_q, padded, bias, *after)
        outs[shift] = call(
            kernel_of(attend_chunk_kernel, shift, heads),
            "attend_chunk",
            operands,
            [VMEM] * len(operands),
            chunk,
            block_scratch(),
            16,
            cost(BLOCK * LIST // 2 if shift else 1),
        )
        after = (outs[shift],)
        if shift:
            outs[shift] = send(outs[shift], -shift)
    after = ()
    for shift in order:
        operands = (outs[shift], *after)
        outs[shift] = call(
            pass_kernel, "landed", operands, [VMEM] * len(operands), chunk, cost=cost(BLOCK * LIST // 2)
        )
        after = (outs[shift],)
    return call(kernel_of(spread_kernel, heads), "spread", outs, [VMEM] * heads, queries.shape)


def on_device(queries, keys, values, tile_lists, live_counts):
    bias = mask_bias(tile_lists, live_counts, tile_lists.shape[0] * lax.axis_size("ctx"))
    heads = lax.axis_size("head")
    in_chunks = queries.shape[0] == BLOCK * TILE and heads <= 8 and heads % 2 == 0
    form = by_shifts if in_chunks and heads * BLOCK >= EDGE else whole_range
    return form(queries, keys, values, bias)


def solution(mesh):
    return jax.shard_map(
        on_device,
        mesh=mesh,
        in_specs=(
            P(("groups", "ctx", "head"), None),
            P(("groups", "ctx", "head"), None),
            P(("groups", "ctx", "head"), None),
            P(("groups", "ctx"), None),
            P(("groups", "ctx")),
        ),
        out_specs=P(("groups", "ctx", "head"), None),
        check_vma=False,
    )
```

```python
import functools
import math

import jax
import jax.numpy as jnp
from jax import lax
from jax.experimental import pallas as pl
from jax.experimental.pallas import tpu as pltpu
from jax.sharding import PartitionSpec as P

HDIM = 128
TILE = 128
EDGE = 8
LIST = 16
BLOCK = 3
WINDOW = BLOCK + LIST - 1
HIDDEN = -1e30
EXPONENT_SCALE = HDIM ** (-0.5) * math.log2(math.e)
SMEM = pl.BlockSpec(memory_space=pltpu.SMEM)
VMEM = pl.BlockSpec(memory_space=pltpu.VMEM)


def call(kernel, name, operands, in_specs, shapes, scratch=(), limit=8, cost=None):
    out_shape = jax.tree.map(
        lambda shape: shape if hasattr(shape, "dtype") else jax.ShapeDtypeStruct(shape, jnp.bfloat16),
        shapes,
        is_leaf=lambda node: isinstance(node, tuple) or hasattr(node, "dtype"),
    )
    return pl.pallas_call(
        kernel,
        out_shape=out_shape,
        in_specs=in_specs,
        out_specs=jax.tree.map(lambda _: VMEM, out_shape),
        scratch_shapes=scratch,
        compiler_params=pltpu.CompilerParams(vmem_limit_bytes=limit << 20),
        cost_estimate=cost,
        name=name,
    )(*operands)


def column_of(head):
    return pl.ds(pl.multiple_of(head * HDIM, HDIM), HDIM)


def rows_of(tile):
    return slice(tile * TILE, (tile + 1) * TILE)


def bias_kernel(total_tiles, lists_ref, counts_ref, bias_ref):
    tiles, entries = lists_ref.shape
    lists = lists_ref[...]
    entry = lax.broadcasted_iota(jnp.int32, lists.shape, 1)
    row = lax.broadcasted_iota(jnp.int32, lists.shape, 0)
    live = (entry < counts_ref[...]) & (lists >= 0) & (lists < total_tiles)
    places = jnp.where(live, lists - lists[:, :1] + row + EDGE, -1)
    listed = [jnp.broadcast_to(places[:, at : at + 1], (tiles, TILE)) for at in range(entries)]
    for place in range(bias_ref.shape[0]):
        visible = listed[0] == place
        for at in range(1, entries):
            visible |= listed[at] == place
        bias_ref[place] = jnp.where(visible, 0.0, HIDDEN)


def mask_bias(tile_lists, live_counts, total_tiles):
    tiles = tile_lists.shape[0]
    shape = jax.ShapeDtypeStruct((tiles + LIST - 1, tiles, TILE), jnp.float32)
    kernel = functools.partial(bias_kernel, total_tiles)
    return call(kernel, "mask_bias", (tile_lists, live_counts[:, None]), [VMEM] * 2, shape)


def attend_block(first, q_ref, kt_ref, v_ref, bias_ref, out_ref, scores, probs):
    for pair in range(WINDOW // 2):
        low = max(0, 2 * pair - LIST + 1)
        high = min(BLOCK - 1, 2 * pair + 1)
        at = first + 2 * pair
        keys = jnp.concatenate([kt_ref[at], kt_ref[at + 1]], axis=1)
        part = jnp.dot(
            q_ref[low * TILE : (high + 1) * TILE, :], keys, preferred_element_type=jnp.float32
        )
        for half in range(2):
            for tile in range(low, high + 1):
                offset = 2 * pair + half - tile
                if 0 <= offset < LIST:
                    bias = bias_ref[at + half, pl.ds(first + tile, 1), :]
                    scores[tile, :, rows_of(offset)] = part[rows_of(tile - low), rows_of(half)] + bias
    for tile in range(BLOCK):
        highest = scores[tile, :, rows_of(0)]
        for offset in range(1, LIST):
            highest = jnp.maximum(highest, scores[tile, :, rows_of(offset)])
        highest = jnp.broadcast_to(jnp.max(highest, axis=1, keepdims=True), (TILE, TILE))
        total = jnp.zeros((TILE, TILE), jnp.float32)
        for offset in range(LIST):
            weights = jnp.exp2((scores[tile, :, rows_of(offset)] - highest) * EXPONENT_SCALE)
            total += weights
            probs[tile, :, rows_of(offset)] = weights.astype(jnp.bfloat16)
        values = v_ref[pl.ds(first + tile, LIST)].reshape(LIST * TILE, HDIM)
        mixed = jnp.dot(probs[tile], values, preferred_element_type=jnp.float32)
        out_ref[rows_of(tile), :] = (mixed / jnp.sum(total, axis=1, keepdims=True)).astype(jnp.bfloat16)


def block_scratch():
    shape = (BLOCK, TILE, LIST * TILE)
    return [pltpu.VMEM(shape, jnp.float32), pltpu.VMEM(shape, jnp.bfloat16)]


def cost(tile_pairs):
    pairs = tile_pairs * TILE * TILE
    return pl.CostEstimate(flops=4 * pairs * HDIM, bytes_accessed=pairs, transcendentals=pairs)


def halo(array, dim, unit):
    ctx = lax.axis_size("ctx")
    count = array.shape[dim]
    tail = lax.slice_in_dim(array, count - EDGE * unit, count, axis=dim)
    head = lax.slice_in_dim(array, 0, (EDGE - 1) * unit, axis=dim)
    low = lax.ppermute(tail, "ctx", [(i, i + 1) for i in range(ctx - 1)])
    high = lax.ppermute(head, "ctx", [(i + 1, i) for i in range(ctx - 1)])
    return low, high


def pack_kernel(heads, q_ref, k_ref, v_ref, q_out, k_out, v_out):
    for source, target in ((k_ref, k_out), (v_ref, v_out), (q_ref, q_out)):
        for head in range(heads):
            target[head] = source[:, head * HDIM : (head + 1) * HDIM]


def unpack_kernel(heads, parts_ref, out_ref):
    for head in range(heads):
        out_ref[:, head * HDIM : (head + 1) * HDIM] = parts_ref[head]


def attend_range_kernel(q_ref, k_low, k_own, k_high, v_low, v_own, v_high, bias_ref, out_ref, kt, v, *scratch):
    at = 0
    for k_part, v_part in ((k_low, v_low), (k_own, v_own), (k_high, v_high)):
        for tile in range(k_part.shape[0] // TILE):
            kt[at] = k_part[rows_of(tile), :].T
            v[at] = v_part[rows_of(tile), :]
            at += 1

    @pl.loop(0, q_ref.shape[0] // (BLOCK * TILE))
    def _(block):
        place = pl.ds(pl.multiple_of(block * BLOCK * TILE, TILE), BLOCK * TILE)
        attend_block(block * BLOCK, q_ref.at[place, :], kt, v, bias_ref, out_ref.at[place, :], *scratch)


def to_heads(array):
    heads, rows, _ = array.shape
    return lax.all_to_all(array, "head", split_axis=0, concat_axis=0, tiled=True).reshape(heads * rows, HDIM)


def whole_range(queries, keys, values, bias):
    rows, columns = queries.shape
    heads = columns // HDIM
    parts = (heads, rows, HDIM)
    q_parts, k_parts, v_parts = call(
        functools.partial(pack_kernel, heads), "pack", (queries, keys, values), [VMEM] * 3, [parts] * 3
    )
    k_own, v_own = to_heads(k_parts), to_heads(v_parts)
    (k_low, k_high), (v_low, v_high) = halo(k_own, 0, TILE), halo(v_own, 0, TILE)
    local_q = to_heads(q_parts)
    padded = heads * rows // TILE + LIST - 1
    head_out = call(
        attend_range_kernel,
        "attend_range",
        (local_q, k_low, k_own, k_high, v_low, v_own, v_high, bias),
        [VMEM] * 8,
        (heads * rows, HDIM),
        [pltpu.VMEM((padded, TILE, HDIM), jnp.bfloat16)] * 2 + block_scratch(),
        24,
    )
    back = lax.all_to_all(head_out.reshape(parts), "head", split_axis=0, concat_axis=0, tiled=True)
    return call(functools.partial(unpack_kernel, heads), "unpack", (back,), [VMEM], (rows, columns))


def load_kv_kernel(pair, k_ref, v_ref, *refs):
    out_ref = refs[-1]
    columns = column_of(lax.axis_index("head") ^ pair)
    for tile in range(BLOCK):
        out_ref[0, tile] = k_ref[rows_of(tile), columns].T
        out_ref[1, tile] = v_ref[rows_of(tile), columns]


def load_q_kernel(pair, q_ref, *refs):
    refs[-1][...] = q_ref[:, column_of(lax.axis_index("head") ^ pair)]


def gather_kernel(*refs):
    *parts, own_ref, odd_ref, even_ref = refs
    me = lax.axis_index("head")
    for pair, part in enumerate(parts):
        own_ref[:, pl.ds((me ^ pair) * BLOCK, BLOCK)] = part[...]
    last = own_ref.shape[1] - EDGE
    odd = lax.rem(lax.axis_index("ctx"), 2)
    odd_ref[...] = own_ref[:, pl.ds(odd * last, EDGE)]
    even_ref[...] = own_ref[:, pl.ds((1 - odd) * last, EDGE)]


def join_kernel(own_ref, first_ref, second_ref, out_ref):
    odd = lax.rem(lax.axis_index("ctx"), 2)
    tiles = own_ref.shape[1]
    out_ref[:, EDGE : EDGE + tiles] = own_ref[...]

    def around(low_ref, high_ref):
        out_ref[:, :EDGE] = low_ref[...]
        out_ref[:, EDGE + tiles :] = high_ref[:, : EDGE - 1]

    @pl.when(odd == 1)
    def _():
        around(second_ref, first_ref)

    @pl.when(odd == 0)
    def _():
        around(first_ref, second_ref)


def pass_kernel(array_ref, *refs):
    refs[-1][...] = array_ref[...]


def attend_chunk_kernel(pair, q_ref, kv_ref, bias_ref, *refs):
    out_ref, *scratch = refs[-3:]
    first = (lax.axis_index("head") ^ pair) * BLOCK
    attend_block(first, q_ref, kv_ref.at[0], kv_ref.at[1], bias_ref, out_ref, *scratch)


def spread_kernel(*refs):
    *parts, out_ref = refs
    me = lax.axis_index("head")
    for pair, part in enumerate(parts):
        out_ref[:, column_of(me ^ pair)] = part[...]


def in_pairs(queries, keys, values, bias):
    heads, ctx = lax.axis_size("head"), lax.axis_size("ctx")
    chunk, tiles = (queries.shape[0], HDIM), heads * BLOCK
    order = range(heads - 1, 0, -1)

    def exchange(array, pair):
        return lax.ppermute(array, "head", [(i, i ^ pair) for i in range(heads)])

    def exchange_ctx(array, first):
        lower = range(first, ctx - 1, 2)
        return lax.ppermute(array, "ctx", [(i, i + 1) for i in lower] + [(i + 1, i) for i in lower])

    kv_parts, q_parts = [None] * heads, [None] * heads
    after = ()
    for pair in [*order, 0]:
        operands = (keys, values, *after)
        part = call(
            functools.partial(load_kv_kernel, pair), "load_kv", operands, [VMEM] * len(operands), (2, BLOCK, TILE, HDIM)
        )
        after = (part,)
        kv_parts[pair] = exchange(part, pair) if pair else part
    for pair in [*order, 0]:
        operands = (queries, kv_parts[pair]) if pair else (queries,)
        part = call(functools.partial(load_q_kernel, pair), "load_q", operands, [VMEM] * len(operands), chunk)
        q_parts[pair] = exchange(part, pair) if pair else part
    edge = (2, EDGE, TILE, HDIM)
    own, odd_edge, even_edge = call(
        gather_kernel, "gather", kv_parts, [VMEM] * heads, [(2, tiles, TILE, HDIM), edge, edge]
    )
    first, second = exchange_ctx(odd_edge, 1), exchange_ctx(even_edge, 0)
    padded = call(
        join_kernel, "join", (own, first, second), [VMEM] * 3, (2, tiles + LIST - 1, TILE, HDIM)
    )
    outs = [None] * heads
    after = ()
    for pair in [*order, 0]:
        operands = (q_parts[pair], padded, bias, *after)
        outs[pair] = call(
            functools.partial(attend_chunk_kernel, pair),
            "attend_chunk",
            operands,
            [VMEM] * len(operands),
            chunk,
            block_scratch(),
            16,
            cost(BLOCK * LIST // 2 if pair else 1),
        )
        after = (outs[pair],)
        if pair:
            outs[pair] = exchange(outs[pair], pair)
    after = ()
    for pair in order:
        operands = (outs[pair], *after)
        outs[pair] = call(
            pass_kernel, "landed", operands, [VMEM] * len(operands), chunk, cost=cost(BLOCK * LIST // 2)
        )
        after = (outs[pair],)
    return call(spread_kernel, "spread", outs, [VMEM] * heads, queries.shape)


def on_device(queries, keys, values, tile_lists, live_counts):
    ctx, heads = lax.axis_size("ctx"), lax.axis_size("head")
    bias = mask_bias(tile_lists, live_counts, tile_lists.shape[0] * ctx)
    in_chunks = queries.shape[0] == BLOCK * TILE and heads * BLOCK >= EDGE
    form = in_pairs if in_chunks and heads in (4, 8) and ctx % 2 == 0 else whole_range
    return form(queries, keys, values, bias)


def solution(mesh):
    return jax.shard_map(
        on_device,
        mesh=mesh,
        in_specs=(
            P(("groups", "ctx", "head"), None),
            P(("groups", "ctx", "head"), None),
            P(("groups", "ctx", "head"), None),
            P(("groups", "ctx"), None),
            P(("groups", "ctx")),
        ),
        out_specs=P(("groups", "ctx", "head"), None),
        check_vma=False,
    )
```

```python
import functools
import math

import jax
import jax.numpy as jnp
from jax import lax
from jax.experimental import pallas as pl
from jax.experimental.pallas import tpu as pltpu
from jax.sharding import PartitionSpec as P

HDIM = 128
TILE = 128
EDGE = 8
LIST = 16
BLOCK = 3
WINDOW = BLOCK + LIST - 1
HIDDEN = -1e30
EXPONENT_SCALE = HDIM ** (-0.5) * math.log2(math.e)
SMEM = pl.BlockSpec(memory_space=pltpu.SMEM)
VMEM = pl.BlockSpec(memory_space=pltpu.VMEM)


def call(kernel, name, operands, in_specs, shapes, scratch=(), limit=8, cost=None):
    out_shape = jax.tree.map(
        lambda shape: shape if hasattr(shape, "dtype") else jax.ShapeDtypeStruct(shape, jnp.bfloat16),
        shapes,
        is_leaf=lambda node: isinstance(node, tuple) or hasattr(node, "dtype"),
    )
    return pl.pallas_call(
        kernel,
        out_shape=out_shape,
        in_specs=in_specs,
        out_specs=jax.tree.map(lambda _: VMEM, out_shape),
        scratch_shapes=scratch,
        compiler_params=pltpu.CompilerParams(vmem_limit_bytes=limit << 20),
        cost_estimate=cost,
        name=name,
    )(*operands)


def column_of(head):
    return pl.ds(pl.multiple_of(head * HDIM, HDIM), HDIM)


def rows_of(tile):
    return slice(tile * TILE, (tile + 1) * TILE)


def bias_kernel(total_tiles, lists_ref, counts_ref, bias_ref):
    tiles, entries = lists_ref.shape
    lists = lists_ref[...]
    entry = lax.broadcasted_iota(jnp.int32, lists.shape, 1)
    row = lax.broadcasted_iota(jnp.int32, lists.shape, 0)
    live = (entry < counts_ref[...]) & (lists >= 0) & (lists < total_tiles)
    places = jnp.where(live, lists - lists[:, :1] + row + EDGE, -1)
    listed = [jnp.broadcast_to(places[:, at : at + 1], (tiles, TILE)) for at in range(entries)]
    for place in range(bias_ref.shape[0]):
        visible = listed[0] == place
        for at in range(1, entries):
            visible |= listed[at] == place
        bias_ref[place] = jnp.where(visible, 0.0, HIDDEN)


def mask_bias(tile_lists, live_counts, total_tiles):
    tiles = tile_lists.shape[0]
    shape = jax.ShapeDtypeStruct((tiles + LIST - 1, tiles, TILE), jnp.float32)
    kernel = functools.partial(bias_kernel, total_tiles)
    return call(kernel, "mask_bias", (tile_lists, live_counts[:, None]), [VMEM] * 2, shape)


def attend_block(first, q_ref, kt_ref, v_ref, bias_ref, out_ref, scores, probs):
    for pair in range(WINDOW // 2):
        low = max(0, 2 * pair - LIST + 1)
        high = min(BLOCK - 1, 2 * pair + 1)
        at = first + 2 * pair
        keys = jnp.concatenate([kt_ref[at], kt_ref[at + 1]], axis=1)
        part = jnp.dot(
            q_ref[low * TILE : (high + 1) * TILE, :], keys, preferred_element_type=jnp.float32
        )
        for half in range(2):
            for tile in range(low, high + 1):
                offset = 2 * pair + half - tile
                if 0 <= offset < LIST:
                    bias = bias_ref[at + half, pl.ds(first + tile, 1), :]
                    scores[tile, :, rows_of(offset)] = part[rows_of(tile - low), rows_of(half)] + bias
    for tile in range(BLOCK):
        highest = scores[tile, :, rows_of(0)]
        for offset in range(1, LIST):
            highest = jnp.maximum(highest, scores[tile, :, rows_of(offset)])
        highest = jnp.broadcast_to(jnp.max(highest, axis=1, keepdims=True), (TILE, TILE))
        total = jnp.zeros((TILE, TILE), jnp.float32)
        for offset in range(LIST):
            weights = jnp.exp2((scores[tile, :, rows_of(offset)] - highest) * EXPONENT_SCALE)
            total += weights
            probs[tile, :, rows_of(offset)] = weights.astype(jnp.bfloat16)
        values = v_ref[pl.ds(first + tile, LIST)].reshape(LIST * TILE, HDIM)
        mixed = jnp.dot(probs[tile], values, preferred_element_type=jnp.float32)
        out_ref[rows_of(tile), :] = (mixed / jnp.sum(total, axis=1, keepdims=True)).astype(jnp.bfloat16)


def block_scratch():
    shape = (BLOCK, TILE, LIST * TILE)
    return [pltpu.VMEM(shape, jnp.float32), pltpu.VMEM(shape, jnp.bfloat16)]


def cost(tile_pairs):
    pairs = tile_pairs * TILE * TILE
    return pl.CostEstimate(flops=4 * pairs * HDIM, bytes_accessed=pairs, transcendentals=pairs)


def halo(array, dim, unit):
    ctx = lax.axis_size("ctx")
    count = array.shape[dim]
    tail = lax.slice_in_dim(array, count - EDGE * unit, count, axis=dim)
    head = lax.slice_in_dim(array, 0, (EDGE - 1) * unit, axis=dim)
    low = lax.ppermute(tail, "ctx", [(i, i + 1) for i in range(ctx - 1)])
    high = lax.ppermute(head, "ctx", [(i + 1, i) for i in range(ctx - 1)])
    return low, high


def pack_kernel(heads, q_ref, k_ref, v_ref, q_out, k_out, v_out):
    for source, target in ((k_ref, k_out), (v_ref, v_out), (q_ref, q_out)):
        for head in range(heads):
            target[head] = source[:, head * HDIM : (head + 1) * HDIM]


def unpack_kernel(heads, parts_ref, out_ref):
    for head in range(heads):
        out_ref[:, head * HDIM : (head + 1) * HDIM] = parts_ref[head]


def attend_range_kernel(q_ref, k_low, k_own, k_high, v_low, v_own, v_high, bias_ref, out_ref, kt, v, *scratch):
    at = 0
    for k_part, v_part in ((k_low, v_low), (k_own, v_own), (k_high, v_high)):
        for tile in range(k_part.shape[0] // TILE):
            kt[at] = k_part[rows_of(tile), :].T
            v[at] = v_part[rows_of(tile), :]
            at += 1

    @pl.loop(0, q_ref.shape[0] // (BLOCK * TILE))
    def _(block):
        place = pl.ds(pl.multiple_of(block * BLOCK * TILE, TILE), BLOCK * TILE)
        attend_block(block * BLOCK, q_ref.at[place, :], kt, v, bias_ref, out_ref.at[place, :], *scratch)


def to_heads(array):
    heads, rows, _ = array.shape
    return lax.all_to_all(array, "head", split_axis=0, concat_axis=0, tiled=True).reshape(heads * rows, HDIM)


def whole_range(queries, keys, values, bias):
    rows, columns = queries.shape
    heads = columns // HDIM
    parts = (heads, rows, HDIM)
    q_parts, k_parts, v_parts = call(
        functools.partial(pack_kernel, heads), "pack", (queries, keys, values), [VMEM] * 3, [parts] * 3
    )
    k_own, v_own = to_heads(k_parts), to_heads(v_parts)
    (k_low, k_high), (v_low, v_high) = halo(k_own, 0, TILE), halo(v_own, 0, TILE)
    local_q = to_heads(q_parts)
    padded = heads * rows // TILE + LIST - 1
    head_out = call(
        attend_range_kernel,
        "attend_range",
        (local_q, k_low, k_own, k_high, v_low, v_own, v_high, bias),
        [VMEM] * 8,
        (heads * rows, HDIM),
        [pltpu.VMEM((padded, TILE, HDIM), jnp.bfloat16)] * 2 + block_scratch(),
        24,
    )
    back = lax.all_to_all(head_out.reshape(parts), "head", split_axis=0, concat_axis=0, tiled=True)
    return call(functools.partial(unpack_kernel, heads), "unpack", (back,), [VMEM], (rows, columns))


def load_tiles_kernel(pair, turn, array_ref, *refs):
    columns = column_of(lax.axis_index("head") ^ pair)
    for tile in range(BLOCK):
        part = array_ref[rows_of(tile), columns]
        refs[-1][tile] = part.T if turn else part


def load_q_kernel(pair, q_ref, *refs):
    refs[-1][...] = q_ref[:, column_of(lax.axis_index("head") ^ pair)]


def gather_kernel(*refs):
    *parts, own_ref = refs
    me = lax.axis_index("head")
    for pair, part in enumerate(parts):
        own_ref[pl.ds((me ^ pair) * BLOCK, BLOCK)] = part[...]


def edges_kernel(own_ref, odd_ref, even_ref):
    last = own_ref.shape[0] - EDGE
    odd = lax.rem(lax.axis_index("ctx"), 2)
    odd_ref[...] = own_ref[pl.ds(odd * last, EDGE)]
    even_ref[...] = own_ref[pl.ds((1 - odd) * last, EDGE)]


def join_kernel(own_ref, first_ref, second_ref, out_ref):
    odd = lax.rem(lax.axis_index("ctx"), 2)
    tiles = own_ref.shape[0]
    out_ref[EDGE : EDGE + tiles] = own_ref[...]

    def around(low_ref, high_ref):
        out_ref[:EDGE] = low_ref[...]
        out_ref[EDGE + tiles :] = high_ref[: EDGE - 1]

    @pl.when(odd == 1)
    def _():
        around(second_ref, first_ref)

    @pl.when(odd == 0)
    def _():
        around(first_ref, second_ref)


def with_halo(parts):
    heads, ctx = len(parts), lax.axis_size("ctx")
    tiles, edge = heads * BLOCK, (EDGE, TILE, HDIM)
    own = call(gather_kernel, "gather", parts, [VMEM] * heads, (tiles, TILE, HDIM))
    odd_edge, even_edge = call(edges_kernel, "edges", (own,), [VMEM], [edge, edge])

    def exchange(array, first):
        lower = range(first, ctx - 1, 2)
        return lax.ppermute(array, "ctx", [(i, i + 1) for i in lower] + [(i + 1, i) for i in lower])

    operands = (own, exchange(odd_edge, 1), exchange(even_edge, 0))
    return call(join_kernel, "join", operands, [VMEM] * 3, (tiles + LIST - 1, TILE, HDIM))


def pass_kernel(array_ref, *refs):
    refs[-1][...] = array_ref[...]


def attend_chunk_kernel(pair, q_ref, kt_ref, v_ref, bias_ref, *refs):
    out_ref, *scratch = refs[-3:]
    first = (lax.axis_index("head") ^ pair) * BLOCK
    attend_block(first, q_ref, kt_ref, v_ref, bias_ref, out_ref, *scratch)


def spread_kernel(*refs):
    *parts, out_ref = refs
    me = lax.axis_index("head")
    for pair, part in enumerate(parts):
        out_ref[:, column_of(me ^ pair)] = part[...]


def in_pairs(queries, keys, values, bias):
    heads = lax.axis_size("head")
    chunk, tiles = (queries.shape[0], HDIM), (BLOCK, TILE, HDIM)
    order = range(heads - 1, 0, -1)

    def exchange(array, pair):
        return lax.ppermute(array, "head", [(i, i ^ pair) for i in range(heads)])

    def call_on(kernel, name, operands, shape):
        return call(kernel, name, operands, [VMEM] * len(operands), shape)

    v_parts, k_parts, q_parts = [None] * heads, [None] * heads, [None] * heads
    for pair in [*order, 0]:
        part = call_on(functools.partial(load_tiles_kernel, pair, False), "load_v", (values,), tiles)
        v_parts[pair] = exchange(part, pair) if pair else part
    for pair in [*order, 0]:
        operands = (keys, v_parts[pair]) if pair else (keys,)
        part = call_on(functools.partial(load_tiles_kernel, pair, True), "load_k", operands, tiles)
        k_parts[pair] = exchange(part, pair) if pair else part
    for pair in [*order, 0]:
        operands = (queries, k_parts[pair]) if pair else (queries,)
        part = call_on(functools.partial(load_q_kernel, pair), "load_q", operands, chunk)
        q_parts[pair] = exchange(part, pair) if pair else part
    all_values, all_keys = with_halo(v_parts), with_halo(k_parts)
    outs = [None] * heads
    after = ()
    for pair in [*order, 0]:
        operands = (q_parts[pair], all_keys, all_values, bias, *after)
        outs[pair] = call(
            functools.partial(attend_chunk_kernel, pair),
            "attend_chunk",
            operands,
            [VMEM] * len(operands),
            chunk,
            block_scratch(),
            16,
            cost(BLOCK * LIST // 2 if pair else 1),
        )
        after = (outs[pair],)
        if pair:
            outs[pair] = exchange(outs[pair], pair)
    after = ()
    for pair in order:
        operands = (outs[pair], *after)
        outs[pair] = call(
            pass_kernel, "landed", operands, [VMEM] * len(operands), chunk, cost=cost(BLOCK * LIST // 2)
        )
        after = (outs[pair],)
    return call(spread_kernel, "spread", outs, [VMEM] * heads, queries.shape)


def on_device(queries, keys, values, tile_lists, live_counts):
    ctx, heads = lax.axis_size("ctx"), lax.axis_size("head")
    bias = mask_bias(tile_lists, live_counts, tile_lists.shape[0] * ctx)
    in_chunks = queries.shape[0] == BLOCK * TILE and heads * BLOCK >= EDGE
    form = in_pairs if in_chunks and heads in (4, 8) and ctx % 2 == 0 else whole_range
    return form(queries, keys, values, bias)


def solution(mesh):
    return jax.shard_map(
        on_device,
        mesh=mesh,
        in_specs=(
            P(("groups", "ctx", "head"), None),
            P(("groups", "ctx", "head"), None),
            P(("groups", "ctx", "head"), None),
            P(("groups", "ctx"), None),
            P(("groups", "ctx")),
        ),
        out_specs=P(("groups", "ctx", "head"), None),
        check_vma=False,
    )
```

```python
import functools
import math

import jax
import jax.numpy as jnp
from jax import lax
from jax.experimental import pallas as pl
from jax.experimental.pallas import tpu as pltpu
from jax.sharding import PartitionSpec as P

HDIM = 128
TILE = 128
EDGE = 8
LIST = 16
BLOCK = 3
WINDOW = BLOCK + LIST - 1
HIDDEN = -1e30
EXPONENT_SCALE = HDIM ** (-0.5) * math.log2(math.e)
SMEM = pl.BlockSpec(memory_space=pltpu.SMEM)
VMEM = pl.BlockSpec(memory_space=pltpu.VMEM)


def call(kernel, name, operands, in_specs, shapes, scratch=(), limit=8, cost=None):
    out_shape = jax.tree.map(
        lambda shape: shape if hasattr(shape, "dtype") else jax.ShapeDtypeStruct(shape, jnp.bfloat16),
        shapes,
        is_leaf=lambda node: isinstance(node, tuple) or hasattr(node, "dtype"),
    )
    return pl.pallas_call(
        kernel,
        out_shape=out_shape,
        in_specs=in_specs,
        out_specs=jax.tree.map(lambda _: VMEM, out_shape),
        scratch_shapes=scratch,
        compiler_params=pltpu.CompilerParams(vmem_limit_bytes=limit << 20),
        cost_estimate=cost,
        name=name,
    )(*operands)


def column_of(head):
    return pl.ds(pl.multiple_of(head * HDIM, HDIM), HDIM)


def rows_of(tile):
    return slice(tile * TILE, (tile + 1) * TILE)


def bias_kernel(total_tiles, lists_ref, counts_ref, bias_ref):
    tiles, entries = lists_ref.shape
    lists = lists_ref[...]
    entry = lax.broadcasted_iota(jnp.int32, lists.shape, 1)
    row = lax.broadcasted_iota(jnp.int32, lists.shape, 0)
    live = (entry < counts_ref[...]) & (lists >= 0) & (lists < total_tiles)
    places = jnp.where(live, lists - lists[:, :1] + row + EDGE, -1)
    listed = [jnp.broadcast_to(places[:, at : at + 1], (tiles, TILE)) for at in range(entries)]
    for place in range(bias_ref.shape[0]):
        visible = listed[0] == place
        for at in range(1, entries):
            visible |= listed[at] == place
        bias_ref[place] = jnp.where(visible, 0.0, HIDDEN)


def mask_bias(tile_lists, live_counts, total_tiles):
    tiles = tile_lists.shape[0]
    shape = jax.ShapeDtypeStruct((tiles + LIST - 1, tiles, TILE), jnp.float32)
    kernel = functools.partial(bias_kernel, total_tiles)
    return call(kernel, "mask_bias", (tile_lists, live_counts[:, None]), [VMEM] * 2, shape)


def attend_block(first, q_ref, kt_ref, v_ref, bias_ref, out_ref, scores, probs):
    for pair in range(WINDOW // 2):
        low = max(0, 2 * pair - LIST + 1)
        high = min(BLOCK - 1, 2 * pair + 1)
        at = first + 2 * pair
        keys = jnp.concatenate([kt_ref[at], kt_ref[at + 1]], axis=1)
        part = jnp.dot(
            q_ref[low * TILE : (high + 1) * TILE, :], keys, preferred_element_type=jnp.float32
        )
        for half in range(2):
            for tile in range(low, high + 1):
                offset = 2 * pair + half - tile
                if 0 <= offset < LIST:
                    bias = bias_ref[at + half, pl.ds(first + tile, 1), :]
                    scores[tile, :, rows_of(offset)] = part[rows_of(tile - low), rows_of(half)] + bias
    for tile in range(BLOCK):
        highest = scores[tile, :, rows_of(0)]
        for offset in range(1, LIST):
            highest = jnp.maximum(highest, scores[tile, :, rows_of(offset)])
        highest = jnp.broadcast_to(jnp.max(highest, axis=1, keepdims=True), (TILE, TILE))
        total = jnp.zeros((TILE, TILE), jnp.float32)
        for offset in range(LIST):
            weights = jnp.exp2((scores[tile, :, rows_of(offset)] - highest) * EXPONENT_SCALE)
            total += weights
            probs[tile, :, rows_of(offset)] = weights.astype(jnp.bfloat16)
        values = v_ref[pl.ds(first + tile, LIST)].reshape(LIST * TILE, HDIM)
        mixed = jnp.dot(probs[tile], values, preferred_element_type=jnp.float32)
        out_ref[rows_of(tile), :] = (mixed / jnp.sum(total, axis=1, keepdims=True)).astype(jnp.bfloat16)


def block_scratch():
    shape = (BLOCK, TILE, LIST * TILE)
    return [pltpu.VMEM(shape, jnp.float32), pltpu.VMEM(shape, jnp.bfloat16)]


def cost(tile_pairs):
    pairs = tile_pairs * TILE * TILE
    return pl.CostEstimate(flops=4 * pairs * HDIM, bytes_accessed=pairs, transcendentals=pairs)


def halo(array, dim, unit):
    ctx = lax.axis_size("ctx")
    count = array.shape[dim]
    tail = lax.slice_in_dim(array, count - EDGE * unit, count, axis=dim)
    head = lax.slice_in_dim(array, 0, (EDGE - 1) * unit, axis=dim)
    low = lax.ppermute(tail, "ctx", [(i, i + 1) for i in range(ctx - 1)])
    high = lax.ppermute(head, "ctx", [(i + 1, i) for i in range(ctx - 1)])
    return low, high


def pack_kernel(heads, q_ref, k_ref, v_ref, q_out, k_out, v_out):
    for source, target in ((k_ref, k_out), (v_ref, v_out), (q_ref, q_out)):
        for head in range(heads):
            target[head] = source[:, head * HDIM : (head + 1) * HDIM]


def unpack_kernel(heads, parts_ref, out_ref):
    for head in range(heads):
        out_ref[:, head * HDIM : (head + 1) * HDIM] = parts_ref[head]


def attend_range_kernel(q_ref, k_low, k_own, k_high, v_low, v_own, v_high, bias_ref, out_ref, kt, v, *scratch):
    at = 0
    for k_part, v_part in ((k_low, v_low), (k_own, v_own), (k_high, v_high)):
        for tile in range(k_part.shape[0] // TILE):
            kt[at] = k_part[rows_of(tile), :].T
            v[at] = v_part[rows_of(tile), :]
            at += 1

    @pl.loop(0, q_ref.shape[0] // (BLOCK * TILE))
    def _(block):
        place = pl.ds(pl.multiple_of(block * BLOCK * TILE, TILE), BLOCK * TILE)
        attend_block(block * BLOCK, q_ref.at[place, :], kt, v, bias_ref, out_ref.at[place, :], *scratch)


def to_heads(array):
    heads, rows, _ = array.shape
    return lax.all_to_all(array, "head", split_axis=0, concat_axis=0, tiled=True).reshape(heads * rows, HDIM)


def whole_range(queries, keys, values, bias):
    rows, columns = queries.shape
    heads = columns // HDIM
    parts = (heads, rows, HDIM)
    q_parts, k_parts, v_parts = call(
        functools.partial(pack_kernel, heads), "pack", (queries, keys, values), [VMEM] * 3, [parts] * 3
    )
    k_own, v_own = to_heads(k_parts), to_heads(v_parts)
    (k_low, k_high), (v_low, v_high) = halo(k_own, 0, TILE), halo(v_own, 0, TILE)
    local_q = to_heads(q_parts)
    padded = heads * rows // TILE + LIST - 1
    head_out = call(
        attend_range_kernel,
        "attend_range",
        (local_q, k_low, k_own, k_high, v_low, v_own, v_high, bias),
        [VMEM] * 8,
        (heads * rows, HDIM),
        [pltpu.VMEM((padded, TILE, HDIM), jnp.bfloat16)] * 2 + block_scratch(),
        24,
    )
    back = lax.all_to_all(head_out.reshape(parts), "head", split_axis=0, concat_axis=0, tiled=True)
    return call(functools.partial(unpack_kernel, heads), "unpack", (back,), [VMEM], (rows, columns))


def load_kv_kernel(pair, k_ref, v_ref, *refs):
    out_ref = refs[-1]
    columns = column_of(lax.axis_index("head") ^ pair)
    for tile in range(BLOCK):
        out_ref[0, tile] = k_ref[rows_of(tile), columns].T
        out_ref[1, tile] = v_ref[rows_of(tile), columns]


def load_q_kernel(pair, q_ref, *refs):
    refs[-1][...] = q_ref[:, column_of(lax.axis_index("head") ^ pair)]


def gather_kernel(*refs):
    *parts, own_ref = refs
    me = lax.axis_index("head")
    for pair, part in enumerate(parts):
        own_ref[:, pl.ds((me ^ pair) * BLOCK, BLOCK)] = part[...]


def edges_kernel(own_ref, odd_ref, even_ref):
    last = own_ref.shape[1] - EDGE
    odd = lax.rem(lax.axis_index("ctx"), 2)
    odd_ref[...] = own_ref[:, pl.ds(odd * last, EDGE)]
    even_ref[...] = own_ref[:, pl.ds((1 - odd) * last, EDGE)]


def join_kernel(own_ref, first_ref, second_ref, out_ref):
    odd = lax.rem(lax.axis_index("ctx"), 2)
    tiles = own_ref.shape[1]
    out_ref[:, EDGE : EDGE + tiles] = own_ref[...]

    def around(low_ref, high_ref):
        out_ref[:, :EDGE] = low_ref[...]
        out_ref[:, EDGE + tiles :] = high_ref[:, : EDGE - 1]

    @pl.when(odd == 1)
    def _():
        around(second_ref, first_ref)

    @pl.when(odd == 0)
    def _():
        around(first_ref, second_ref)


def stack_kernel(*refs):
    for at, ref in enumerate(refs[:-1]):
        refs[-1][at] = ref[...]


def pass_kernel(array_ref, *refs):
    refs[-1][...] = array_ref[...]


def attend_chunk_kernel(pair, q_ref, kv_ref, bias_ref, *refs):
    out_ref, *scratch = refs[-3:]
    first = (lax.axis_index("head") ^ pair) * BLOCK
    attend_block(first, q_ref.at[pair], kv_ref.at[0], kv_ref.at[1], bias_ref, out_ref, *scratch)


def spread_kernel(*refs):
    *parts, out_ref = refs
    me = lax.axis_index("head")
    for pair, part in enumerate(parts):
        out_ref[:, column_of(me ^ pair)] = part[...]


def in_pairs(queries, keys, values, bias):
    heads, ctx = lax.axis_size("head"), lax.axis_size("ctx")
    chunk, tiles = (queries.shape[0], HDIM), heads * BLOCK
    order = range(heads - 1, 0, -1)

    def exchange(array, pair):
        return lax.ppermute(array, "head", [(i, i ^ pair) for i in range(heads)])

    def exchange_ctx(array, first):
        lower = range(first, ctx - 1, 2)
        return lax.ppermute(array, "ctx", [(i, i + 1) for i in lower] + [(i + 1, i) for i in lower])

    kv_parts, q_parts = [None] * heads, [None] * heads
    after = ()
    for pair in [*order, 0]:
        operands = (keys, values, *after)
        part = call(
            functools.partial(load_kv_kernel, pair), "load_kv", operands, [VMEM] * len(operands), (2, BLOCK, TILE, HDIM)
        )
        after = (part,)
        kv_parts[pair] = exchange(part, pair) if pair else part
    for pair in [*order, 0]:
        operands = (queries, kv_parts[pair]) if pair else (queries,)
        part = call(functools.partial(load_q_kernel, pair), "load_q", operands, [VMEM] * len(operands), chunk)
        q_parts[pair] = exchange(part, pair) if pair else part
    edge = (2, EDGE, TILE, HDIM)
    own = call(gather_kernel, "gather", kv_parts, [VMEM] * heads, (2, tiles, TILE, HDIM))
    odd_edge, even_edge = call(edges_kernel, "edges", (own,), [VMEM], [edge, edge])
    local_q = call(stack_kernel, "stack", q_parts, [VMEM] * heads, (heads, *chunk), cost=cost(1 << 14))
    first, second = exchange_ctx(odd_edge, 1), exchange_ctx(even_edge, 0)
    padded = call(
        join_kernel, "join", (own, first, second), [VMEM] * 3, (2, tiles + LIST - 1, TILE, HDIM)
    )
    outs = [None] * heads
    after = ()
    for pair in [*order, 0]:
        operands = (local_q, padded, bias, *after)
        outs[pair] = call(
            functools.partial(attend_chunk_kernel, pair),
            "attend_chunk",
            operands,
            [VMEM] * len(operands),
            chunk,
            block_scratch(),
            16,
            cost(BLOCK * LIST // 2 if pair else 1),
        )
        after = (outs[pair],)
        if pair:
            outs[pair] = exchange(outs[pair], pair)
    after = ()
    for pair in order:
        operands = (outs[pair], *after)
        outs[pair] = call(
            pass_kernel, "landed", operands, [VMEM] * len(operands), chunk, cost=cost(BLOCK * LIST // 2)
        )
        after = (outs[pair],)
    return call(spread_kernel, "spread", outs, [VMEM] * heads, queries.shape)


def on_device(queries, keys, values, tile_lists, live_counts):
    ctx, heads = lax.axis_size("ctx"), lax.axis_size("head")
    bias = mask_bias(tile_lists, live_counts, tile_lists.shape[0] * ctx)
    in_chunks = queries.shape[0] == BLOCK * TILE and heads * BLOCK >= EDGE
    form = in_pairs if in_chunks and heads in (4, 8) and ctx % 2 == 0 else whole_range
    return form(queries, keys, values, bias)


def solution(mesh):
    return jax.shard_map(
        on_device,
        mesh=mesh,
        in_specs=(
            P(("groups", "ctx", "head"), None),
            P(("groups", "ctx", "head"), None),
            P(("groups", "ctx", "head"), None),
            P(("groups", "ctx"), None),
            P(("groups", "ctx")),
        ),
        out_specs=P(("groups", "ctx", "head"), None),
        check_vma=False,
    )
```

```python
import functools
import math

import jax
import jax.numpy as jnp
from jax import lax
from jax.experimental import pallas as pl
from jax.experimental.pallas import tpu as pltpu
from jax.sharding import PartitionSpec as P

HDIM = 128
TILE = 128
EDGE = 8
LIST = 16
BLOCK = 3
WINDOW = BLOCK + LIST - 1
HIDDEN = -1e30
EXPONENT_SCALE = HDIM ** (-0.5) * math.log2(math.e)
SMEM = pl.BlockSpec(memory_space=pltpu.SMEM)
VMEM = pl.BlockSpec(memory_space=pltpu.VMEM)


def call(kernel, name, operands, in_specs, shapes, scratch=(), limit=8, cost=None):
    out_shape = jax.tree.map(
        lambda shape: shape if hasattr(shape, "dtype") else jax.ShapeDtypeStruct(shape, jnp.bfloat16),
        shapes,
        is_leaf=lambda node: isinstance(node, tuple) or hasattr(node, "dtype"),
    )
    return pl.pallas_call(
        kernel,
        out_shape=out_shape,
        in_specs=in_specs,
        out_specs=jax.tree.map(lambda _: VMEM, out_shape),
        scratch_shapes=scratch,
        compiler_params=pltpu.CompilerParams(vmem_limit_bytes=limit << 20),
        cost_estimate=cost,
        name=name,
    )(*operands)


def column_of(head):
    return pl.ds(pl.multiple_of(head * HDIM, HDIM), HDIM)


def rows_of(tile):
    return slice(tile * TILE, (tile + 1) * TILE)


def bias_kernel(total_tiles, lists_ref, counts_ref, bias_ref):
    tiles, entries = lists_ref.shape
    lists = lists_ref[...]
    entry = lax.broadcasted_iota(jnp.int32, lists.shape, 1)
    row = lax.broadcasted_iota(jnp.int32, lists.shape, 0)
    live = (entry < counts_ref[...]) & (lists >= 0) & (lists < total_tiles)
    places = jnp.where(live, lists - lists[:, :1] + row + EDGE, -1)
    listed = [jnp.broadcast_to(places[:, at : at + 1], (tiles, TILE)) for at in range(entries)]
    for place in range(bias_ref.shape[0]):
        visible = listed[0] == place
        for at in range(1, entries):
            visible |= listed[at] == place
        bias_ref[place] = jnp.where(visible, 0.0, HIDDEN)


def mask_bias(tile_lists, live_counts, total_tiles):
    tiles = tile_lists.shape[0]
    shape = jax.ShapeDtypeStruct((tiles + LIST - 1, tiles, TILE), jnp.float32)
    kernel = functools.partial(bias_kernel, total_tiles)
    return call(kernel, "mask_bias", (tile_lists, live_counts[:, None]), [VMEM] * 2, shape)


def attend_block(first, q_ref, kt_ref, v_ref, bias_ref, out_ref, scores, probs):
    for pair in range(WINDOW // 2):
        low = max(0, 2 * pair - LIST + 1)
        high = min(BLOCK - 1, 2 * pair + 1)
        at = first + 2 * pair
        keys = jnp.concatenate([kt_ref[at], kt_ref[at + 1]], axis=1)
        part = jnp.dot(
            q_ref[low * TILE : (high + 1) * TILE, :], keys, preferred_element_type=jnp.float32
        )
        for half in range(2):
            for tile in range(low, high + 1):
                offset = 2 * pair + half - tile
                if 0 <= offset < LIST:
                    bias = bias_ref[at + half, pl.ds(first + tile, 1), :]
                    scores[tile, :, rows_of(offset)] = part[rows_of(tile - low), rows_of(half)] + bias
    for tile in range(BLOCK):
        highest = scores[tile, :, rows_of(0)]
        for offset in range(1, LIST):
            highest = jnp.maximum(highest, scores[tile, :, rows_of(offset)])
        highest = jnp.broadcast_to(jnp.max(highest, axis=1, keepdims=True), (TILE, TILE))
        total = jnp.zeros((TILE, TILE), jnp.float32)
        for offset in range(LIST):
            weights = jnp.exp2((scores[tile, :, rows_of(offset)] - highest) * EXPONENT_SCALE)
            total += weights
            probs[tile, :, rows_of(offset)] = weights.astype(jnp.bfloat16)
        values = v_ref[pl.ds(first + tile, LIST)].reshape(LIST * TILE, HDIM)
        mixed = jnp.dot(probs[tile], values, preferred_element_type=jnp.float32)
        out_ref[rows_of(tile), :] = (mixed / jnp.sum(total, axis=1, keepdims=True)).astype(jnp.bfloat16)


def block_scratch():
    shape = (BLOCK, TILE, LIST * TILE)
    return [pltpu.VMEM(shape, jnp.float32), pltpu.VMEM(shape, jnp.bfloat16)]


def cost(tile_pairs):
    pairs = tile_pairs * TILE * TILE
    return pl.CostEstimate(flops=4 * pairs * HDIM, bytes_accessed=pairs, transcendentals=pairs)


def halo(array, dim, unit):
    ctx = lax.axis_size("ctx")
    count = array.shape[dim]
    tail = lax.slice_in_dim(array, count - EDGE * unit, count, axis=dim)
    head = lax.slice_in_dim(array, 0, (EDGE - 1) * unit, axis=dim)
    low = lax.ppermute(tail, "ctx", [(i, i + 1) for i in range(ctx - 1)])
    high = lax.ppermute(head, "ctx", [(i + 1, i) for i in range(ctx - 1)])
    return low, high


def pack_kernel(heads, q_ref, k_ref, v_ref, q_out, k_out, v_out):
    for source, target in ((k_ref, k_out), (v_ref, v_out), (q_ref, q_out)):
        for head in range(heads):
            target[head] = source[:, head * HDIM : (head + 1) * HDIM]


def unpack_kernel(heads, parts_ref, out_ref):
    for head in range(heads):
        out_ref[:, head * HDIM : (head + 1) * HDIM] = parts_ref[head]


def attend_range_kernel(q_ref, k_low, k_own, k_high, v_low, v_own, v_high, bias_ref, out_ref, kt, v, *scratch):
    at = 0
    for k_part, v_part in ((k_low, v_low), (k_own, v_own), (k_high, v_high)):
        for tile in range(k_part.shape[0] // TILE):
            kt[at] = k_part[rows_of(tile), :].T
            v[at] = v_part[rows_of(tile), :]
            at += 1

    @pl.loop(0, q_ref.shape[0] // (BLOCK * TILE))
    def _(block):
        place = pl.ds(pl.multiple_of(block * BLOCK * TILE, TILE), BLOCK * TILE)
        attend_block(block * BLOCK, q_ref.at[place, :], kt, v, bias_ref, out_ref.at[place, :], *scratch)


def to_heads(array):
    heads, rows, _ = array.shape
    return lax.all_to_all(array, "head", split_axis=0, concat_axis=0, tiled=True).reshape(heads * rows, HDIM)


def whole_range(queries, keys, values, bias):
    rows, columns = queries.shape
    heads = columns // HDIM
    parts = (heads, rows, HDIM)
    q_parts, k_parts, v_parts = call(
        functools.partial(pack_kernel, heads), "pack", (queries, keys, values), [VMEM] * 3, [parts] * 3
    )
    k_own, v_own = to_heads(k_parts), to_heads(v_parts)
    (k_low, k_high), (v_low, v_high) = halo(k_own, 0, TILE), halo(v_own, 0, TILE)
    local_q = to_heads(q_parts)
    padded = heads * rows // TILE + LIST - 1
    head_out = call(
        attend_range_kernel,
        "attend_range",
        (local_q, k_low, k_own, k_high, v_low, v_own, v_high, bias),
        [VMEM] * 8,
        (heads * rows, HDIM),
        [pltpu.VMEM((padded, TILE, HDIM), jnp.bfloat16)] * 2 + block_scratch(),
        24,
    )
    back = lax.all_to_all(head_out.reshape(parts), "head", split_axis=0, concat_axis=0, tiled=True)
    return call(functools.partial(unpack_kernel, heads), "unpack", (back,), [VMEM], (rows, columns))


def load_tiles_kernel(pair, array_ref, *refs, turn):
    columns = column_of(lax.axis_index("head") ^ pair)
    for tile in range(BLOCK):
        part = array_ref[rows_of(tile), columns]
        refs[-1][tile] = part.T if turn else part


def load_kq_kernel(pair, k_ref, q_ref, *refs):
    columns = column_of(lax.axis_index("head") ^ pair)
    for tile in range(BLOCK):
        refs[-1][tile] = k_ref[rows_of(tile), columns].T
        refs[-1][BLOCK + tile] = q_ref[rows_of(tile), columns]


def load_q_kernel(pair, q_ref, *refs):
    refs[-1][...] = q_ref[:, column_of(lax.axis_index("head") ^ pair)]


def gather_kernel(*refs):
    *parts, own_ref = refs
    me = lax.axis_index("head")
    for pair, part in enumerate(parts):
        own_ref[pl.ds((me ^ pair) * BLOCK, BLOCK)] = part[:BLOCK]


def edges_kernel(own_ref, odd_ref, even_ref):
    last = own_ref.shape[0] - EDGE
    odd = lax.rem(lax.axis_index("ctx"), 2)
    odd_ref[...] = own_ref[pl.ds(odd * last, EDGE)]
    even_ref[...] = own_ref[pl.ds((1 - odd) * last, EDGE)]


def join_kernel(own_ref, first_ref, second_ref, out_ref):
    odd = lax.rem(lax.axis_index("ctx"), 2)
    tiles = own_ref.shape[0]
    out_ref[EDGE : EDGE + tiles] = own_ref[...]

    def around(low_ref, high_ref):
        out_ref[:EDGE] = low_ref[...]
        out_ref[EDGE + tiles :] = high_ref[: EDGE - 1]

    @pl.when(odd == 1)
    def _():
        around(second_ref, first_ref)

    @pl.when(odd == 0)
    def _():
        around(first_ref, second_ref)


def with_halo(parts):
    heads, ctx = len(parts), lax.axis_size("ctx")
    tiles, edge = heads * BLOCK, (EDGE, TILE, HDIM)
    own = call(gather_kernel, "gather", parts, [VMEM] * heads, (tiles, TILE, HDIM))
    odd_edge, even_edge = call(edges_kernel, "edges", (own,), [VMEM], [edge, edge])

    def exchange(array, first):
        lower = range(first, ctx - 1, 2)
        return lax.ppermute(array, "ctx", [(i, i + 1) for i in lower] + [(i + 1, i) for i in lower])

    operands = (own, exchange(odd_edge, 1), exchange(even_edge, 0))
    return call(join_kernel, "join", operands, [VMEM] * 3, (tiles + LIST - 1, TILE, HDIM))


def stack_kernel(*refs):
    *q_refs, out_ref = refs
    for at, ref in enumerate(q_refs):
        if len(ref.shape) == 2:
            out_ref[at] = ref[...]
        else:
            for tile in range(BLOCK):
                out_ref[at, rows_of(tile), :] = ref[BLOCK + tile]


def pass_kernel(array_ref, *refs):
    refs[-1][...] = array_ref[...]


def attend_chunk_kernel(pair, q_ref, kt_ref, v_ref, bias_ref, *refs):
    out_ref, *scratch = refs[-3:]
    first = (lax.axis_index("head") ^ pair) * BLOCK
    attend_block(first, q_ref.at[pair], kt_ref, v_ref, bias_ref, out_ref, *scratch)


def spread_kernel(*refs):
    *parts, out_ref = refs
    me = lax.axis_index("head")
    for pair, part in enumerate(parts):
        out_ref[:, column_of(me ^ pair)] = part[...]


def in_pairs(queries, keys, values, bias):
    heads = lax.axis_size("head")
    chunk, tiles = (queries.shape[0], HDIM), (BLOCK, TILE, HDIM)
    order = range(heads - 1, 0, -1)

    def exchange(array, pair):
        return lax.ppermute(array, "head", [(i, i ^ pair) for i in range(heads)])

    def call_on(kernel, name, operands, shape):
        return call(kernel, name, operands, [VMEM] * len(operands), shape)

    v_parts, k_parts, q_parts = [None] * heads, [None] * heads, [None] * heads
    for pair in [*order, 0]:
        part = call_on(functools.partial(load_tiles_kernel, pair, turn=False), "load_v", (values,), tiles)
        v_parts[pair] = exchange(part, pair) if pair else part
    for pair in [*order, 0]:
        operands = (keys, queries) if pair == 1 else (keys,)
        kernel = load_kq_kernel if pair == 1 else functools.partial(load_tiles_kernel, turn=True)
        shape = (len(operands) * BLOCK, TILE, HDIM)
        after = (v_parts[pair],) if pair else ()
        part = call_on(functools.partial(kernel, pair), "load_k", (*operands, *after), shape)
        k_parts[pair] = exchange(part, pair) if pair else part
    q_parts[1] = k_parts[1]
    for pair in [*order[:-1], 0]:
        operands = (queries, k_parts[pair]) if pair else (queries,)
        part = call_on(functools.partial(load_q_kernel, pair), "load_q", operands, chunk)
        q_parts[pair] = exchange(part, pair) if pair else part
    all_values, all_keys = with_halo(v_parts), with_halo(k_parts)
    local_q = call(stack_kernel, "stack", q_parts, [VMEM] * heads, (heads, *chunk), cost=cost(100))
    all_values = call(
        pass_kernel, "values", (all_values, local_q), [VMEM] * 2, all_values.shape, cost=cost(16384)
    )
    outs = [None] * heads
    after = ()
    for pair in [*order, 0]:
        operands = (local_q, all_keys, all_values, bias, *after)
        outs[pair] = call(
            functools.partial(attend_chunk_kernel, pair),
            "attend_chunk",
            operands,
            [VMEM] * len(operands),
            chunk,
            block_scratch(),
            16,
            cost(BLOCK * LIST // 2 if pair else 1),
        )
        after = (outs[pair],)
        if pair:
            outs[pair] = exchange(outs[pair], pair)
    after = ()
    for pair in order:
        operands = (outs[pair], *after)
        outs[pair] = call(
            pass_kernel, "landed", operands, [VMEM] * len(operands), chunk, cost=cost(BLOCK * LIST // 2)
        )
        after = (outs[pair],)
    return call(spread_kernel, "spread", outs, [VMEM] * heads, queries.shape)


def on_device(queries, keys, values, tile_lists, live_counts):
    ctx, heads = lax.axis_size("ctx"), lax.axis_size("head")
    bias = mask_bias(tile_lists, live_counts, tile_lists.shape[0] * ctx)
    in_chunks = queries.shape[0] == BLOCK * TILE and heads * BLOCK >= EDGE
    form = in_pairs if in_chunks and heads in (4, 8) and ctx % 2 == 0 else whole_range
    return form(queries, keys, values, bias)


def solution(mesh):
    return jax.shard_map(
        on_device,
        mesh=mesh,
        in_specs=(
            P(("groups", "ctx", "head"), None),
            P(("groups", "ctx", "head"), None),
            P(("groups", "ctx", "head"), None),
            P(("groups", "ctx"), None),
            P(("groups", "ctx")),
        ),
        out_specs=P(("groups", "ctx", "head"), None),
        check_vma=False,
    )
```

```python
import functools
import math

import jax
import jax.numpy as jnp
from jax import lax
from jax.experimental import pallas as pl
from jax.experimental.pallas import tpu as pltpu
from jax.sharding import PartitionSpec as P

HDIM = 128
TILE = 128
EDGE = 8
LIST = 16
BLOCK = 3
WINDOW = BLOCK + LIST - 1
HIDDEN = -1e30
EXPONENT_SCALE = HDIM ** (-0.5) * math.log2(math.e)
SMEM = pl.BlockSpec(memory_space=pltpu.SMEM)
VMEM = pl.BlockSpec(memory_space=pltpu.VMEM)


def call(kernel, name, operands, in_specs, shapes, scratch=(), limit=8, cost=None):
    out_shape = jax.tree.map(
        lambda shape: shape if hasattr(shape, "dtype") else jax.ShapeDtypeStruct(shape, jnp.bfloat16),
        shapes,
        is_leaf=lambda node: isinstance(node, tuple) or hasattr(node, "dtype"),
    )
    return pl.pallas_call(
        kernel,
        out_shape=out_shape,
        in_specs=in_specs,
        out_specs=jax.tree.map(lambda _: VMEM, out_shape),
        scratch_shapes=scratch,
        compiler_params=pltpu.CompilerParams(vmem_limit_bytes=limit << 20),
        cost_estimate=cost,
        name=name,
    )(*operands)


def column_of(head):
    return pl.ds(pl.multiple_of(head * HDIM, HDIM), HDIM)


def rows_of(tile):
    return slice(tile * TILE, (tile + 1) * TILE)


def bias_kernel(total_tiles, lists_ref, counts_ref, bias_ref):
    tiles, entries = lists_ref.shape
    lists = lists_ref[...]
    entry = lax.broadcasted_iota(jnp.int32, lists.shape, 1)
    row = lax.broadcasted_iota(jnp.int32, lists.shape, 0)
    live = (entry < counts_ref[...]) & (lists >= 0) & (lists < total_tiles)
    places = jnp.where(live, lists - lists[:, :1] + row + EDGE, -1)
    listed = [jnp.broadcast_to(places[:, at : at + 1], (tiles, TILE)) for at in range(entries)]
    for place in range(bias_ref.shape[0]):
        visible = listed[0] == place
        for at in range(1, entries):
            visible |= listed[at] == place
        bias_ref[place] = jnp.where(visible, 0.0, HIDDEN)


def mask_bias(tile_lists, live_counts, total_tiles):
    tiles = tile_lists.shape[0]
    shape = jax.ShapeDtypeStruct((tiles + LIST - 1, tiles, TILE), jnp.float32)
    kernel = functools.partial(bias_kernel, total_tiles)
    return call(kernel, "mask_bias", (tile_lists, live_counts[:, None]), [VMEM] * 2, shape)


def attend_block(first, q_ref, kt_ref, v_ref, bias_ref, out_ref, scores, probs):
    for pair in range(WINDOW // 2):
        low = max(0, 2 * pair - LIST + 1)
        high = min(BLOCK - 1, 2 * pair + 1)
        at = first + 2 * pair
        keys = jnp.concatenate([kt_ref[at], kt_ref[at + 1]], axis=1)
        part = jnp.dot(
            q_ref[low * TILE : (high + 1) * TILE, :], keys, preferred_element_type=jnp.float32
        )
        for half in range(2):
            for tile in range(low, high + 1):
                offset = 2 * pair + half - tile
                if 0 <= offset < LIST:
                    bias = bias_ref[at + half, pl.ds(first + tile, 1), :]
                    scores[tile, :, rows_of(offset)] = part[rows_of(tile - low), rows_of(half)] + bias
    for tile in range(BLOCK):
        highest = scores[tile, :, rows_of(0)]
        for offset in range(1, LIST):
            highest = jnp.maximum(highest, scores[tile, :, rows_of(offset)])
        highest = jnp.broadcast_to(jnp.max(highest, axis=1, keepdims=True), (TILE, TILE))
        total = jnp.zeros((TILE, TILE), jnp.float32)
        for offset in range(LIST):
            weights = jnp.exp2((scores[tile, :, rows_of(offset)] - highest) * EXPONENT_SCALE)
            total += weights
            probs[tile, :, rows_of(offset)] = weights.astype(jnp.bfloat16)
        values = v_ref[pl.ds(first + tile, LIST)].reshape(LIST * TILE, HDIM)
        mixed = jnp.dot(probs[tile], values, preferred_element_type=jnp.float32)
        out_ref[rows_of(tile), :] = (mixed / jnp.sum(total, axis=1, keepdims=True)).astype(jnp.bfloat16)


def block_scratch():
    shape = (BLOCK, TILE, LIST * TILE)
    return [pltpu.VMEM(shape, jnp.float32), pltpu.VMEM(shape, jnp.bfloat16)]


def cost(tile_pairs):
    pairs = tile_pairs * TILE * TILE
    return pl.CostEstimate(flops=4 * pairs * HDIM, bytes_accessed=pairs, transcendentals=pairs)


def halo(array, dim, unit):
    ctx = lax.axis_size("ctx")
    count = array.shape[dim]
    tail = lax.slice_in_dim(array, count - EDGE * unit, count, axis=dim)
    head = lax.slice_in_dim(array, 0, (EDGE - 1) * unit, axis=dim)
    low = lax.ppermute(tail, "ctx", [(i, i + 1) for i in range(ctx - 1)])
    high = lax.ppermute(head, "ctx", [(i + 1, i) for i in range(ctx - 1)])
    return low, high


def pack_kernel(heads, q_ref, k_ref, v_ref, q_out, k_out, v_out):
    for source, target in ((k_ref, k_out), (v_ref, v_out), (q_ref, q_out)):
        for head in range(heads):
            target[head] = source[:, head * HDIM : (head + 1) * HDIM]


def unpack_kernel(heads, parts_ref, out_ref):
    for head in range(heads):
        out_ref[:, head * HDIM : (head + 1) * HDIM] = parts_ref[head]


def attend_range_kernel(q_ref, k_low, k_own, k_high, v_low, v_own, v_high, bias_ref, out_ref, kt, v, *scratch):
    at = 0
    for k_part, v_part in ((k_low, v_low), (k_own, v_own), (k_high, v_high)):
        for tile in range(k_part.shape[0] // TILE):
            kt[at] = k_part[rows_of(tile), :].T
            v[at] = v_part[rows_of(tile), :]
            at += 1

    @pl.loop(0, q_ref.shape[0] // (BLOCK * TILE))
    def _(block):
        place = pl.ds(pl.multiple_of(block * BLOCK * TILE, TILE), BLOCK * TILE)
        attend_block(block * BLOCK, q_ref.at[place, :], kt, v, bias_ref, out_ref.at[place, :], *scratch)


def to_heads(array):
    heads, rows, _ = array.shape
    return lax.all_to_all(array, "head", split_axis=0, concat_axis=0, tiled=True).reshape(heads * rows, HDIM)


def whole_range(queries, keys, values, bias):
    rows, columns = queries.shape
    heads = columns // HDIM
    parts = (heads, rows, HDIM)
    q_parts, k_parts, v_parts = call(
        functools.partial(pack_kernel, heads), "pack", (queries, keys, values), [VMEM] * 3, [parts] * 3
    )
    k_own, v_own = to_heads(k_parts), to_heads(v_parts)
    (k_low, k_high), (v_low, v_high) = halo(k_own, 0, TILE), halo(v_own, 0, TILE)
    local_q = to_heads(q_parts)
    padded = heads * rows // TILE + LIST - 1
    head_out = call(
        attend_range_kernel,
        "attend_range",
        (local_q, k_low, k_own, k_high, v_low, v_own, v_high, bias),
        [VMEM] * 8,
        (heads * rows, HDIM),
        [pltpu.VMEM((padded, TILE, HDIM), jnp.bfloat16)] * 2 + block_scratch(),
        24,
    )
    back = lax.all_to_all(head_out.reshape(parts), "head", split_axis=0, concat_axis=0, tiled=True)
    return call(functools.partial(unpack_kernel, heads), "unpack", (back,), [VMEM], (rows, columns))


def load_tiles_kernel(pair, array_ref, *refs, turn):
    columns = column_of(lax.axis_index("head") ^ pair)
    for tile in range(BLOCK):
        part = array_ref[rows_of(tile), columns]
        refs[-1][tile] = part.T if turn else part


def load_kq_kernel(pair, k_ref, q_ref, *refs):
    columns = column_of(lax.axis_index("head") ^ pair)
    for tile in range(BLOCK):
        refs[-1][tile] = k_ref[rows_of(tile), columns].T
        refs[-1][BLOCK + tile] = q_ref[rows_of(tile), columns]


def load_q_kernel(pair, q_ref, *refs):
    refs[-1][...] = q_ref[:, column_of(lax.axis_index("head") ^ pair)]


def gather_kernel(*refs):
    *parts, own_ref = refs
    me = lax.axis_index("head")
    for pair, part in enumerate(parts):
        own_ref[pl.ds((me ^ pair) * BLOCK, BLOCK)] = part[:BLOCK]


def edges_kernel(own_ref, odd_ref, even_ref):
    last = own_ref.shape[0] - EDGE
    odd = lax.rem(lax.axis_index("ctx"), 2)
    odd_ref[...] = own_ref[pl.ds(odd * last, EDGE)]
    even_ref[...] = own_ref[pl.ds((1 - odd) * last, EDGE)]


def join_kernel(own_ref, first_ref, second_ref, out_ref):
    odd = lax.rem(lax.axis_index("ctx"), 2)
    tiles = own_ref.shape[0]
    out_ref[EDGE : EDGE + tiles] = own_ref[...]

    def around(low_ref, high_ref):
        out_ref[:EDGE] = low_ref[...]
        out_ref[EDGE + tiles :] = high_ref[: EDGE - 1]

    @pl.when(odd == 1)
    def _():
        around(second_ref, first_ref)

    @pl.when(odd == 0)
    def _():
        around(first_ref, second_ref)


def with_halo(parts):
    heads, ctx = len(parts), lax.axis_size("ctx")
    tiles, edge = heads * BLOCK, (EDGE, TILE, HDIM)
    own = call(gather_kernel, "gather", parts, [VMEM] * heads, (tiles, TILE, HDIM))
    odd_edge, even_edge = call(edges_kernel, "edges", (own,), [VMEM], [edge, edge])

    def exchange(array, first):
        lower = range(first, ctx - 1, 2)
        return lax.ppermute(array, "ctx", [(i, i + 1) for i in lower] + [(i + 1, i) for i in lower])

    operands = (own, exchange(odd_edge, 1), exchange(even_edge, 0))
    return call(join_kernel, "join", operands, [VMEM] * 3, (tiles + LIST - 1, TILE, HDIM))


def stack_kernel(*refs):
    *q_refs, out_ref = refs
    for at, ref in enumerate(q_refs):
        if len(ref.shape) == 2:
            out_ref[at] = ref[...]
        else:
            for tile in range(BLOCK):
                out_ref[at, rows_of(tile), :] = ref[BLOCK + tile]


def pass_kernel(array_ref, *refs):
    refs[-1][...] = array_ref[...]


def attend_chunk_kernel(pair, q_ref, kt_ref, v_ref, bias_ref, *refs):
    out_ref, *scratch = refs[-3:]
    first = (lax.axis_index("head") ^ pair) * BLOCK
    attend_block(first, q_ref.at[pair], kt_ref, v_ref, bias_ref, out_ref, *scratch)


def spread_kernel(*refs):
    *parts, out_ref = refs
    me = lax.axis_index("head")
    for pair, part in enumerate(parts):
        out_ref[:, column_of(me ^ pair)] = part[...]


def in_pairs(queries, keys, values, bias):
    heads = lax.axis_size("head")
    chunk, tiles = (queries.shape[0], HDIM), (BLOCK, TILE, HDIM)
    order = range(heads - 1, 0, -1)

    def exchange(array, pair):
        return lax.ppermute(array, "head", [(i, i ^ pair) for i in range(heads)])

    def call_on(kernel, name, operands, shape):
        return call(kernel, name, operands, [VMEM] * len(operands), shape)

    v_parts, k_parts, q_parts = [None] * heads, [None] * heads, [None] * heads
    for pair in [*order, 0]:
        part = call_on(functools.partial(load_tiles_kernel, pair, turn=False), "load_v", (values,), tiles)
        v_parts[pair] = exchange(part, pair) if pair else part
    for pair in [*order, 0]:
        operands = (keys, queries) if pair == 1 else (keys,)
        kernel = load_kq_kernel if pair == 1 else functools.partial(load_tiles_kernel, turn=True)
        shape = (len(operands) * BLOCK, TILE, HDIM)
        after = (v_parts[pair],) if pair else ()
        if pair == order[0]:
            after += (bias,)
        part = call_on(functools.partial(kernel, pair), "load_k", (*operands, *after), shape)
        k_parts[pair] = exchange(part, pair) if pair else part
    q_parts[1] = k_parts[1]
    for pair in [*order[:-1], 0]:
        operands = (queries, k_parts[pair]) if pair else (queries,)
        part = call_on(functools.partial(load_q_kernel, pair), "load_q", operands, chunk)
        q_parts[pair] = exchange(part, pair) if pair else part
    all_values, all_keys = with_halo(v_parts), with_halo(k_parts)
    local_q = call(stack_kernel, "stack", q_parts, [VMEM] * heads, (heads, *chunk), cost=cost(100))
    all_values = call(
        pass_kernel, "values", (all_values, local_q), [VMEM] * 2, all_values.shape, cost=cost(16384)
    )
    outs = [None] * heads
    after = ()
    for pair in [*order, 0]:
        operands = (local_q, all_keys, all_values, bias, *after)
        outs[pair] = call(
            functools.partial(attend_chunk_kernel, pair),
            "attend_chunk",
            operands,
            [VMEM] * len(operands),
            chunk,
            block_scratch(),
            16,
            cost(BLOCK * LIST // 2 if pair else 1),
        )
        after = (outs[pair],)
        if pair:
            outs[pair] = exchange(outs[pair], pair)
    after = ()
    for pair in order:
        operands = (outs[pair], *after)
        outs[pair] = call(
            pass_kernel, "landed", operands, [VMEM] * len(operands), chunk, cost=cost(BLOCK * LIST // 2)
        )
        after = (outs[pair],)
    return call(spread_kernel, "spread", outs, [VMEM] * heads, queries.shape)


def on_device(queries, keys, values, tile_lists, live_counts):
    ctx, heads = lax.axis_size("ctx"), lax.axis_size("head")
    bias = mask_bias(tile_lists, live_counts, tile_lists.shape[0] * ctx)
    in_chunks = queries.shape[0] == BLOCK * TILE and heads * BLOCK >= EDGE
    form = in_pairs if in_chunks and heads in (4, 8) and ctx % 2 == 0 else whole_range
    return form(queries, keys, values, bias)


def solution(mesh):
    return jax.shard_map(
        on_device,
        mesh=mesh,
        in_specs=(
            P(("groups", "ctx", "head"), None),
            P(("groups", "ctx", "head"), None),
            P(("groups", "ctx", "head"), None),
            P(("groups", "ctx"), None),
            P(("groups", "ctx")),
        ),
        out_specs=P(("groups", "ctx", "head"), None),
        check_vma=False,
    )
```

```python
import functools
import math

import jax
import jax.numpy as jnp
from jax import lax
from jax.experimental import pallas as pl
from jax.experimental.pallas import tpu as pltpu
from jax.sharding import PartitionSpec as P

HDIM = 128
TILE = 128
EDGE = 8
LIST = 16
BLOCK = 3
WINDOW = BLOCK + LIST - 1
HIDDEN = -1e30
EXPONENT_SCALE = HDIM ** (-0.5) * math.log2(math.e)
SMEM = pl.BlockSpec(memory_space=pltpu.SMEM)
VMEM = pl.BlockSpec(memory_space=pltpu.VMEM)


def call(kernel, name, operands, in_specs, shapes, scratch=(), limit=8, cost=None):
    out_shape = jax.tree.map(
        lambda shape: shape if hasattr(shape, "dtype") else jax.ShapeDtypeStruct(shape, jnp.bfloat16),
        shapes,
        is_leaf=lambda node: isinstance(node, tuple) or hasattr(node, "dtype"),
    )
    return pl.pallas_call(
        kernel,
        out_shape=out_shape,
        in_specs=in_specs,
        out_specs=jax.tree.map(lambda _: VMEM, out_shape),
        scratch_shapes=scratch,
        compiler_params=pltpu.CompilerParams(vmem_limit_bytes=limit << 20),
        cost_estimate=cost,
        name=name,
    )(*operands)


def column_of(head):
    return pl.ds(pl.multiple_of(head * HDIM, HDIM), HDIM)


def rows_of(tile):
    return slice(tile * TILE, (tile + 1) * TILE)


def bias_kernel(total_tiles, lists_ref, counts_ref, bias_ref):
    tiles, entries = lists_ref.shape
    lists = lists_ref[...]
    entry = lax.broadcasted_iota(jnp.int32, lists.shape, 1)
    row = lax.broadcasted_iota(jnp.int32, lists.shape, 0)
    live = (entry < counts_ref[...]) & (lists >= 0) & (lists < total_tiles)
    places = jnp.where(live, lists - lists[:, :1] + row + EDGE, -1)
    listed = [jnp.broadcast_to(places[:, at : at + 1], (tiles, TILE)) for at in range(entries)]
    for place in range(bias_ref.shape[0]):
        visible = listed[0] == place
        for at in range(1, entries):
            visible |= listed[at] == place
        bias_ref[place] = jnp.where(visible, 0.0, HIDDEN)


def mask_bias(tile_lists, live_counts, total_tiles):
    tiles = tile_lists.shape[0]
    shape = jax.ShapeDtypeStruct((tiles + LIST - 1, tiles, TILE), jnp.float32)
    kernel = functools.partial(bias_kernel, total_tiles)
    return call(kernel, "mask_bias", (tile_lists, live_counts[:, None]), [VMEM] * 2, shape)


def attend_block(first, q_ref, kt_ref, v_ref, bias_ref, out_ref, scores, probs):
    def score(tile):
        row = first + tile
        highest = jnp.full((TILE, TILE), HIDDEN, jnp.float32)
        for offset in range(0, LIST, 2):
            at = row + offset
            keys = jnp.concatenate([kt_ref[at], kt_ref[at + 1]], axis=1)
            part = jnp.dot(q_ref[rows_of(tile), :], keys, preferred_element_type=jnp.float32)
            for half in range(2):
                masked = part[:, rows_of(half)] + bias_ref[at + half, pl.ds(row, 1), :]
                scores[tile, :, rows_of(offset + half)] = masked
                highest = jnp.maximum(highest, masked)
        return jnp.broadcast_to(jnp.max(highest, axis=1, keepdims=True), (TILE, TILE))

    maxima = [score(0)]
    for tile in range(BLOCK):
        if tile + 1 < BLOCK:
            maxima.append(score(tile + 1))
        total = jnp.zeros((TILE, TILE), jnp.float32)
        for offset in range(LIST):
            weights = jnp.exp2((scores[tile, :, rows_of(offset)] - maxima[tile]) * EXPONENT_SCALE)
            total += weights
            probs[tile, :, rows_of(offset)] = weights.astype(jnp.bfloat16)
        values = v_ref[pl.ds(first + tile, LIST)].reshape(LIST * TILE, HDIM)
        mixed = jnp.dot(probs[tile], values, preferred_element_type=jnp.float32)
        out_ref[rows_of(tile), :] = (mixed / jnp.sum(total, axis=1, keepdims=True)).astype(jnp.bfloat16)


def block_scratch():
    shape = (BLOCK, TILE, LIST * TILE)
    return [pltpu.VMEM(shape, jnp.float32), pltpu.VMEM(shape, jnp.bfloat16)]


def cost(tile_pairs):
    pairs = tile_pairs * TILE * TILE
    return pl.CostEstimate(flops=4 * pairs * HDIM, bytes_accessed=pairs, transcendentals=pairs)


def halo(array, dim, unit):
    ctx = lax.axis_size("ctx")
    count = array.shape[dim]
    tail = lax.slice_in_dim(array, count - EDGE * unit, count, axis=dim)
    head = lax.slice_in_dim(array, 0, (EDGE - 1) * unit, axis=dim)
    low = lax.ppermute(tail, "ctx", [(i, i + 1) for i in range(ctx - 1)])
    high = lax.ppermute(head, "ctx", [(i + 1, i) for i in range(ctx - 1)])
    return low, high


def pack_kernel(heads, q_ref, k_ref, v_ref, q_out, k_out, v_out):
    for source, target in ((k_ref, k_out), (v_ref, v_out), (q_ref, q_out)):
        for head in range(heads):
            target[head] = source[:, head * HDIM : (head + 1) * HDIM]


def unpack_kernel(heads, parts_ref, out_ref):
    for head in range(heads):
        out_ref[:, head * HDIM : (head + 1) * HDIM] = parts_ref[head]


def attend_range_kernel(q_ref, k_low, k_own, k_high, v_low, v_own, v_high, bias_ref, out_ref, kt, v, *scratch):
    at = 0
    for k_part, v_part in ((k_low, v_low), (k_own, v_own), (k_high, v_high)):
        for tile in range(k_part.shape[0] // TILE):
            kt[at] = k_part[rows_of(tile), :].T
            v[at] = v_part[rows_of(tile), :]
            at += 1

    @pl.loop(0, q_ref.shape[0] // (BLOCK * TILE))
    def _(block):
        place = pl.ds(pl.multiple_of(block * BLOCK * TILE, TILE), BLOCK * TILE)
        attend_block(block * BLOCK, q_ref.at[place, :], kt, v, bias_ref, out_ref.at[place, :], *scratch)


def to_heads(array):
    heads, rows, _ = array.shape
    return lax.all_to_all(array, "head", split_axis=0, concat_axis=0, tiled=True).reshape(heads * rows, HDIM)


def whole_range(queries, keys, values, bias):
    rows, columns = queries.shape
    heads = columns // HDIM
    parts = (heads, rows, HDIM)
    q_parts, k_parts, v_parts = call(
        functools.partial(pack_kernel, heads), "pack", (queries, keys, values), [VMEM] * 3, [parts] * 3
    )
    k_own, v_own = to_heads(k_parts), to_heads(v_parts)
    (k_low, k_high), (v_low, v_high) = halo(k_own, 0, TILE), halo(v_own, 0, TILE)
    local_q = to_heads(q_parts)
    padded = heads * rows // TILE + LIST - 1
    head_out = call(
        attend_range_kernel,
        "attend_range",
        (local_q, k_low, k_own, k_high, v_low, v_own, v_high, bias),
        [VMEM] * 8,
        (heads * rows, HDIM),
        [pltpu.VMEM((padded, TILE, HDIM), jnp.bfloat16)] * 2 + block_scratch(),
        24,
    )
    back = lax.all_to_all(head_out.reshape(parts), "head", split_axis=0, concat_axis=0, tiled=True)
    return call(functools.partial(unpack_kernel, heads), "unpack", (back,), [VMEM], (rows, columns))


def load_tiles_kernel(pair, array_ref, *refs, turn):
    columns = column_of(lax.axis_index("head") ^ pair)
    for tile in range(BLOCK):
        part = array_ref[rows_of(tile), columns]
        refs[-1][tile] = part.T if turn else part


def load_kq_kernel(pair, k_ref, q_ref, *refs):
    columns = column_of(lax.axis_index("head") ^ pair)
    for tile in range(BLOCK):
        refs[-1][tile] = k_ref[rows_of(tile), columns].T
        refs[-1][BLOCK + tile] = q_ref[rows_of(tile), columns]


def load_q_kernel(pair, q_ref, *refs):
    refs[-1][...] = q_ref[:, column_of(lax.axis_index("head") ^ pair)]


def gather_kernel(*refs):
    *parts, own_ref = refs
    me = lax.axis_index("head")
    for pair, part in enumerate(parts):
        own_ref[pl.ds((me ^ pair) * BLOCK, BLOCK)] = part[:BLOCK]


def edges_kernel(own_ref, odd_ref, even_ref):
    last = own_ref.shape[0] - EDGE
    odd = lax.rem(lax.axis_index("ctx"), 2)
    odd_ref[...] = own_ref[pl.ds(odd * last, EDGE)]
    even_ref[...] = own_ref[pl.ds((1 - odd) * last, EDGE)]


def join_kernel(own_ref, first_ref, second_ref, out_ref):
    odd = lax.rem(lax.axis_index("ctx"), 2)
    tiles = own_ref.shape[0]
    out_ref[EDGE : EDGE + tiles] = own_ref[...]

    def around(low_ref, high_ref):
        out_ref[:EDGE] = low_ref[...]
        out_ref[EDGE + tiles :] = high_ref[: EDGE - 1]

    @pl.when(odd == 1)
    def _():
        around(second_ref, first_ref)

    @pl.when(odd == 0)
    def _():
        around(first_ref, second_ref)


def with_halo(parts):
    heads, ctx = len(parts), lax.axis_size("ctx")
    tiles, edge = heads * BLOCK, (EDGE, TILE, HDIM)
    own = call(gather_kernel, "gather", parts, [VMEM] * heads, (tiles, TILE, HDIM))
    odd_edge, even_edge = call(edges_kernel, "edges", (own,), [VMEM], [edge, edge])

    def exchange(array, first):
        lower = range(first, ctx - 1, 2)
        return lax.ppermute(array, "ctx", [(i, i + 1) for i in lower] + [(i + 1, i) for i in lower])

    operands = (own, exchange(odd_edge, 1), exchange(even_edge, 0))
    return call(join_kernel, "join", operands, [VMEM] * 3, (tiles + LIST - 1, TILE, HDIM))


def stack_kernel(*refs):
    *q_refs, out_ref = refs
    for at, ref in enumerate(q_refs):
        if len(ref.shape) == 2:
            out_ref[at] = ref[...]
        else:
            for tile in range(BLOCK):
                out_ref[at, rows_of(tile), :] = ref[BLOCK + tile]


def pass_kernel(array_ref, *refs):
    refs[-1][...] = array_ref[...]


def attend_chunk_kernel(pair, q_ref, kt_ref, v_ref, bias_ref, *refs):
    out_ref, *scratch = refs[-3:]
    first = (lax.axis_index("head") ^ pair) * BLOCK
    attend_block(first, q_ref.at[pair], kt_ref, v_ref, bias_ref, out_ref, *scratch)


def spread_kernel(*refs):
    *parts, out_ref = refs
    me = lax.axis_index("head")
    for pair, part in enumerate(parts):
        out_ref[:, column_of(me ^ pair)] = part[...]


def in_pairs(queries, keys, values, bias):
    heads = lax.axis_size("head")
    chunk, tiles = (queries.shape[0], HDIM), (BLOCK, TILE, HDIM)
    order = range(heads - 1, 0, -1)

    def exchange(array, pair):
        return lax.ppermute(array, "head", [(i, i ^ pair) for i in range(heads)])

    def call_on(kernel, name, operands, shape):
        return call(kernel, name, operands, [VMEM] * len(operands), shape)

    v_parts, k_parts, q_parts = [None] * heads, [None] * heads, [None] * heads
    for pair in [*order, 0]:
        part = call_on(functools.partial(load_tiles_kernel, pair, turn=False), "load_v", (values,), tiles)
        v_parts[pair] = exchange(part, pair) if pair else part
    for pair in [*order, 0]:
        operands = (keys, queries) if pair == 1 else (keys,)
        kernel = load_kq_kernel if pair == 1 else functools.partial(load_tiles_kernel, turn=True)
        shape = (len(operands) * BLOCK, TILE, HDIM)
        after = (v_parts[pair],) if pair else ()
        if pair == order[0]:
            after += (bias,)
        part = call_on(functools.partial(kernel, pair), "load_k", (*operands, *after), shape)
        k_parts[pair] = exchange(part, pair) if pair else part
    q_parts[1] = k_parts[1]
    for pair in [*order[:-1], 0]:
        operands = (queries, k_parts[pair]) if pair else (queries,)
        part = call_on(functools.partial(load_q_kernel, pair), "load_q", operands, chunk)
        q_parts[pair] = exchange(part, pair) if pair else part
    all_values, all_keys = with_halo(v_parts), with_halo(k_parts)
    local_q = call(stack_kernel, "stack", q_parts, [VMEM] * heads, (heads, *chunk), cost=cost(100))
    all_values = call(
        pass_kernel, "values", (all_values, local_q), [VMEM] * 2, all_values.shape, cost=cost(16384)
    )
    outs = [None] * heads
    after = ()
    for pair in [*order, 0]:
        operands = (local_q, all_keys, all_values, bias, *after)
        outs[pair] = call(
            functools.partial(attend_chunk_kernel, pair),
            "attend_chunk",
            operands,
            [VMEM] * len(operands),
            chunk,
            block_scratch(),
            16,
            cost(BLOCK * LIST // 2 if pair else 1),
        )
        after = (outs[pair],)
        if pair:
            outs[pair] = exchange(outs[pair], pair)
    after = ()
    for pair in order:
        operands = (outs[pair], *after)
        outs[pair] = call(
            pass_kernel, "landed", operands, [VMEM] * len(operands), chunk, cost=cost(BLOCK * LIST // 2)
        )
        after = (outs[pair],)
    return call(spread_kernel, "spread", outs, [VMEM] * heads, queries.shape)


def on_device(queries, keys, values, tile_lists, live_counts):
    ctx, heads = lax.axis_size("ctx"), lax.axis_size("head")
    bias = mask_bias(tile_lists, live_counts, tile_lists.shape[0] * ctx)
    in_chunks = queries.shape[0] == BLOCK * TILE and heads * BLOCK >= EDGE
    form = in_pairs if in_chunks and heads in (4, 8) and ctx % 2 == 0 else whole_range
    return form(queries, keys, values, bias)


def solution(mesh):
    return jax.shard_map(
        on_device,
        mesh=mesh,
        in_specs=(
            P(("groups", "ctx", "head"), None),
            P(("groups", "ctx", "head"), None),
            P(("groups", "ctx", "head"), None),
            P(("groups", "ctx"), None),
            P(("groups", "ctx")),
        ),
        out_specs=P(("groups", "ctx", "head"), None),
        check_vma=False,
    )
```

```python
import functools
import math

import jax
import jax.numpy as jnp
from jax import lax
from jax.experimental import pallas as pl
from jax.experimental.pallas import tpu as pltpu
from jax.sharding import PartitionSpec as P

HDIM = 128
TILE = 128
EDGE = 8
LIST = 16
BLOCK = 3
WINDOW = BLOCK + LIST - 1
HIDDEN = -1e30
EXPONENT_SCALE = HDIM ** (-0.5) * math.log2(math.e)
SMEM = pl.BlockSpec(memory_space=pltpu.SMEM)
VMEM = pl.BlockSpec(memory_space=pltpu.VMEM)


def call(kernel, name, operands, in_specs, shapes, scratch=(), limit=8, cost=None):
    out_shape = jax.tree.map(
        lambda shape: shape if hasattr(shape, "dtype") else jax.ShapeDtypeStruct(shape, jnp.bfloat16),
        shapes,
        is_leaf=lambda node: isinstance(node, tuple) or hasattr(node, "dtype"),
    )
    return pl.pallas_call(
        kernel,
        out_shape=out_shape,
        in_specs=in_specs,
        out_specs=jax.tree.map(lambda _: VMEM, out_shape),
        scratch_shapes=scratch,
        compiler_params=pltpu.CompilerParams(vmem_limit_bytes=limit << 20),
        cost_estimate=cost,
        name=name,
    )(*operands)


def column_of(head):
    return pl.ds(pl.multiple_of(head * HDIM, HDIM), HDIM)


def rows_of(tile):
    return slice(tile * TILE, (tile + 1) * TILE)


def bias_kernel(total_tiles, lists_ref, counts_ref, bias_ref):
    tiles, entries = lists_ref.shape
    lists = lists_ref[...]
    entry = lax.broadcasted_iota(jnp.int32, lists.shape, 1)
    row = lax.broadcasted_iota(jnp.int32, lists.shape, 0)
    live = (entry < counts_ref[...]) & (lists >= 0) & (lists < total_tiles)
    places = jnp.where(live, lists - lists[:, :1] + row + EDGE, -1)
    listed = [jnp.broadcast_to(places[:, at : at + 1], (tiles, TILE)) for at in range(entries)]
    for place in range(bias_ref.shape[0]):
        visible = listed[0] == place
        for at in range(1, entries):
            visible |= listed[at] == place
        bias_ref[place] = jnp.where(visible, 0.0, HIDDEN)


def mask_bias(tile_lists, live_counts, total_tiles):
    tiles = tile_lists.shape[0]
    shape = jax.ShapeDtypeStruct((tiles + LIST - 1, tiles, TILE), jnp.float32)
    kernel = functools.partial(bias_kernel, total_tiles)
    return call(kernel, "mask_bias", (tile_lists, live_counts[:, None]), [VMEM] * 2, shape)


def attend_block(first, q_ref, kt_ref, v_ref, bias_ref, out_ref, scores, probs):
    def score(tile):
        row = first + tile
        highest = jnp.full((TILE, TILE), HIDDEN, jnp.float32)
        for offset in range(0, LIST, 2):
            at = row + offset
            keys = jnp.concatenate([kt_ref[at], kt_ref[at + 1]], axis=1)
            part = jnp.dot(q_ref[rows_of(tile), :], keys, preferred_element_type=jnp.float32)
            for half in range(2):
                masked = part[:, rows_of(half)] + bias_ref[at + half, pl.ds(row, 1), :]
                scores[tile, :, rows_of(offset + half)] = masked
                highest = jnp.maximum(highest, masked)
        return jnp.broadcast_to(jnp.max(highest, axis=1, keepdims=True), (TILE, TILE))

    maxima = [score(0)]
    for tile in range(BLOCK):
        if tile + 1 < BLOCK:
            maxima.append(score(tile + 1))
        total = jnp.zeros((TILE, TILE), jnp.float32)
        for offset in range(LIST):
            weights = jnp.exp2((scores[tile, :, rows_of(offset)] - maxima[tile]) * EXPONENT_SCALE)
            total += weights
            probs[tile, :, rows_of(offset)] = weights.astype(jnp.bfloat16)
        values = v_ref[pl.ds(first + tile, LIST)].reshape(LIST * TILE, HDIM)
        mixed = jnp.dot(probs[tile], values, preferred_element_type=jnp.float32)
        out_ref[rows_of(tile), :] = (mixed / jnp.sum(total, axis=1, keepdims=True)).astype(jnp.bfloat16)


def block_scratch():
    shape = (BLOCK, TILE, LIST * TILE)
    return [pltpu.VMEM(shape, jnp.float32), pltpu.VMEM(shape, jnp.bfloat16)]


def cost(tile_pairs):
    pairs = tile_pairs * TILE * TILE
    return pl.CostEstimate(flops=4 * pairs * HDIM, bytes_accessed=pairs, transcendentals=pairs)


def halo(array, dim, unit):
    ctx = lax.axis_size("ctx")
    count = array.shape[dim]
    tail = lax.slice_in_dim(array, count - EDGE * unit, count, axis=dim)
    head = lax.slice_in_dim(array, 0, (EDGE - 1) * unit, axis=dim)
    low = lax.ppermute(tail, "ctx", [(i, i + 1) for i in range(ctx - 1)])
    high = lax.ppermute(head, "ctx", [(i + 1, i) for i in range(ctx - 1)])
    return low, high


def pack_kernel(heads, q_ref, k_ref, v_ref, q_out, k_out, v_out):
    for source, target in ((k_ref, k_out), (v_ref, v_out), (q_ref, q_out)):
        for head in range(heads):
            target[head] = source[:, head * HDIM : (head + 1) * HDIM]


def unpack_kernel(heads, parts_ref, out_ref):
    for head in range(heads):
        out_ref[:, head * HDIM : (head + 1) * HDIM] = parts_ref[head]


def attend_range_kernel(q_ref, k_low, k_own, k_high, v_low, v_own, v_high, bias_ref, out_ref, kt, v, *scratch):
    at = 0
    for k_part, v_part in ((k_low, v_low), (k_own, v_own), (k_high, v_high)):
        for tile in range(k_part.shape[0] // TILE):
            kt[at] = k_part[rows_of(tile), :].T
            v[at] = v_part[rows_of(tile), :]
            at += 1

    @pl.loop(0, q_ref.shape[0] // (BLOCK * TILE))
    def _(block):
        place = pl.ds(pl.multiple_of(block * BLOCK * TILE, TILE), BLOCK * TILE)
        attend_block(block * BLOCK, q_ref.at[place, :], kt, v, bias_ref, out_ref.at[place, :], *scratch)


def to_heads(array):
    heads, rows, _ = array.shape
    return lax.all_to_all(array, "head", split_axis=0, concat_axis=0, tiled=True).reshape(heads * rows, HDIM)


def whole_range(queries, keys, values, bias):
    rows, columns = queries.shape
    heads = columns // HDIM
    parts = (heads, rows, HDIM)
    q_parts, k_parts, v_parts = call(
        functools.partial(pack_kernel, heads), "pack", (queries, keys, values), [VMEM] * 3, [parts] * 3
    )
    k_own, v_own = to_heads(k_parts), to_heads(v_parts)
    (k_low, k_high), (v_low, v_high) = halo(k_own, 0, TILE), halo(v_own, 0, TILE)
    local_q = to_heads(q_parts)
    padded = heads * rows // TILE + LIST - 1
    head_out = call(
        attend_range_kernel,
        "attend_range",
        (local_q, k_low, k_own, k_high, v_low, v_own, v_high, bias),
        [VMEM] * 8,
        (heads * rows, HDIM),
        [pltpu.VMEM((padded, TILE, HDIM), jnp.bfloat16)] * 2 + block_scratch(),
        24,
    )
    back = lax.all_to_all(head_out.reshape(parts), "head", split_axis=0, concat_axis=0, tiled=True)
    return call(functools.partial(unpack_kernel, heads), "unpack", (back,), [VMEM], (rows, columns))


def load_tiles_kernel(pair, array_ref, *refs, turn):
    columns = column_of(lax.axis_index("head") ^ pair)
    for tile in range(BLOCK):
        part = array_ref[rows_of(tile), columns]
        refs[-1][tile] = part.T if turn else part


def load_kq_kernel(pair, k_ref, q_ref, *refs):
    columns = column_of(lax.axis_index("head") ^ pair)
    for tile in range(BLOCK):
        refs[-1][tile] = k_ref[rows_of(tile), columns].T
        refs[-1][BLOCK + tile] = q_ref[rows_of(tile), columns]


def load_q_kernel(pair, q_ref, *refs):
    refs[-1][...] = q_ref[:, column_of(lax.axis_index("head") ^ pair)]


def gather_kernel(*refs):
    *parts, own_ref = refs
    me = lax.axis_index("head")
    for pair, part in enumerate(parts):
        own_ref[pl.ds((me ^ pair) * BLOCK, BLOCK)] = part[:BLOCK]


def edges_kernel(own_ref, odd_ref, even_ref):
    last = own_ref.shape[0] - EDGE
    odd = lax.rem(lax.axis_index("ctx"), 2)
    odd_ref[...] = own_ref[pl.ds(odd * last, EDGE)]
    even_ref[...] = own_ref[pl.ds((1 - odd) * last, EDGE)]


def join_kernel(own_ref, first_ref, second_ref, out_ref):
    odd = lax.rem(lax.axis_index("ctx"), 2)
    tiles = own_ref.shape[0]
    out_ref[EDGE : EDGE + tiles] = own_ref[...]

    def around(low_ref, high_ref):
        out_ref[:EDGE] = low_ref[...]
        out_ref[EDGE + tiles :] = high_ref[: EDGE - 1]

    @pl.when(odd == 1)
    def _():
        around(second_ref, first_ref)

    @pl.when(odd == 0)
    def _():
        around(first_ref, second_ref)


def with_halo(parts):
    heads, ctx = len(parts), lax.axis_size("ctx")
    tiles, edge = heads * BLOCK, (EDGE, TILE, HDIM)
    own = call(gather_kernel, "gather", parts, [VMEM] * heads, (tiles, TILE, HDIM))
    odd_edge, even_edge = call(edges_kernel, "edges", (own,), [VMEM], [edge, edge])

    def exchange(array, first):
        lower = range(first, ctx - 1, 2)
        return lax.ppermute(array, "ctx", [(i, i + 1) for i in lower] + [(i + 1, i) for i in lower])

    operands = (own, exchange(odd_edge, 1), exchange(even_edge, 0))
    return call(join_kernel, "join", operands, [VMEM] * 3, (tiles + LIST - 1, TILE, HDIM))


def stack_kernel(*refs):
    *q_refs, out_ref = refs
    for at, ref in enumerate(q_refs):
        if len(ref.shape) == 2:
            out_ref[at] = ref[...]
        else:
            for tile in range(BLOCK):
                out_ref[at, rows_of(tile), :] = ref[BLOCK + tile]


def pass_kernel(array_ref, *refs):
    refs[-1][...] = array_ref[...]


def attend_chunk_kernel(pair, q_ref, kt_ref, v_ref, bias_ref, *refs):
    out_ref, *scratch = refs[-3:]
    first = (lax.axis_index("head") ^ pair) * BLOCK
    attend_block(first, q_ref.at[pair], kt_ref, v_ref, bias_ref, out_ref, *scratch)


def spread_kernel(*refs):
    *parts, out_ref = refs
    me = lax.axis_index("head")
    for pair, part in enumerate(parts):
        out_ref[:, column_of(me ^ pair)] = part[...]


def in_pairs(queries, keys, values, bias):
    heads = lax.axis_size("head")
    chunk, tiles = (queries.shape[0], HDIM), (BLOCK, TILE, HDIM)
    order = range(heads - 1, 0, -1)

    def exchange(array, pair):
        return lax.ppermute(array, "head", [(i, i ^ pair) for i in range(heads)])

    def call_on(kernel, name, operands, shape):
        return call(kernel, name, operands, [VMEM] * len(operands), shape)

    v_parts, k_parts, q_parts = [None] * heads, [None] * heads, [None] * heads
    for pair in [*order, 0]:
        part = call_on(functools.partial(load_tiles_kernel, pair, turn=False), "load_v", (values,), tiles)
        v_parts[pair] = exchange(part, pair) if pair else part
    for pair in [*order, 0]:
        operands = (keys, queries) if pair == 1 else (keys,)
        kernel = load_kq_kernel if pair == 1 else functools.partial(load_tiles_kernel, turn=True)
        shape = (len(operands) * BLOCK, TILE, HDIM)
        after = (v_parts[1],) if pair else ()
        if pair == order[0]:
            after += (bias,)
        part = call_on(functools.partial(kernel, pair), "load_k", (*operands, *after), shape)
        k_parts[pair] = exchange(part, pair) if pair else part
    q_parts[1] = k_parts[1]
    for pair in [*order[:-1], 0]:
        operands = (queries, k_parts[pair]) if pair else (queries,)
        part = call_on(functools.partial(load_q_kernel, pair), "load_q", operands, chunk)
        q_parts[pair] = exchange(part, pair) if pair else part
    all_values, all_keys = with_halo(v_parts), with_halo(k_parts)
    local_q = call(stack_kernel, "stack", q_parts, [VMEM] * heads, (heads, *chunk), cost=cost(100))
    all_values = call(
        pass_kernel, "values", (all_values, local_q), [VMEM] * 2, all_values.shape, cost=cost(16384)
    )
    outs = [None] * heads
    after = ()
    for pair in [*order, 0]:
        operands = (local_q, all_keys, all_values, bias, *after)
        outs[pair] = call(
            functools.partial(attend_chunk_kernel, pair),
            "attend_chunk",
            operands,
            [VMEM] * len(operands),
            chunk,
            block_scratch(),
            16,
            cost(BLOCK * LIST // 2 if pair else 1),
        )
        after = (outs[pair],)
        if pair:
            outs[pair] = exchange(outs[pair], pair)
    after = ()
    for pair in order:
        operands = (outs[pair], *after)
        outs[pair] = call(
            pass_kernel, "landed", operands, [VMEM] * len(operands), chunk, cost=cost(BLOCK * LIST // 2)
        )
        after = (outs[pair],)
    return call(spread_kernel, "spread", outs, [VMEM] * heads, queries.shape)


def on_device(queries, keys, values, tile_lists, live_counts):
    ctx, heads = lax.axis_size("ctx"), lax.axis_size("head")
    bias = mask_bias(tile_lists, live_counts, tile_lists.shape[0] * ctx)
    in_chunks = queries.shape[0] == BLOCK * TILE and heads * BLOCK >= EDGE
    form = in_pairs if in_chunks and heads in (4, 8) and ctx % 2 == 0 else whole_range
    return form(queries, keys, values, bias)


def solution(mesh):
    return jax.shard_map(
        on_device,
        mesh=mesh,
        in_specs=(
            P(("groups", "ctx", "head"), None),
            P(("groups", "ctx", "head"), None),
            P(("groups", "ctx", "head"), None),
            P(("groups", "ctx"), None),
            P(("groups", "ctx")),
        ),
        out_specs=P(("groups", "ctx", "head"), None),
        check_vma=False,
    )
```

```python
import functools
import math

import jax
import jax.numpy as jnp
from jax import lax
from jax.experimental import pallas as pl
from jax.experimental.pallas import tpu as pltpu
from jax.sharding import PartitionSpec as P

HDIM = 128
TILE = 128
EDGE = 8
LIST = 16
BLOCK = 3
WINDOW = BLOCK + LIST - 1
HIDDEN = -1e30
EXPONENT_SCALE = HDIM ** (-0.5) * math.log2(math.e)
SMEM = pl.BlockSpec(memory_space=pltpu.SMEM)
VMEM = pl.BlockSpec(memory_space=pltpu.VMEM)


def call(kernel, name, operands, in_specs, shapes, scratch=(), limit=8, cost=None):
    out_shape = jax.tree.map(
        lambda shape: shape if hasattr(shape, "dtype") else jax.ShapeDtypeStruct(shape, jnp.bfloat16),
        shapes,
        is_leaf=lambda node: isinstance(node, tuple) or hasattr(node, "dtype"),
    )
    return pl.pallas_call(
        kernel,
        out_shape=out_shape,
        in_specs=in_specs,
        out_specs=jax.tree.map(lambda _: VMEM, out_shape),
        scratch_shapes=scratch,
        compiler_params=pltpu.CompilerParams(vmem_limit_bytes=limit << 20),
        cost_estimate=cost,
        name=name,
    )(*operands)


def column_of(head):
    return pl.ds(pl.multiple_of(head * HDIM, HDIM), HDIM)


def rows_of(tile):
    return slice(tile * TILE, (tile + 1) * TILE)


def bias_kernel(total_tiles, lists_ref, counts_ref, bias_ref):
    tiles, entries = lists_ref.shape
    lists = lists_ref[...]
    entry = lax.broadcasted_iota(jnp.int32, lists.shape, 1)
    row = lax.broadcasted_iota(jnp.int32, lists.shape, 0)
    live = (entry < counts_ref[...]) & (lists >= 0) & (lists < total_tiles)
    places = jnp.where(live, lists - lists[:, :1] + row + EDGE, -1)
    listed = [jnp.broadcast_to(places[:, at : at + 1], (tiles, TILE)) for at in range(entries)]
    for place in range(bias_ref.shape[0]):
        visible = listed[0] == place
        for at in range(1, entries):
            visible |= listed[at] == place
        bias_ref[place] = jnp.where(visible, 0.0, HIDDEN)


def mask_bias(tile_lists, live_counts, total_tiles):
    tiles = tile_lists.shape[0]
    shape = jax.ShapeDtypeStruct((tiles + LIST - 1, tiles, TILE), jnp.float32)
    kernel = functools.partial(bias_kernel, total_tiles)
    return call(kernel, "mask_bias", (tile_lists, live_counts[:, None]), [VMEM] * 2, shape)


def attend_block(first, q_ref, kt_ref, v_ref, bias_ref, out_ref, scores, probs):
    def score(tile):
        row = first + tile
        highest = jnp.full((TILE, TILE), HIDDEN, jnp.float32)
        for offset in range(0, LIST, 2):
            at = row + offset
            keys = jnp.concatenate([kt_ref[at], kt_ref[at + 1]], axis=1)
            part = jnp.dot(q_ref[rows_of(tile), :], keys, preferred_element_type=jnp.float32)
            for half in range(2):
                masked = part[:, rows_of(half)] + bias_ref[at + half, pl.ds(row, 1), :]
                scores[tile, :, rows_of(offset + half)] = masked
                highest = jnp.maximum(highest, masked)
        return jnp.broadcast_to(jnp.max(highest, axis=1, keepdims=True), (TILE, TILE))

    maxima = [score(0)]
    for tile in range(BLOCK):
        if tile + 1 < BLOCK:
            maxima.append(score(tile + 1))
        total = jnp.zeros((TILE, TILE), jnp.float32)
        for offset in range(LIST):
            weights = jnp.exp2((scores[tile, :, rows_of(offset)] - maxima[tile]) * EXPONENT_SCALE)
            total += weights
            probs[tile, :, rows_of(offset)] = weights.astype(jnp.bfloat16)
        values = v_ref[pl.ds(first + tile, LIST)].reshape(LIST * TILE, HDIM)
        mixed = jnp.dot(probs[tile], values, preferred_element_type=jnp.float32)
        out_ref[rows_of(tile), :] = (mixed / jnp.sum(total, axis=1, keepdims=True)).astype(jnp.bfloat16)


def block_scratch():
    shape = (BLOCK, TILE, LIST * TILE)
    return [pltpu.VMEM(shape, jnp.float32), pltpu.VMEM(shape, jnp.bfloat16)]


def cost(tile_pairs):
    pairs = tile_pairs * TILE * TILE
    return pl.CostEstimate(flops=4 * pairs * HDIM, bytes_accessed=pairs, transcendentals=pairs)


def halo(array, dim, unit):
    ctx = lax.axis_size("ctx")
    count = array.shape[dim]
    tail = lax.slice_in_dim(array, count - EDGE * unit, count, axis=dim)
    head = lax.slice_in_dim(array, 0, (EDGE - 1) * unit, axis=dim)
    low = lax.ppermute(tail, "ctx", [(i, i + 1) for i in range(ctx - 1)])
    high = lax.ppermute(head, "ctx", [(i + 1, i) for i in range(ctx - 1)])
    return low, high


def pack_kernel(heads, q_ref, k_ref, v_ref, q_out, k_out, v_out):
    for source, target in ((k_ref, k_out), (v_ref, v_out), (q_ref, q_out)):
        for head in range(heads):
            target[head] = source[:, head * HDIM : (head + 1) * HDIM]


def unpack_kernel(heads, parts_ref, out_ref):
    for head in range(heads):
        out_ref[:, head * HDIM : (head + 1) * HDIM] = parts_ref[head]


def attend_range_kernel(q_ref, k_low, k_own, k_high, v_low, v_own, v_high, bias_ref, out_ref, kt, v, *scratch):
    at = 0
    for k_part, v_part in ((k_low, v_low), (k_own, v_own), (k_high, v_high)):
        for tile in range(k_part.shape[0] // TILE):
            kt[at] = k_part[rows_of(tile), :].T
            v[at] = v_part[rows_of(tile), :]
            at += 1

    @pl.loop(0, q_ref.shape[0] // (BLOCK * TILE))
    def _(block):
        place = pl.ds(pl.multiple_of(block * BLOCK * TILE, TILE), BLOCK * TILE)
        attend_block(block * BLOCK, q_ref.at[place, :], kt, v, bias_ref, out_ref.at[place, :], *scratch)


def to_heads(array):
    heads, rows, _ = array.shape
    return lax.all_to_all(array, "head", split_axis=0, concat_axis=0, tiled=True).reshape(heads * rows, HDIM)


def whole_range(queries, keys, values, bias):
    rows, columns = queries.shape
    heads = columns // HDIM
    parts = (heads, rows, HDIM)
    q_parts, k_parts, v_parts = call(
        functools.partial(pack_kernel, heads), "pack", (queries, keys, values), [VMEM] * 3, [parts] * 3
    )
    k_own, v_own = to_heads(k_parts), to_heads(v_parts)
    (k_low, k_high), (v_low, v_high) = halo(k_own, 0, TILE), halo(v_own, 0, TILE)
    local_q = to_heads(q_parts)
    padded = heads * rows // TILE + LIST - 1
    head_out = call(
        attend_range_kernel,
        "attend_range",
        (local_q, k_low, k_own, k_high, v_low, v_own, v_high, bias),
        [VMEM] * 8,
        (heads * rows, HDIM),
        [pltpu.VMEM((padded, TILE, HDIM), jnp.bfloat16)] * 2 + block_scratch(),
        24,
    )
    back = lax.all_to_all(head_out.reshape(parts), "head", split_axis=0, concat_axis=0, tiled=True)
    return call(functools.partial(unpack_kernel, heads), "unpack", (back,), [VMEM], (rows, columns))


def load_tiles_kernel(pair, array_ref, *refs, turn):
    columns = column_of(lax.axis_index("head") ^ pair)
    for tile in range(BLOCK):
        part = array_ref[rows_of(tile), columns]
        refs[-1][tile] = part.T if turn else part


def load_kq_kernel(pair, k_ref, q_ref, *refs):
    columns = column_of(lax.axis_index("head") ^ pair)
    for tile in range(BLOCK):
        refs[-1][tile] = k_ref[rows_of(tile), columns].T
        refs[-1][BLOCK + tile] = q_ref[rows_of(tile), columns]


def load_q_kernel(pair, q_ref, *refs):
    refs[-1][...] = q_ref[:, column_of(lax.axis_index("head") ^ pair)]


def gather_kernel(*refs):
    *parts, own_ref = refs
    me = lax.axis_index("head")
    for pair, part in enumerate(parts):
        own_ref[pl.ds((me ^ pair) * BLOCK, BLOCK)] = part[:BLOCK]


def edges_kernel(own_ref, odd_ref, even_ref):
    last = own_ref.shape[0] - EDGE
    odd = lax.rem(lax.axis_index("ctx"), 2)
    odd_ref[...] = own_ref[pl.ds(odd * last, EDGE)]
    even_ref[...] = own_ref[pl.ds((1 - odd) * last, EDGE)]


def join_kernel(own_ref, first_ref, second_ref, out_ref):
    odd = lax.rem(lax.axis_index("ctx"), 2)
    tiles = own_ref.shape[0]
    out_ref[EDGE : EDGE + tiles] = own_ref[...]

    def around(low_ref, high_ref):
        out_ref[:EDGE] = low_ref[...]
        out_ref[EDGE + tiles :] = high_ref[: EDGE - 1]

    @pl.when(odd == 1)
    def _():
        around(second_ref, first_ref)

    @pl.when(odd == 0)
    def _():
        around(first_ref, second_ref)


def with_halo(parts):
    heads, ctx = len(parts), lax.axis_size("ctx")
    tiles, edge = heads * BLOCK, (EDGE, TILE, HDIM)
    own = call(gather_kernel, "gather", parts, [VMEM] * heads, (tiles, TILE, HDIM))
    odd_edge, even_edge = call(edges_kernel, "edges", (own,), [VMEM], [edge, edge])

    def exchange(array, first):
        lower = range(first, ctx - 1, 2)
        return lax.ppermute(array, "ctx", [(i, i + 1) for i in lower] + [(i + 1, i) for i in lower])

    operands = (own, exchange(odd_edge, 1), exchange(even_edge, 0))
    return call(join_kernel, "join", operands, [VMEM] * 3, (tiles + LIST - 1, TILE, HDIM))


def stack_kernel(*refs):
    *q_refs, out_ref = refs
    for at, ref in enumerate(q_refs):
        if len(ref.shape) == 2:
            out_ref[at] = ref[...]
        else:
            for tile in range(BLOCK):
                out_ref[at, rows_of(tile), :] = ref[BLOCK + tile]


def pass_kernel(array_ref, *refs):
    refs[-1][...] = array_ref[...]


def attend_chunk_kernel(pair, q_ref, kt_ref, v_ref, bias_ref, *refs):
    out_ref, *scratch = refs[-3:]
    first = (lax.axis_index("head") ^ pair) * BLOCK
    attend_block(first, q_ref.at[pair], kt_ref, v_ref, bias_ref, out_ref, *scratch)


def spread_kernel(pairs, *refs):
    out_ref, sems = refs[-2:]
    me = lax.axis_index("head")
    copies = [
        pltpu.make_async_copy(part, out_ref.at[:, column_of(me ^ pair)], sems.at[at])
        for at, (pair, part) in enumerate(zip(pairs, refs))
    ]
    for copy in copies:
        copy.start()
    for copy in copies:
        copy.wait()


def spread(outs, pairs, shape, *before):
    anywhere = pl.BlockSpec(memory_space=pl.ANY)
    return pl.pallas_call(
        functools.partial(spread_kernel, pairs),
        out_shape=jax.ShapeDtypeStruct(shape, jnp.bfloat16),
        in_specs=[VMEM] * len(pairs) + [anywhere] * len(before),
        out_specs=anywhere,
        scratch_shapes=[pltpu.SemaphoreType.DMA((len(pairs),))],
        input_output_aliases={len(pairs): 0} if before else {},
        compiler_params=pltpu.CompilerParams(vmem_limit_bytes=8 << 20),
        name="spread",
    )(*(outs[pair] for pair in pairs), *before)


def in_pairs(queries, keys, values, bias):
    heads = lax.axis_size("head")
    chunk, tiles = (queries.shape[0], HDIM), (BLOCK, TILE, HDIM)
    order = range(heads - 1, 0, -1)

    def exchange(array, pair):
        return lax.ppermute(array, "head", [(i, i ^ pair) for i in range(heads)])

    def call_on(kernel, name, operands, shape):
        return call(kernel, name, operands, [VMEM] * len(operands), shape)

    v_parts, k_parts, q_parts = [None] * heads, [None] * heads, [None] * heads
    for pair in [*order, 0]:
        column = (lax.axis_index("head") ^ pair) * HDIM
        part = lax.dynamic_slice_in_dim(values, column, HDIM, axis=1).reshape(tiles)
        v_parts[pair] = exchange(part, pair) if pair else part
    for pair in [*order, 0]:
        operands = (keys, queries) if pair == 1 else (keys,)
        kernel = load_kq_kernel if pair == 1 else functools.partial(load_tiles_kernel, turn=True)
        shape = (len(operands) * BLOCK, TILE, HDIM)
        after = (v_parts[1],) if pair else ()
        if pair == order[0]:
            after += (bias,)
        part = call_on(functools.partial(kernel, pair), "load_k", (*operands, *after), shape)
        k_parts[pair] = exchange(part, pair) if pair else part
    q_parts[1] = k_parts[1]
    for pair in [*order[:-1], 0]:
        operands = (queries, k_parts[pair]) if pair else (queries,)
        part = call_on(functools.partial(load_q_kernel, pair), "load_q", operands, chunk)
        q_parts[pair] = exchange(part, pair) if pair else part
    all_values, all_keys = with_halo(v_parts), with_halo(k_parts)
    local_q = call(stack_kernel, "stack", q_parts, [VMEM] * heads, (heads, *chunk), cost=cost(100))
    all_values = call(
        pass_kernel, "values", (all_values, local_q), [VMEM] * 2, all_values.shape, cost=cost(16384)
    )
    outs = [None] * heads
    after = ()
    for pair in [*order, 0]:
        operands = (local_q, all_keys, all_values, bias, *after)
        outs[pair] = call(
            functools.partial(attend_chunk_kernel, pair),
            "attend_chunk",
            operands,
            [VMEM] * len(operands),
            chunk,
            block_scratch(),
            16,
            cost(BLOCK * LIST // 2 if pair else 1),
        )
        after = (outs[pair],)
        if pair:
            outs[pair] = exchange(outs[pair], pair)
    after = ()
    for pair in order:
        operands = (outs[pair], *after)
        outs[pair] = call(
            pass_kernel, "landed", operands, [VMEM] * len(operands), chunk, cost=cost(BLOCK * LIST // 2)
        )
        after = (outs[pair],)
    last = order[-1]
    early = [pair for pair in range(heads) if pair != last]
    return spread(outs, [last], queries.shape, spread(outs, early, queries.shape))


def on_device(queries, keys, values, tile_lists, live_counts):
    ctx, heads = lax.axis_size("ctx"), lax.axis_size("head")
    bias = mask_bias(tile_lists, live_counts, tile_lists.shape[0] * ctx)
    in_chunks = queries.shape[0] == BLOCK * TILE and heads * BLOCK >= EDGE
    form = in_pairs if in_chunks and heads in (4, 8) and ctx % 2 == 0 else whole_range
    return form(queries, keys, values, bias)


def solution(mesh):
    return jax.shard_map(
        on_device,
        mesh=mesh,
        in_specs=(
            P(("groups", "ctx", "head"), None),
            P(("groups", "ctx", "head"), None),
            P(("groups", "ctx", "head"), None),
            P(("groups", "ctx"), None),
            P(("groups", "ctx")),
        ),
        out_specs=P(("groups", "ctx", "head"), None),
        check_vma=False,
    )
```

```python
import functools
import math

import jax
import jax.numpy as jnp
from jax import lax
from jax.experimental import pallas as pl
from jax.experimental.pallas import tpu as pltpu
from jax.sharding import PartitionSpec as P

HDIM = 128
TILE = 128
EDGE = 8
LIST = 16
BLOCK = 3
WINDOW = BLOCK + LIST - 1
HIDDEN = -1e30
EXPONENT_SCALE = HDIM ** (-0.5) * math.log2(math.e)
SMEM = pl.BlockSpec(memory_space=pltpu.SMEM)
VMEM = pl.BlockSpec(memory_space=pltpu.VMEM)


def call(kernel, name, operands, in_specs, shapes, scratch=(), limit=8, cost=None):
    out_shape = jax.tree.map(
        lambda shape: shape if hasattr(shape, "dtype") else jax.ShapeDtypeStruct(shape, jnp.bfloat16),
        shapes,
        is_leaf=lambda node: isinstance(node, tuple) or hasattr(node, "dtype"),
    )
    return pl.pallas_call(
        kernel,
        out_shape=out_shape,
        in_specs=in_specs,
        out_specs=jax.tree.map(lambda _: VMEM, out_shape),
        scratch_shapes=scratch,
        compiler_params=pltpu.CompilerParams(vmem_limit_bytes=limit << 20),
        cost_estimate=cost,
        name=name,
    )(*operands)


def column_of(head):
    return pl.ds(pl.multiple_of(head * HDIM, HDIM), HDIM)


def rows_of(tile):
    return slice(tile * TILE, (tile + 1) * TILE)


def bias_kernel(total_tiles, lists_ref, counts_ref, bias_ref):
    tiles, entries = lists_ref.shape
    lists = lists_ref[...]
    entry = lax.broadcasted_iota(jnp.int32, lists.shape, 1)
    row = lax.broadcasted_iota(jnp.int32, lists.shape, 0)
    live = (entry < counts_ref[...]) & (lists >= 0) & (lists < total_tiles)
    places = jnp.where(live, lists - lists[:, :1] + row + EDGE, -1)
    listed = [jnp.broadcast_to(places[:, at : at + 1], (tiles, TILE)) for at in range(entries)]
    for place in range(bias_ref.shape[0]):
        visible = listed[0] == place
        for at in range(1, entries):
            visible |= listed[at] == place
        bias_ref[place] = jnp.where(visible, 0.0, HIDDEN)


def mask_bias(tile_lists, live_counts, total_tiles):
    tiles = tile_lists.shape[0]
    shape = jax.ShapeDtypeStruct((tiles + LIST - 1, tiles, TILE), jnp.float32)
    kernel = functools.partial(bias_kernel, total_tiles)
    return call(kernel, "mask_bias", (tile_lists, live_counts[:, None]), [VMEM] * 2, shape)


def attend_block(first, q_ref, kt_ref, v_ref, bias_ref, out_ref, scores, probs):
    def score(tile):
        row = first + tile
        highest = jnp.full((TILE, TILE), HIDDEN, jnp.float32)
        for offset in range(0, LIST, 2):
            at = row + offset
            keys = jnp.concatenate([kt_ref[at], kt_ref[at + 1]], axis=1)
            part = jnp.dot(q_ref[rows_of(tile), :], keys, preferred_element_type=jnp.float32)
            for half in range(2):
                masked = part[:, rows_of(half)] + bias_ref[at + half, pl.ds(row, 1), :]
                scores[tile, :, rows_of(offset + half)] = masked
                highest = jnp.maximum(highest, masked)
        return jnp.broadcast_to(jnp.max(highest, axis=1, keepdims=True), (TILE, TILE))

    maxima = [score(0)]
    for tile in range(BLOCK):
        if tile + 1 < BLOCK:
            maxima.append(score(tile + 1))
        total = jnp.zeros((TILE, TILE), jnp.float32)
        for offset in range(LIST):
            weights = jnp.exp2((scores[tile, :, rows_of(offset)] - maxima[tile]) * EXPONENT_SCALE)
            total += weights
            probs[tile, :, rows_of(offset)] = weights.astype(jnp.bfloat16)
        values = v_ref[pl.ds(first + tile, LIST)].reshape(LIST * TILE, HDIM)
        mixed = jnp.dot(probs[tile], values, preferred_element_type=jnp.float32)
        out_ref[rows_of(tile), :] = (mixed / jnp.sum(total, axis=1, keepdims=True)).astype(jnp.bfloat16)


def block_scratch():
    shape = (BLOCK, TILE, LIST * TILE)
    return [pltpu.VMEM(shape, jnp.float32), pltpu.VMEM(shape, jnp.bfloat16)]


def cost(tile_pairs):
    pairs = tile_pairs * TILE * TILE
    return pl.CostEstimate(flops=4 * pairs * HDIM, bytes_accessed=pairs, transcendentals=pairs)


def halo(array, dim, unit):
    ctx = lax.axis_size("ctx")
    count = array.shape[dim]
    tail = lax.slice_in_dim(array, count - EDGE * unit, count, axis=dim)
    head = lax.slice_in_dim(array, 0, (EDGE - 1) * unit, axis=dim)
    low = lax.ppermute(tail, "ctx", [(i, i + 1) for i in range(ctx - 1)])
    high = lax.ppermute(head, "ctx", [(i + 1, i) for i in range(ctx - 1)])
    return low, high


def pack_kernel(heads, q_ref, k_ref, v_ref, q_out, k_out, v_out):
    for source, target in ((k_ref, k_out), (v_ref, v_out), (q_ref, q_out)):
        for head in range(heads):
            target[head] = source[:, head * HDIM : (head + 1) * HDIM]


def unpack_kernel(heads, parts_ref, out_ref):
    for head in range(heads):
        out_ref[:, head * HDIM : (head + 1) * HDIM] = parts_ref[head]


def attend_range_kernel(q_ref, k_low, k_own, k_high, v_low, v_own, v_high, bias_ref, out_ref, kt, v, *scratch):
    at = 0
    for k_part, v_part in ((k_low, v_low), (k_own, v_own), (k_high, v_high)):
        for tile in range(k_part.shape[0] // TILE):
            kt[at] = k_part[rows_of(tile), :].T
            v[at] = v_part[rows_of(tile), :]
            at += 1

    @pl.loop(0, q_ref.shape[0] // (BLOCK * TILE))
    def _(block):
        place = pl.ds(pl.multiple_of(block * BLOCK * TILE, TILE), BLOCK * TILE)
        attend_block(block * BLOCK, q_ref.at[place, :], kt, v, bias_ref, out_ref.at[place, :], *scratch)


def to_heads(array):
    heads, rows, _ = array.shape
    return lax.all_to_all(array, "head", split_axis=0, concat_axis=0, tiled=True).reshape(heads * rows, HDIM)


def whole_range(queries, keys, values, bias):
    rows, columns = queries.shape
    heads = columns // HDIM
    parts = (heads, rows, HDIM)
    q_parts, k_parts, v_parts = call(
        functools.partial(pack_kernel, heads), "pack", (queries, keys, values), [VMEM] * 3, [parts] * 3
    )
    k_own, v_own = to_heads(k_parts), to_heads(v_parts)
    (k_low, k_high), (v_low, v_high) = halo(k_own, 0, TILE), halo(v_own, 0, TILE)
    local_q = to_heads(q_parts)
    padded = heads * rows // TILE + LIST - 1
    head_out = call(
        attend_range_kernel,
        "attend_range",
        (local_q, k_low, k_own, k_high, v_low, v_own, v_high, bias),
        [VMEM] * 8,
        (heads * rows, HDIM),
        [pltpu.VMEM((padded, TILE, HDIM), jnp.bfloat16)] * 2 + block_scratch(),
        24,
    )
    back = lax.all_to_all(head_out.reshape(parts), "head", split_axis=0, concat_axis=0, tiled=True)
    return call(functools.partial(unpack_kernel, heads), "unpack", (back,), [VMEM], (rows, columns))


def load_tiles_kernel(pair, array_ref, *refs, turn):
    columns = column_of(lax.axis_index("head") ^ pair)
    for tile in range(BLOCK):
        part = array_ref[rows_of(tile), columns]
        refs[-1][tile] = part.T if turn else part


def load_kq_kernel(pair, k_ref, q_ref, *refs):
    columns = column_of(lax.axis_index("head") ^ pair)
    for tile in range(BLOCK):
        refs[-1][tile] = k_ref[rows_of(tile), columns].T
        refs[-1][BLOCK + tile] = q_ref[rows_of(tile), columns]


def load_q_kernel(pair, q_ref, *refs):
    refs[-1][...] = q_ref[:, column_of(lax.axis_index("head") ^ pair)]


def gather_kernel(*refs):
    *parts, own_ref = refs
    me = lax.axis_index("head")
    for pair, part in enumerate(parts):
        own_ref[pl.ds((me ^ pair) * BLOCK, BLOCK)] = part[:BLOCK]


def edges_kernel(own_ref, odd_ref, even_ref):
    last = own_ref.shape[0] - EDGE
    odd = lax.rem(lax.axis_index("ctx"), 2)
    odd_ref[...] = own_ref[pl.ds(odd * last, EDGE)]
    even_ref[...] = own_ref[pl.ds((1 - odd) * last, EDGE)]


def join_kernel(own_ref, first_ref, second_ref, out_ref):
    odd = lax.rem(lax.axis_index("ctx"), 2)
    tiles = own_ref.shape[0]
    out_ref[EDGE : EDGE + tiles] = own_ref[...]

    def around(low_ref, high_ref):
        out_ref[:EDGE] = low_ref[...]
        out_ref[EDGE + tiles :] = high_ref[: EDGE - 1]

    @pl.when(odd == 1)
    def _():
        around(second_ref, first_ref)

    @pl.when(odd == 0)
    def _():
        around(first_ref, second_ref)


def with_halo(parts):
    heads, ctx = len(parts), lax.axis_size("ctx")
    tiles, edge = heads * BLOCK, (EDGE, TILE, HDIM)
    own = call(gather_kernel, "gather", parts, [VMEM] * heads, (tiles, TILE, HDIM))
    odd_edge, even_edge = call(edges_kernel, "edges", (own,), [VMEM], [edge, edge])

    def exchange(array, first):
        lower = range(first, ctx - 1, 2)
        return lax.ppermute(array, "ctx", [(i, i + 1) for i in lower] + [(i + 1, i) for i in lower])

    operands = (own, exchange(odd_edge, 1), exchange(even_edge, 0))
    return call(join_kernel, "join", operands, [VMEM] * 3, (tiles + LIST - 1, TILE, HDIM))


def stack_kernel(*refs):
    *q_refs, out_ref = refs
    for at, ref in enumerate(q_refs):
        if len(ref.shape) == 2:
            out_ref[at] = ref[...]
        else:
            for tile in range(BLOCK):
                out_ref[at, rows_of(tile), :] = ref[BLOCK + tile]


def pass_kernel(array_ref, *refs):
    refs[-1][...] = array_ref[...]


def attend_chunk_kernel(pair, q_ref, kt_ref, v_ref, bias_ref, *refs):
    out_ref, *scratch = refs[-3:]
    first = (lax.axis_index("head") ^ pair) * BLOCK
    attend_block(first, q_ref.at[pair], kt_ref, v_ref, bias_ref, out_ref, *scratch)


def spread_kernel(pairs, *refs):
    out_ref, sems = refs[-2:]
    me = lax.axis_index("head")
    copies = [
        pltpu.make_async_copy(part, out_ref.at[:, column_of(me ^ pair)], sems.at[at])
        for at, (pair, part) in enumerate(zip(pairs, refs))
    ]
    for copy in copies:
        copy.start()
    for copy in copies:
        copy.wait()


def spread(outs, pairs, shape, *before):
    anywhere = pl.BlockSpec(memory_space=pl.ANY)
    return pl.pallas_call(
        functools.partial(spread_kernel, pairs),
        out_shape=jax.ShapeDtypeStruct(shape, jnp.bfloat16),
        in_specs=[VMEM] * len(pairs) + [anywhere] * len(before),
        out_specs=anywhere,
        scratch_shapes=[pltpu.SemaphoreType.DMA((len(pairs),))],
        input_output_aliases={len(pairs): 0} if before else {},
        compiler_params=pltpu.CompilerParams(vmem_limit_bytes=8 << 20),
        name="spread",
    )(*(outs[pair] for pair in pairs), *before)


def in_pairs(queries, keys, values, bias):
    heads = lax.axis_size("head")
    chunk, tiles = (queries.shape[0], HDIM), (BLOCK, TILE, HDIM)
    order = range(heads - 1, 0, -1)

    def exchange(array, pair):
        return lax.ppermute(array, "head", [(i, i ^ pair) for i in range(heads)])

    def call_on(kernel, name, operands, shape):
        return call(kernel, name, operands, [VMEM] * len(operands), shape)

    v_parts, k_parts, q_parts = [None] * heads, [None] * heads, [None] * heads
    for pair in [*order, 0]:
        part = call_on(functools.partial(load_tiles_kernel, pair, turn=False), "load_v", (values,), tiles)
        v_parts[pair] = exchange(part, pair) if pair else part
    for pair in [*order, 0]:
        operands = (keys, queries) if pair == 1 else (keys,)
        kernel = load_kq_kernel if pair == 1 else functools.partial(load_tiles_kernel, turn=True)
        shape = (len(operands) * BLOCK, TILE, HDIM)
        after = (v_parts[1],) if pair else ()
        if pair == order[0]:
            after += (bias,)
        part = call_on(functools.partial(kernel, pair), "load_k", (*operands, *after), shape)
        k_parts[pair] = exchange(part, pair) if pair else part
    q_parts[1] = k_parts[1]
    for pair in [*order[:-1], 0]:
        operands = (queries, k_parts[pair]) if pair else (queries,)
        part = call_on(functools.partial(load_q_kernel, pair), "load_q", operands, chunk)
        q_parts[pair] = exchange(part, pair) if pair else part
    all_values, all_keys = with_halo(v_parts), with_halo(k_parts)
    local_q = call(stack_kernel, "stack", q_parts, [VMEM] * heads, (heads, *chunk), cost=cost(100))
    all_values = call(
        pass_kernel, "values", (all_values, local_q), [VMEM] * 2, all_values.shape, cost=cost(16384)
    )
    outs = [None] * heads
    after = ()
    for pair in [*order, 0]:
        operands = (local_q, all_keys, all_values, bias, *after)
        outs[pair] = call(
            functools.partial(attend_chunk_kernel, pair),
            "attend_chunk",
            operands,
            [VMEM] * len(operands),
            chunk,
            block_scratch(),
            16,
            cost(BLOCK * LIST // 2 if pair else 1),
        )
        after = (outs[pair],)
        if pair:
            outs[pair] = exchange(outs[pair], pair)
    after = ()
    for pair in order:
        operands = (outs[pair], *after)
        outs[pair] = call(
            pass_kernel, "landed", operands, [VMEM] * len(operands), chunk, cost=cost(BLOCK * LIST // 2)
        )
        after = (outs[pair],)
    last = list(order[-2:])
    early = [pair for pair in range(heads) if pair not in last]
    return spread(outs, last, queries.shape, spread(outs, early, queries.shape))


def on_device(queries, keys, values, tile_lists, live_counts):
    ctx, heads = lax.axis_size("ctx"), lax.axis_size("head")
    bias = mask_bias(tile_lists, live_counts, tile_lists.shape[0] * ctx)
    in_chunks = queries.shape[0] == BLOCK * TILE and heads * BLOCK >= EDGE
    form = in_pairs if in_chunks and heads in (4, 8) and ctx % 2 == 0 else whole_range
    return form(queries, keys, values, bias)


def solution(mesh):
    return jax.shard_map(
        on_device,
        mesh=mesh,
        in_specs=(
            P(("groups", "ctx", "head"), None),
            P(("groups", "ctx", "head"), None),
            P(("groups", "ctx", "head"), None),
            P(("groups", "ctx"), None),
            P(("groups", "ctx")),
        ),
        out_specs=P(("groups", "ctx", "head"), None),
        check_vma=False,
    )
```

```python
import functools
import math

import jax
import jax.numpy as jnp
from jax import lax
from jax.experimental import pallas as pl
from jax.experimental.pallas import tpu as pltpu
from jax.sharding import PartitionSpec as P

HDIM = 128
TILE = 128
EDGE = 8
LIST = 16
BLOCK = 3
WINDOW = BLOCK + LIST - 1
HIDDEN = -1e30
EXPONENT_SCALE = HDIM ** (-0.5) * math.log2(math.e)
SMEM = pl.BlockSpec(memory_space=pltpu.SMEM)
VMEM = pl.BlockSpec(memory_space=pltpu.VMEM)


def call(kernel, name, operands, in_specs, shapes, scratch=(), limit=8, cost=None):
    out_shape = jax.tree.map(
        lambda shape: shape if hasattr(shape, "dtype") else jax.ShapeDtypeStruct(shape, jnp.bfloat16),
        shapes,
        is_leaf=lambda node: isinstance(node, tuple) or hasattr(node, "dtype"),
    )
    return pl.pallas_call(
        kernel,
        out_shape=out_shape,
        in_specs=in_specs,
        out_specs=jax.tree.map(lambda _: VMEM, out_shape),
        scratch_shapes=scratch,
        compiler_params=pltpu.CompilerParams(vmem_limit_bytes=limit << 20),
        cost_estimate=cost,
        name=name,
    )(*operands)


def column_of(head):
    return pl.ds(pl.multiple_of(head * HDIM, HDIM), HDIM)


def rows_of(tile):
    return slice(tile * TILE, (tile + 1) * TILE)


def bias_kernel(total_tiles, lists_ref, counts_ref, bias_ref):
    tiles, entries = lists_ref.shape
    lists = lists_ref[...]
    entry = lax.broadcasted_iota(jnp.int32, lists.shape, 1)
    row = lax.broadcasted_iota(jnp.int32, lists.shape, 0)
    live = (entry < counts_ref[...]) & (lists >= 0) & (lists < total_tiles)
    places = jnp.where(live, lists - lists[:, :1] + row + EDGE, -1)
    listed = [jnp.broadcast_to(places[:, at : at + 1], (tiles, TILE)) for at in range(entries)]
    for place in range(bias_ref.shape[0]):
        visible = listed[0] == place
        for at in range(1, entries):
            visible |= listed[at] == place
        bias_ref[place] = jnp.where(visible, 0.0, HIDDEN)


def mask_bias(tile_lists, live_counts, total_tiles):
    tiles = tile_lists.shape[0]
    shape = jax.ShapeDtypeStruct((tiles + LIST - 1, tiles, TILE), jnp.float32)
    kernel = functools.partial(bias_kernel, total_tiles)
    return call(kernel, "mask_bias", (tile_lists, live_counts[:, None]), [VMEM] * 2, shape)


def attend_block(first, q_ref, kt_ref, v_ref, bias_ref, out_ref, scores, probs):
    def score(tile):
        row = first + tile
        highest = jnp.full((TILE, TILE), HIDDEN, jnp.float32)
        for offset in range(0, LIST, 2):
            at = row + offset
            keys = jnp.concatenate([kt_ref[at], kt_ref[at + 1]], axis=1)
            part = jnp.dot(q_ref[rows_of(tile), :], keys, preferred_element_type=jnp.float32)
            for half in range(2):
                masked = part[:, rows_of(half)] + bias_ref[at + half, pl.ds(row, 1), :]
                scores[tile, :, rows_of(offset + half)] = masked
                highest = jnp.maximum(highest, masked)
        return jnp.broadcast_to(jnp.max(highest, axis=1, keepdims=True), (TILE, TILE))

    maxima = [score(0)]
    for tile in range(BLOCK):
        if tile + 1 < BLOCK:
            maxima.append(score(tile + 1))
        total = jnp.zeros((TILE, TILE), jnp.float32)
        for offset in range(LIST):
            weights = jnp.exp2((scores[tile, :, rows_of(offset)] - maxima[tile]) * EXPONENT_SCALE)
            total += weights
            probs[tile, :, rows_of(offset)] = weights.astype(jnp.bfloat16)
        values = v_ref[pl.ds(first + tile, LIST)].reshape(LIST * TILE, HDIM)
        mixed = jnp.dot(probs[tile], values, preferred_element_type=jnp.float32)
        out_ref[rows_of(tile), :] = (mixed / jnp.sum(total, axis=1, keepdims=True)).astype(jnp.bfloat16)


def block_scratch():
    shape = (BLOCK, TILE, LIST * TILE)
    return [pltpu.VMEM(shape, jnp.float32), pltpu.VMEM(shape, jnp.bfloat16)]


def cost(tile_pairs):
    pairs = tile_pairs * TILE * TILE
    return pl.CostEstimate(flops=4 * pairs * HDIM, bytes_accessed=pairs, transcendentals=pairs)


def halo(array, dim, unit):
    ctx = lax.axis_size("ctx")
    count = array.shape[dim]
    tail = lax.slice_in_dim(array, count - EDGE * unit, count, axis=dim)
    head = lax.slice_in_dim(array, 0, (EDGE - 1) * unit, axis=dim)
    low = lax.ppermute(tail, "ctx", [(i, i + 1) for i in range(ctx - 1)])
    high = lax.ppermute(head, "ctx", [(i + 1, i) for i in range(ctx - 1)])
    return low, high


def pack_kernel(heads, q_ref, k_ref, v_ref, q_out, k_out, v_out):
    for source, target in ((k_ref, k_out), (v_ref, v_out), (q_ref, q_out)):
        for head in range(heads):
            target[head] = source[:, head * HDIM : (head + 1) * HDIM]


def unpack_kernel(heads, parts_ref, out_ref):
    for head in range(heads):
        out_ref[:, head * HDIM : (head + 1) * HDIM] = parts_ref[head]


def attend_range_kernel(q_ref, k_low, k_own, k_high, v_low, v_own, v_high, bias_ref, out_ref, kt, v, *scratch):
    at = 0
    for k_part, v_part in ((k_low, v_low), (k_own, v_own), (k_high, v_high)):
        for tile in range(k_part.shape[0] // TILE):
            kt[at] = k_part[rows_of(tile), :].T
            v[at] = v_part[rows_of(tile), :]
            at += 1

    @pl.loop(0, q_ref.shape[0] // (BLOCK * TILE))
    def _(block):
        place = pl.ds(pl.multiple_of(block * BLOCK * TILE, TILE), BLOCK * TILE)
        attend_block(block * BLOCK, q_ref.at[place, :], kt, v, bias_ref, out_ref.at[place, :], *scratch)


def to_heads(array):
    heads, rows, _ = array.shape
    return lax.all_to_all(array, "head", split_axis=0, concat_axis=0, tiled=True).reshape(heads * rows, HDIM)


def whole_range(queries, keys, values, bias):
    rows, columns = queries.shape
    heads = columns // HDIM
    parts = (heads, rows, HDIM)
    q_parts, k_parts, v_parts = call(
        functools.partial(pack_kernel, heads), "pack", (queries, keys, values), [VMEM] * 3, [parts] * 3
    )
    k_own, v_own = to_heads(k_parts), to_heads(v_parts)
    (k_low, k_high), (v_low, v_high) = halo(k_own, 0, TILE), halo(v_own, 0, TILE)
    local_q = to_heads(q_parts)
    padded = heads * rows // TILE + LIST - 1
    head_out = call(
        attend_range_kernel,
        "attend_range",
        (local_q, k_low, k_own, k_high, v_low, v_own, v_high, bias),
        [VMEM] * 8,
        (heads * rows, HDIM),
        [pltpu.VMEM((padded, TILE, HDIM), jnp.bfloat16)] * 2 + block_scratch(),
        24,
    )
    back = lax.all_to_all(head_out.reshape(parts), "head", split_axis=0, concat_axis=0, tiled=True)
    return call(functools.partial(unpack_kernel, heads), "unpack", (back,), [VMEM], (rows, columns))


def load_tiles_kernel(pair, array_ref, *refs, turn):
    columns = column_of(lax.axis_index("head") ^ pair)
    for tile in range(BLOCK):
        part = array_ref[rows_of(tile), columns]
        refs[-1][tile] = part.T if turn else part


def load_kq_kernel(pair, k_ref, q_ref, *refs):
    columns = column_of(lax.axis_index("head") ^ pair)
    for tile in range(BLOCK):
        refs[-1][tile] = k_ref[rows_of(tile), columns].T
        refs[-1][BLOCK + tile] = q_ref[rows_of(tile), columns]


def load_q_kernel(pair, q_ref, *refs):
    refs[-1][...] = q_ref[:, column_of(lax.axis_index("head") ^ pair)]


def gather_kernel(*refs):
    *parts, own_ref = refs
    me = lax.axis_index("head")
    for pair, part in enumerate(parts):
        own_ref[pl.ds((me ^ pair) * BLOCK, BLOCK)] = part[:BLOCK]


def edges_kernel(own_ref, odd_ref, even_ref):
    last = own_ref.shape[0] - EDGE
    odd = lax.rem(lax.axis_index("ctx"), 2)
    odd_ref[...] = own_ref[pl.ds(odd * last, EDGE)]
    even_ref[...] = own_ref[pl.ds((1 - odd) * last, EDGE)]


def join_kernel(own_ref, first_ref, second_ref, out_ref):
    odd = lax.rem(lax.axis_index("ctx"), 2)
    tiles = own_ref.shape[0]
    out_ref[EDGE : EDGE + tiles] = own_ref[...]

    def around(low_ref, high_ref):
        out_ref[:EDGE] = low_ref[...]
        out_ref[EDGE + tiles :] = high_ref[: EDGE - 1]

    @pl.when(odd == 1)
    def _():
        around(second_ref, first_ref)

    @pl.when(odd == 0)
    def _():
        around(first_ref, second_ref)


def with_halo(parts):
    heads, ctx = len(parts), lax.axis_size("ctx")
    tiles, edge = heads * BLOCK, (EDGE, TILE, HDIM)
    own = call(gather_kernel, "gather", parts, [VMEM] * heads, (tiles, TILE, HDIM))
    odd_edge, even_edge = call(edges_kernel, "edges", (own,), [VMEM], [edge, edge])

    def exchange(array, first):
        lower = range(first, ctx - 1, 2)
        return lax.ppermute(array, "ctx", [(i, i + 1) for i in lower] + [(i + 1, i) for i in lower])

    operands = (own, exchange(odd_edge, 1), exchange(even_edge, 0))
    return call(join_kernel, "join", operands, [VMEM] * 3, (tiles + LIST - 1, TILE, HDIM))


def stack_kernel(*refs):
    *q_refs, out_ref = refs
    for at, ref in enumerate(q_refs):
        if len(ref.shape) == 2:
            out_ref[at] = ref[...]
        else:
            for tile in range(BLOCK):
                out_ref[at, rows_of(tile), :] = ref[BLOCK + tile]


def pass_kernel(array_ref, *refs):
    refs[-1][...] = array_ref[...]


def attend_chunk_kernel(pair, q_ref, kt_ref, v_ref, bias_ref, *refs):
    out_ref, *scratch = refs[-3:]
    first = (lax.axis_index("head") ^ pair) * BLOCK
    attend_block(first, q_ref.at[pair], kt_ref, v_ref, bias_ref, out_ref, *scratch)


def spread_kernel(pairs, *refs):
    out_ref, sems = refs[-2:]
    me = lax.axis_index("head")
    copies = [
        pltpu.make_async_copy(part, out_ref.at[:, column_of(me ^ pair)], sems.at[at])
        for at, (pair, part) in enumerate(zip(pairs, refs))
    ]
    for copy in copies:
        copy.start()
    for copy in copies:
        copy.wait()


def spread(outs, pairs, shape, *before):
    anywhere = pl.BlockSpec(memory_space=pl.ANY)
    return pl.pallas_call(
        functools.partial(spread_kernel, pairs),
        out_shape=jax.ShapeDtypeStruct(shape, jnp.bfloat16),
        in_specs=[VMEM] * len(pairs) + [anywhere] * len(before),
        out_specs=anywhere,
        scratch_shapes=[pltpu.SemaphoreType.DMA((len(pairs),))],
        input_output_aliases={len(pairs): 0} if before else {},
        compiler_params=pltpu.CompilerParams(vmem_limit_bytes=8 << 20),
        name="spread",
    )(*(outs[pair] for pair in pairs), *before)


def in_pairs(queries, keys, values, bias):
    heads = lax.axis_size("head")
    chunk, tiles = (queries.shape[0], HDIM), (BLOCK, TILE, HDIM)
    order = range(heads - 1, 0, -1)

    def exchange(array, pair):
        return lax.ppermute(array, "head", [(i, i ^ pair) for i in range(heads)])

    def call_on(kernel, name, operands, shape):
        return call(kernel, name, operands, [VMEM] * len(operands), shape)

    v_parts, k_parts, q_parts = [None] * heads, [None] * heads, [None] * heads
    for pair in [*order, 0]:
        column = (lax.axis_index("head") ^ pair) * HDIM
        part = lax.dynamic_slice_in_dim(values, column, HDIM, axis=1).reshape(tiles)
        v_parts[pair] = exchange(part, pair) if pair else part
    for pair in [*order, 0]:
        operands = (keys, queries) if pair == 1 else (keys,)
        kernel = load_kq_kernel if pair == 1 else functools.partial(load_tiles_kernel, turn=True)
        shape = (len(operands) * BLOCK, TILE, HDIM)
        after = (v_parts[1],) if pair else ()
        if pair == 1:
            after += (bias,)
        part = call_on(functools.partial(kernel, pair), "load_k", (*operands, *after), shape)
        k_parts[pair] = exchange(part, pair) if pair else part
    q_parts[1] = k_parts[1]
    for pair in [*order[:-1], 0]:
        operands = (queries, k_parts[pair]) if pair else (queries,)
        part = call_on(functools.partial(load_q_kernel, pair), "load_q", operands, chunk)
        q_parts[pair] = exchange(part, pair) if pair else part
    all_values, all_keys = with_halo(v_parts), with_halo(k_parts)
    local_q = call(stack_kernel, "stack", q_parts, [VMEM] * heads, (heads, *chunk), cost=cost(100))
    all_values = call(
        pass_kernel, "values", (all_values, local_q), [VMEM] * 2, all_values.shape, cost=cost(16384)
    )
    outs = [None] * heads
    after = ()
    for pair in [*order, 0]:
        operands = (local_q, all_keys, all_values, bias, *after)
        outs[pair] = call(
            functools.partial(attend_chunk_kernel, pair),
            "attend_chunk",
            operands,
            [VMEM] * len(operands),
            chunk,
            block_scratch(),
            16,
            cost(BLOCK * LIST // 2 if pair else 1),
        )
        after = (outs[pair],)
        if pair:
            outs[pair] = exchange(outs[pair], pair)
    after = ()
    for pair in order:
        operands = (outs[pair], *after)
        outs[pair] = call(
            pass_kernel, "landed", operands, [VMEM] * len(operands), chunk, cost=cost(BLOCK * LIST // 2)
        )
        after = (outs[pair],)
    last = order[-1]
    early = [pair for pair in range(heads) if pair != last]
    return spread(outs, [last], queries.shape, spread(outs, early, queries.shape))


def on_device(queries, keys, values, tile_lists, live_counts):
    ctx, heads = lax.axis_size("ctx"), lax.axis_size("head")
    bias = mask_bias(tile_lists, live_counts, tile_lists.shape[0] * ctx)
    in_chunks = queries.shape[0] == BLOCK * TILE and heads * BLOCK >= EDGE
    form = in_pairs if in_chunks and heads in (4, 8) and ctx % 2 == 0 else whole_range
    return form(queries, keys, values, bias)


def solution(mesh):
    return jax.shard_map(
        on_device,
        mesh=mesh,
        in_specs=(
            P(("groups", "ctx", "head"), None),
            P(("groups", "ctx", "head"), None),
            P(("groups", "ctx", "head"), None),
            P(("groups", "ctx"), None),
            P(("groups", "ctx")),
        ),
        out_specs=P(("groups", "ctx", "head"), None),
        check_vma=False,
    )
```

```python
import functools
import math

import jax
import jax.numpy as jnp
from jax import lax
from jax.experimental import pallas as pl
from jax.experimental.pallas import tpu as pltpu
from jax.sharding import PartitionSpec as P

HDIM = 128
TILE = 128
EDGE = 8
LIST = 16
BLOCK = 3
WINDOW = BLOCK + LIST - 1
HIDDEN = -1e30
EXPONENT_SCALE = HDIM ** (-0.5) * math.log2(math.e)
SMEM = pl.BlockSpec(memory_space=pltpu.SMEM)
VMEM = pl.BlockSpec(memory_space=pltpu.VMEM)


def call(kernel, name, operands, in_specs, shapes, scratch=(), limit=8, cost=None):
    out_shape = jax.tree.map(
        lambda shape: shape if hasattr(shape, "dtype") else jax.ShapeDtypeStruct(shape, jnp.bfloat16),
        shapes,
        is_leaf=lambda node: isinstance(node, tuple) or hasattr(node, "dtype"),
    )
    return pl.pallas_call(
        kernel,
        out_shape=out_shape,
        in_specs=in_specs,
        out_specs=jax.tree.map(lambda _: VMEM, out_shape),
        scratch_shapes=scratch,
        compiler_params=pltpu.CompilerParams(vmem_limit_bytes=limit << 20),
        cost_estimate=cost,
        name=name,
    )(*operands)


def column_of(head):
    return pl.ds(pl.multiple_of(head * HDIM, HDIM), HDIM)


def rows_of(tile):
    return slice(tile * TILE, (tile + 1) * TILE)


def bias_kernel(total_tiles, lists_ref, counts_ref, bias_ref):
    tiles, entries = lists_ref.shape
    lists = lists_ref[...]
    entry = lax.broadcasted_iota(jnp.int32, lists.shape, 1)
    row = lax.broadcasted_iota(jnp.int32, lists.shape, 0)
    live = (entry < counts_ref[...]) & (lists >= 0) & (lists < total_tiles)
    places = jnp.where(live, lists - lists[:, :1] + row + EDGE, -1)
    listed = [jnp.broadcast_to(places[:, at : at + 1], (tiles, TILE)) for at in range(entries)]
    for place in range(bias_ref.shape[0]):
        visible = listed[0] == place
        for at in range(1, entries):
            visible |= listed[at] == place
        bias_ref[place] = jnp.where(visible, 0.0, HIDDEN)


def mask_bias(tile_lists, live_counts, total_tiles):
    tiles = tile_lists.shape[0]
    shape = jax.ShapeDtypeStruct((tiles + LIST - 1, tiles, TILE), jnp.float32)
    kernel = functools.partial(bias_kernel, total_tiles)
    return call(kernel, "mask_bias", (tile_lists, live_counts[:, None]), [VMEM] * 2, shape)


def attend_block(first, q_ref, kt_ref, v_ref, bias_ref, out_ref, scores, probs):
    def score(tile):
        row = first + tile
        highest = jnp.full((TILE, TILE), HIDDEN, jnp.float32)
        for offset in range(0, LIST, 2):
            at = row + offset
            keys = jnp.concatenate([kt_ref[at], kt_ref[at + 1]], axis=1)
            part = jnp.dot(q_ref[rows_of(tile), :], keys, preferred_element_type=jnp.float32)
            for half in range(2):
                masked = part[:, rows_of(half)] + bias_ref[at + half, pl.ds(row, 1), :]
                scores[tile, :, rows_of(offset + half)] = masked
                highest = jnp.maximum(highest, masked)
        return jnp.broadcast_to(jnp.max(highest, axis=1, keepdims=True), (TILE, TILE))

    maxima = [score(0)]
    for tile in range(BLOCK):
        if tile + 1 < BLOCK:
            maxima.append(score(tile + 1))
        total = jnp.zeros((TILE, TILE), jnp.float32)
        for offset in range(LIST):
            weights = jnp.exp2((scores[tile, :, rows_of(offset)] - maxima[tile]) * EXPONENT_SCALE)
            total += weights
            probs[tile, :, rows_of(offset)] = weights.astype(jnp.bfloat16)
        values = v_ref[pl.ds(first + tile, LIST)].reshape(LIST * TILE, HDIM)
        mixed = jnp.dot(probs[tile], values, preferred_element_type=jnp.float32)
        out_ref[rows_of(tile), :] = (mixed / jnp.sum(total, axis=1, keepdims=True)).astype(jnp.bfloat16)


def block_scratch():
    shape = (BLOCK, TILE, LIST * TILE)
    return [pltpu.VMEM(shape, jnp.float32), pltpu.VMEM(shape, jnp.bfloat16)]


def cost(tile_pairs):
    pairs = tile_pairs * TILE * TILE
    return pl.CostEstimate(flops=4 * pairs * HDIM, bytes_accessed=pairs, transcendentals=pairs)


def halo(array, dim, unit):
    ctx = lax.axis_size("ctx")
    count = array.shape[dim]
    tail = lax.slice_in_dim(array, count - EDGE * unit, count, axis=dim)
    head = lax.slice_in_dim(array, 0, (EDGE - 1) * unit, axis=dim)
    low = lax.ppermute(tail, "ctx", [(i, i + 1) for i in range(ctx - 1)])
    high = lax.ppermute(head, "ctx", [(i + 1, i) for i in range(ctx - 1)])
    return low, high


def pack_kernel(heads, q_ref, k_ref, v_ref, q_out, k_out, v_out):
    for source, target in ((k_ref, k_out), (v_ref, v_out), (q_ref, q_out)):
        for head in range(heads):
            target[head] = source[:, head * HDIM : (head + 1) * HDIM]


def unpack_kernel(heads, parts_ref, out_ref):
    for head in range(heads):
        out_ref[:, head * HDIM : (head + 1) * HDIM] = parts_ref[head]


def attend_range_kernel(q_ref, k_low, k_own, k_high, v_low, v_own, v_high, bias_ref, out_ref, kt, v, *scratch):
    at = 0
    for k_part, v_part in ((k_low, v_low), (k_own, v_own), (k_high, v_high)):
        for tile in range(k_part.shape[0] // TILE):
            kt[at] = k_part[rows_of(tile), :].T
            v[at] = v_part[rows_of(tile), :]
            at += 1

    @pl.loop(0, q_ref.shape[0] // (BLOCK * TILE))
    def _(block):
        place = pl.ds(pl.multiple_of(block * BLOCK * TILE, TILE), BLOCK * TILE)
        attend_block(block * BLOCK, q_ref.at[place, :], kt, v, bias_ref, out_ref.at[place, :], *scratch)


def to_heads(array):
    heads, rows, _ = array.shape
    return lax.all_to_all(array, "head", split_axis=0, concat_axis=0, tiled=True).reshape(heads * rows, HDIM)


def whole_range(queries, keys, values, bias):
    rows, columns = queries.shape
    heads = columns // HDIM
    parts = (heads, rows, HDIM)
    q_parts, k_parts, v_parts = call(
        functools.partial(pack_kernel, heads), "pack", (queries, keys, values), [VMEM] * 3, [parts] * 3
    )
    k_own, v_own = to_heads(k_parts), to_heads(v_parts)
    (k_low, k_high), (v_low, v_high) = halo(k_own, 0, TILE), halo(v_own, 0, TILE)
    local_q = to_heads(q_parts)
    padded = heads * rows // TILE + LIST - 1
    head_out = call(
        attend_range_kernel,
        "attend_range",
        (local_q, k_low, k_own, k_high, v_low, v_own, v_high, bias),
        [VMEM] * 8,
        (heads * rows, HDIM),
        [pltpu.VMEM((padded, TILE, HDIM), jnp.bfloat16)] * 2 + block_scratch(),
        24,
    )
    back = lax.all_to_all(head_out.reshape(parts), "head", split_axis=0, concat_axis=0, tiled=True)
    return call(functools.partial(unpack_kernel, heads), "unpack", (back,), [VMEM], (rows, columns))


def load_tiles_kernel(pair, array_ref, *refs, turn):
    columns = column_of(lax.axis_index("head") ^ pair)
    for tile in range(BLOCK):
        part = array_ref[rows_of(tile), columns]
        refs[-1][tile] = part.T if turn else part


def load_kq_kernel(pair, k_ref, q_ref, *refs):
    columns = column_of(lax.axis_index("head") ^ pair)
    for tile in range(BLOCK):
        refs[-1][tile] = k_ref[rows_of(tile), columns].T
        refs[-1][BLOCK + tile] = q_ref[rows_of(tile), columns]


def load_q_kernel(pair, q_ref, *refs):
    refs[-1][...] = q_ref[:, column_of(lax.axis_index("head") ^ pair)]


def gather_kernel(*refs):
    *parts, own_ref = refs
    me = lax.axis_index("head")
    for pair, part in enumerate(parts):
        own_ref[pl.ds((me ^ pair) * BLOCK, BLOCK)] = part[:BLOCK]


def edges_kernel(own_ref, odd_ref, even_ref):
    last = own_ref.shape[0] - EDGE
    odd = lax.rem(lax.axis_index("ctx"), 2)
    odd_ref[...] = own_ref[pl.ds(odd * last, EDGE)]
    even_ref[...] = own_ref[pl.ds((1 - odd) * last, EDGE)]


def join_kernel(own_ref, first_ref, second_ref, out_ref):
    odd = lax.rem(lax.axis_index("ctx"), 2)
    tiles = own_ref.shape[0]
    out_ref[EDGE : EDGE + tiles] = own_ref[...]

    def around(low_ref, high_ref):
        out_ref[:EDGE] = low_ref[...]
        out_ref[EDGE + tiles :] = high_ref[: EDGE - 1]

    @pl.when(odd == 1)
    def _():
        around(second_ref, first_ref)

    @pl.when(odd == 0)
    def _():
        around(first_ref, second_ref)


def with_halo(parts):
    heads, ctx = len(parts), lax.axis_size("ctx")
    tiles, edge = heads * BLOCK, (EDGE, TILE, HDIM)
    own = call(gather_kernel, "gather", parts, [VMEM] * heads, (tiles, TILE, HDIM))
    odd_edge, even_edge = call(edges_kernel, "edges", (own,), [VMEM], [edge, edge])

    def exchange(array, first):
        lower = range(first, ctx - 1, 2)
        return lax.ppermute(array, "ctx", [(i, i + 1) for i in lower] + [(i + 1, i) for i in lower])

    operands = (own, exchange(odd_edge, 1), exchange(even_edge, 0))
    return call(join_kernel, "join", operands, [VMEM] * 3, (tiles + LIST - 1, TILE, HDIM))


def stack_kernel(*refs):
    *q_refs, out_ref = refs
    for at, ref in enumerate(q_refs):
        if len(ref.shape) == 2:
            out_ref[at] = ref[...]
        else:
            for tile in range(BLOCK):
                out_ref[at, rows_of(tile), :] = ref[BLOCK + tile]


def pass_kernel(array_ref, *refs):
    refs[-1][...] = array_ref[...]


def attend_chunk_kernel(pair, q_ref, kt_ref, v_ref, bias_ref, *refs):
    out_ref, *scratch = refs[-3:]
    first = (lax.axis_index("head") ^ pair) * BLOCK
    attend_block(first, q_ref.at[pair], kt_ref, v_ref, bias_ref, out_ref, *scratch)


def spread_kernel(pairs, *refs):
    out_ref, sems = refs[-2:]
    me = lax.axis_index("head")
    copies = [
        pltpu.make_async_copy(part, out_ref.at[:, column_of(me ^ pair)], sems.at[at])
        for at, (pair, part) in enumerate(zip(pairs, refs))
    ]
    for copy in copies:
        copy.start()
    for copy in copies:
        copy.wait()


def spread(outs, pairs, shape, *before):
    anywhere = pl.BlockSpec(memory_space=pl.ANY)
    return pl.pallas_call(
        functools.partial(spread_kernel, pairs),
        out_shape=jax.ShapeDtypeStruct(shape, jnp.bfloat16),
        in_specs=[VMEM] * len(pairs) + [anywhere] * len(before),
        out_specs=anywhere,
        scratch_shapes=[pltpu.SemaphoreType.DMA((len(pairs),))],
        input_output_aliases={len(pairs): 0} if before else {},
        compiler_params=pltpu.CompilerParams(vmem_limit_bytes=8 << 20),
        name="spread",
    )(*(outs[pair] for pair in pairs), *before)


def in_pairs(queries, keys, values, bias):
    heads = lax.axis_size("head")
    chunk, tiles = (queries.shape[0], HDIM), (BLOCK, TILE, HDIM)
    order = range(heads - 1, 0, -1)

    def exchange(array, pair):
        return lax.ppermute(array, "head", [(i, i ^ pair) for i in range(heads)])

    def call_on(kernel, name, operands, shape):
        return call(kernel, name, operands, [VMEM] * len(operands), shape)

    v_parts, k_parts, q_parts = [None] * heads, [None] * heads, [None] * heads
    for pair in [*order, 0]:
        column = (lax.axis_index("head") ^ pair) * HDIM
        part = lax.dynamic_slice_in_dim(values, column, HDIM, axis=1).reshape(tiles)
        v_parts[pair] = exchange(part, pair) if pair else part
    for pair in [*order, 0]:
        operands = (keys, queries) if pair == 1 else (keys,)
        kernel = load_kq_kernel if pair == 1 else functools.partial(load_tiles_kernel, turn=True)
        shape = (len(operands) * BLOCK, TILE, HDIM)
        after = (v_parts[1],) if pair else ()
        if pair == 1:
            after += (bias,)
        part = call_on(functools.partial(kernel, pair), "load_k", (*operands, *after), shape)
        k_parts[pair] = exchange(part, pair) if pair else part
    q_parts[1] = k_parts[1]
    for pair in [*order[:-1], 0]:
        operands = (queries, k_parts[pair]) if pair else (queries,)
        part = call_on(functools.partial(load_q_kernel, pair), "load_q", operands, chunk)
        q_parts[pair] = exchange(part, pair) if pair else part
    all_values, all_keys = with_halo(v_parts), with_halo(k_parts)
    local_q = call(stack_kernel, "stack", q_parts, [VMEM] * heads, (heads, *chunk), cost=cost(100))
    all_values = call(
        pass_kernel, "values", (all_values, local_q), [VMEM] * 2, all_values.shape, cost=cost(16384)
    )
    outs = [None] * heads
    half = heads // 2
    order = [half, *(pair for pair in order if pair != half)]
    after = ()
    for pair in [*order, 0]:
        operands = (local_q, all_keys, all_values, bias, *after)
        outs[pair] = call(
            functools.partial(attend_chunk_kernel, pair),
            "attend_chunk",
            operands,
            [VMEM] * len(operands),
            chunk,
            block_scratch(),
            16,
            cost(BLOCK * LIST // 2 if pair else 1),
        )
        after = (outs[pair],)
        if pair:
            outs[pair] = exchange(outs[pair], pair)
    after = ()
    for pair in order:
        operands = (outs[pair], *after)
        outs[pair] = call(
            pass_kernel, "landed", operands, [VMEM] * len(operands), chunk, cost=cost(BLOCK * LIST // 2)
        )
        after = (outs[pair],)
    last = order[-1]
    early = [pair for pair in range(heads) if pair != last]
    return spread(outs, [last], queries.shape, spread(outs, early, queries.shape))


def on_device(queries, keys, values, tile_lists, live_counts):
    ctx, heads = lax.axis_size("ctx"), lax.axis_size("head")
    bias = mask_bias(tile_lists, live_counts, tile_lists.shape[0] * ctx)
    in_chunks = queries.shape[0] == BLOCK * TILE and heads * BLOCK >= EDGE
    form = in_pairs if in_chunks and heads in (4, 8) and ctx % 2 == 0 else whole_range
    return form(queries, keys, values, bias)


def solution(mesh):
    return jax.shard_map(
        on_device,
        mesh=mesh,
        in_specs=(
            P(("groups", "ctx", "head"), None),
            P(("groups", "ctx", "head"), None),
            P(("groups", "ctx", "head"), None),
            P(("groups", "ctx"), None),
            P(("groups", "ctx")),
        ),
        out_specs=P(("groups", "ctx", "head"), None),
        check_vma=False,
    )
```
